256 devices in a mesh: ctx: 32 (over x_hi, z, core), head: 8 (over y, x_lo).
Axes of the slice: x: 4 (x_hi: 2, x_lo: 2; x = x_hi * 2 + x_lo), y: 4, z: 8, core: 2. Of those that a mesh axis runs over, the one named last changes fastest.
Arguments:
- queries: bfloat16 [4, 2048, 8192], P(None, 'ctx', 'head'), as said below
- key_vectors: bfloat16 [4, 2048, 1024], P(None, 'ctx', 'head'), as said below
- value_vectors: bfloat16 [4, 2048, 1024], P(None, 'ctx', 'head'), may hold values from -6 to 6
- output_gradient: bfloat16 [4, 2048, 8192], P(None, 'ctx', 'head'), may hold values from -6 to 6
- positions: int32 [4, 2048], P(None, 'ctx'), may hold values from 0 to 2047, as said below
- segments: int32 [4, 2048], P(None, 'ctx'), may hold values from 0 to 7, as said below
Outputs:
- query_grad: bfloat16 [4, 2048, 8192], P(None, ('ctx', 'head'))
- key_gradient: bfloat16 [4, 2048, 1024], P(None, ('ctx', 'head'))
- value_gradient: bfloat16 [4, 2048, 1024], P(None, ('ctx', 'head'))
The draws below stay inside these ranges and needn't reach their ends.
Inputs may be any that keep to these rules, and one draw needn't show every extreme that they name: `positions`: in each window each position appears in exactly one row. `segments`: in each window documents are runs of consecutive positions numbered in order of position, and every id of the range is used. `queries`: real-valued. `key_vectors`: real-valued.
All inputs are finite; a program needn't handle non-finite values.
Results may differ from the reference program's by a relative error of at most 0.012.
Values may be sent and summed in bfloat16 or wider, within the bound.
No kernel may reach another device: no remote copies, remote signals or barrier semaphores. Data moves between devices by JAX's collectives and lax.ppermute only.
A program may use at most 64 MiB of HBM per device.

```python
import math
import jax
import jax.numpy as jnp
from jax import lax

QUERY_HEADS = 64
KEY_VALUE_HEADS = 8
HEAD_SIZE = 128
WINDOWS = 4
DOCS = 8
WINDOW_TOKENS = 2048


def one_layout(window_key):
    order_rows = jax.random.permutation(jax.random.fold_in(window_key, 1), WINDOW_TOKENS).astype(jnp.int32)
    cut_span = min(WINDOW_TOKENS - 1, max(DOCS - 1, WINDOW_TOKENS // 16))
    doc_cuts = jax.random.permutation(jax.random.fold_in(window_key, 2), cut_span)[:DOCS - 1].astype(jnp.int32) + (WINDOW_TOKENS - cut_span)
    position_list = jnp.arange(WINDOW_TOKENS, dtype=jnp.int32)
    doc_of_pos = jnp.sum((position_list[:, None] >= doc_cuts[None, :]).astype(jnp.int32), axis=1).astype(jnp.int32)
    return (order_rows, doc_of_pos)


def window_layout(key):
    random_base_key = jax.random.fold_in(key, 101)
    window_keys = jax.vmap(lambda number: jax.random.fold_in(random_base_key, number))(jnp.arange(WINDOWS, dtype=jnp.int32))
    return jax.vmap(one_layout)(window_keys)


def draw_positions(key, part):
    order_rows, doc_of_pos = window_layout(key)
    return order_rows


def draw_segments(key, part):
    order_rows, doc_of_pos = window_layout(key)
    return jnp.take_along_axis(doc_of_pos, order_rows, axis=1).astype(jnp.int32)


def float_pair(key):
    random_base_key = jax.random.fold_in(key, 202)
    queries = jax.random.normal(jax.random.fold_in(random_base_key, 1), (WINDOWS, WINDOW_TOKENS, QUERY_HEADS * HEAD_SIZE), jnp.float32)
    unshaped_keys = jax.random.normal(jax.random.fold_in(random_base_key, 2), (WINDOWS, WINDOW_TOKENS, KEY_VALUE_HEADS * HEAD_SIZE), jnp.float32)
    return (queries, unshaped_keys)


def draw_queries(key, part):
    queries, unshaped_keys = float_pair(key)
    return queries.astype(jnp.bfloat16)


def draw_key_vectors(key, part):
    queries, unshaped_keys = float_pair(key)
    return unshaped_keys.astype(jnp.bfloat16)


def steps_of(stream_key, shape, pieces, smallest, largest):
    def one(dim, blocks):
        steps = jax.random.uniform(jax.random.fold_in(jax.random.fold_in(stream_key, 6), dim), (blocks,), jnp.float32, smallest / len(pieces), largest / len(pieces))
        return jnp.repeat(jnp.exp(steps), shape[dim] // blocks).reshape((-1,) + (1,) * (len(shape) - dim - 1))

    factor_of = one(*pieces[0])
    for cut in pieces[1:]:
        factor_of = factor_of * one(*cut)
    return factor_of


def scatter_about(stream_key, dims, width, limit, cuts=(), kind=jnp.bfloat16):
    gain = steps_of(stream_key, dims, cuts, -0.22, 0.18) if cuts else 1.0
    array = jax.random.normal(stream_key, dims, jnp.float32) * width * gain
    return jnp.minimum(jnp.maximum(array, -limit), limit).astype(kind)


def setup_inputs(seed: int = 0) -> dict:
    streams_of = jax.random.split(jax.random.key(seed), 7)
    queries = draw_queries(jax.random.fold_in(streams_of[6], 71), 0)
    key_vectors = draw_key_vectors(jax.random.fold_in(streams_of[6], 71), 0)
    value_vectors = scatter_about(streams_of[2], (WINDOWS, WINDOW_TOKENS, KEY_VALUE_HEADS * HEAD_SIZE), 1.0, 6.0, ((1, 32), (2, 8)))
    output_gradient = scatter_about(streams_of[3], (WINDOWS, WINDOW_TOKENS, QUERY_HEADS * HEAD_SIZE), 1.0, 6.0, ((1, 32), (2, 8)))
    positions = draw_positions(jax.random.fold_in(streams_of[6], 71), 0)
    segments = draw_segments(jax.random.fold_in(streams_of[6], 71), 0)
    return {"queries": queries, "key_vectors": key_vectors, "value_vectors": value_vectors, "output_gradient": output_gradient, "positions": positions, "segments": segments}


NEG_BIG = -1e+30

def one_window(operands):
    queries, key_vectors, value_vectors, output_gradient, positions, segments = operands
    query_groups = QUERY_HEADS // KEY_VALUE_HEADS
    factor = 1.0 / math.sqrt(HEAD_SIZE)
    allowed = (segments[:, None] == segments[None, :]) & (positions[None, :] <= positions[:, None])
    query_per_head = queries.reshape(WINDOW_TOKENS, KEY_VALUE_HEADS, query_groups, HEAD_SIZE).transpose(1, 2, 0, 3)
    gradient_per_head = output_gradient.reshape(WINDOW_TOKENS, KEY_VALUE_HEADS, query_groups, HEAD_SIZE).transpose(1, 2, 0, 3)
    key_per_head = key_vectors.reshape(WINDOW_TOKENS, KEY_VALUE_HEADS, HEAD_SIZE).transpose(1, 0, 2)
    value_per_head = value_vectors.reshape(WINDOW_TOKENS, KEY_VALUE_HEADS, HEAD_SIZE).transpose(1, 0, 2)

    def one_group(group_operands):
        query_block, grad_block, key_block, value_block = group_operands
        query_wide = query_block.astype(jnp.float32)
        grad_wide = grad_block.astype(jnp.float32)
        key_wide = key_block.astype(jnp.float32)
        value_wide = value_block.astype(jnp.float32)
        scores = jnp.einsum('gtd,sd->gts', query_wide, key_wide) * factor
        scores = jnp.where(allowed[None], scores, NEG_BIG)
        row_max = lax.optimization_barrier(jnp.max(scores, axis=-1, keepdims=True))
        row_sum = lax.optimization_barrier(jnp.sum(jnp.where(allowed[None], jnp.exp(scores - row_max), 0.0), axis=-1, keepdims=True))
        logsum = row_max + jnp.log(row_sum)
        softmax_out = jnp.where(allowed[None], jnp.exp(scores - logsum), 0.0)
        softmax_grad = jnp.einsum('gtd,sd->gts', grad_wide, value_wide)
        row_delta = lax.optimization_barrier(jnp.sum(softmax_out * softmax_grad, axis=-1, keepdims=True))
        score_grad = softmax_out * (softmax_grad - row_delta)
        softmax_low = lax.optimization_barrier(softmax_out.astype(jnp.bfloat16)).astype(jnp.float32)
        score_low = lax.optimization_barrier(score_grad.astype(jnp.bfloat16)).astype(jnp.float32)
        value_part = jnp.einsum('gts,gtd->sd', softmax_low, grad_wide)
        key_part = jnp.einsum('gts,gtd->sd', score_low, query_wide) * factor
        query_part = jnp.einsum('gts,sd->gtd', score_low, key_wide) * factor
        return (query_part, key_part, value_part)
    query_parts, key_pieces_split, value_pieces_split = lax.map(one_group, (query_per_head, gradient_per_head, key_per_head, value_per_head))
    query_grad = query_parts.transpose(2, 0, 1, 3).reshape(WINDOW_TOKENS, QUERY_HEADS * HEAD_SIZE).astype(jnp.bfloat16)
    key_gradient = key_pieces_split.transpose(1, 0, 2).reshape(WINDOW_TOKENS, KEY_VALUE_HEADS * HEAD_SIZE).astype(jnp.bfloat16)
    value_gradient = value_pieces_split.transpose(1, 0, 2).reshape(WINDOW_TOKENS, KEY_VALUE_HEADS * HEAD_SIZE).astype(jnp.bfloat16)
    return (query_grad, key_gradient, value_gradient)

def reference(queries, key_vectors, value_vectors, output_gradient, positions, segments):
    query_grad, key_gradient, value_gradient = lax.map(one_window, (queries, key_vectors, value_vectors, output_gradient, positions, segments))
    return (query_grad, key_gradient, value_gradient)
```

```python
import functools
import math

import jax
import jax.numpy as jnp
from jax import lax
from jax.experimental import pallas as pl
from jax.experimental.pallas import tpu as pltpu
from jax.sharding import Mesh, PartitionSpec as P

QUERY_HEADS = 64
KEY_VALUE_HEADS = 8
HEAD_SIZE = 128
GROUP = QUERY_HEADS // KEY_VALUE_HEADS
NEG_BIG = -1e30
CODE_SPAN = 2048
META_ROWS = 16
SCALE = 1.0 / math.sqrt(HEAD_SIZE)
EXP2_SCALE = SCALE * math.log2(math.e)

NT = (((1,), (1,)), ((), ()))
NN = (((1,), (0,)), ((), ()))


def dot(a, b, dims):
    return lax.dot_general(a, b, dims, preferred_element_type=jnp.float32)


def attention_kernel(q_ref, do_ref, kv_ref, code_ref, low_ref, high_ref, dq_ref, dkv_ref,
                     bias_ref, kt_ref, s_ref, p_ref, dp_ref, acc_ref):
    blocks, sources, _, _ = kv_ref.shape
    row_count = dkv_ref.shape[2]
    chunk = sources * row_count
    keys = blocks * chunk
    rows = q_ref.shape[0] * q_ref.shape[1]

    for c in range(keys // 128):
        column = jnp.broadcast_to(code_ref[c:c + 1, :], (128, 128)).T
        for r in range(rows // 128):
            low = low_ref[:, r * 128:(r + 1) * 128]
            high = high_ref[:, r * 128:(r + 1) * 128]
            allowed = (column >= low) & (column <= high)
            bias_ref[c * 128:(c + 1) * 128, r * 128:(r + 1) * 128] = jnp.where(allowed, 0.0, NEG_BIG)
    for b in range(blocks):
        key_block = kv_ref[b, :, 0:row_count, 0:HEAD_SIZE].reshape(chunk, HEAD_SIZE)
        kt_ref[:, b * chunk:(b + 1) * chunk] = key_block.T
    acc_ref[...] = jnp.zeros_like(acc_ref)

    def head(h, carry):
        lanes = pl.ds(pl.multiple_of(h * HEAD_SIZE, HEAD_SIZE), HEAD_SIZE)
        q = q_ref[:, :, lanes].reshape(rows, HEAD_SIZE)
        do = do_ref[:, :, lanes].reshape(rows, HEAD_SIZE)
        top = jnp.full((8, rows), NEG_BIG, jnp.float32)
        for b in range(blocks):
            part = slice(b * chunk, (b + 1) * chunk)
            key_block = kv_ref[b, :, 0:row_count, 0:HEAD_SIZE].reshape(chunk, HEAD_SIZE)
            s = dot(key_block, q, NT) + bias_ref[part, :]
            s_ref[part, :] = s
            top = jnp.maximum(top, jnp.max(s.reshape(chunk // 8, 8, rows), axis=0))
        top = jnp.max(top, axis=0, keepdims=True) * EXP2_SCALE
        total = jnp.zeros((8, rows), jnp.float32)
        cross = jnp.zeros((8, rows), jnp.float32)
        for b in range(blocks):
            part = slice(b * chunk, (b + 1) * chunk)
            value_block = kv_ref[b, :, 0:row_count, HEAD_SIZE:2 * HEAD_SIZE].reshape(chunk, HEAD_SIZE)
            p = jnp.exp2(s_ref[part, :] * EXP2_SCALE - top)
            dp = dot(value_block, do, NT)
            total = total + jnp.sum(p.reshape(chunk // 8, 8, rows), axis=0)
            cross = cross + jnp.sum((p * dp).reshape(chunk // 8, 8, rows), axis=0)
            p_ref[part, :] = p
            dp_ref[part, :] = dp
        inverse = 1.0 / jnp.sum(total, axis=0, keepdims=True)
        delta = jnp.sum(cross, axis=0, keepdims=True) * inverse
        dqt = jnp.zeros((HEAD_SIZE, rows), jnp.float32)
        for b in range(blocks):
            part = slice(b * chunk, (b + 1) * chunk)
            p = p_ref[part, :] * inverse
            ds = (p * (dp_ref[part, :] - delta)).astype(jnp.bfloat16)
            acc_ref[part, HEAD_SIZE:2 * HEAD_SIZE] += dot(p.astype(jnp.bfloat16), do, NN)
            acc_ref[part, 0:HEAD_SIZE] += dot(ds, q, NN)
            dqt = dqt + dot(kt_ref[:, part], ds, NN)
        dq_ref[:, :, lanes] = (dqt * SCALE).T.astype(jnp.bfloat16).reshape(dq_ref.shape[0], row_count, HEAD_SIZE)
        return carry

    lax.fori_loop(0, GROUP, head, 0)
    for b in range(blocks):
        part = slice(b * chunk, (b + 1) * chunk)
        shape = (sources, row_count, HEAD_SIZE)
        dkv_ref[b, :, :, 0:HEAD_SIZE] = (acc_ref[part, 0:HEAD_SIZE] * SCALE).astype(jnp.bfloat16).reshape(shape)
        dkv_ref[b, :, :, HEAD_SIZE:2 * HEAD_SIZE] = acc_ref[part, HEAD_SIZE:2 * HEAD_SIZE].astype(jnp.bfloat16).reshape(shape)


def attention(q, do, kv, code, low, high):
    blocks, sources, _, width = kv.shape
    row_count = q.shape[1]
    rows = q.shape[0] * row_count
    keys = blocks * sources * row_count
    vmem = pl.BlockSpec(memory_space=pltpu.VMEM)
    return pl.pallas_call(
        attention_kernel,
        out_shape=(
            jax.ShapeDtypeStruct(q.shape, jnp.bfloat16),
            jax.ShapeDtypeStruct((blocks, sources, row_count, width), jnp.bfloat16),
        ),
        in_specs=[vmem] * 6,
        out_specs=(vmem, vmem),
        scratch_shapes=[
            pltpu.VMEM((keys, rows), jnp.float32),
            pltpu.VMEM((HEAD_SIZE, keys), jnp.bfloat16),
            pltpu.VMEM((keys, rows), jnp.float32),
            pltpu.VMEM((keys, rows), jnp.float32),
            pltpu.VMEM((keys, rows), jnp.float32),
            pltpu.VMEM((keys, width), jnp.float32),
        ],
        compiler_params=pltpu.CompilerParams(vmem_limit_bytes=48 * 1024 * 1024),
        cost_estimate=pl.CostEstimate(
            flops=10 * keys * rows * HEAD_SIZE * GROUP, bytes_accessed=4 * 1024 * 1024,
            transcendentals=keys * rows * GROUP),
    )(q, do, kv, code, low, high)


PLANE = ("xh", "core")
FINAL = ("xh", "core", "y", "xl")


def on_device(queries, key_vectors, value_vectors, output_gradient, positions, segments):
    window_count, row_count, _ = queries.shape
    code = segments * CODE_SPAN + positions
    meta = jnp.concatenate([code // 128, code % 128], axis=1).astype(jnp.bfloat16)
    meta = jnp.pad(meta[:, None, :], ((0, 0), (0, META_ROWS - 1), (0, 2 * HEAD_SIZE - 2 * row_count)))
    packed = jnp.concatenate([jnp.concatenate([key_vectors, value_vectors], axis=2), meta], axis=1)
    mine = lax.all_to_all(packed, PLANE, split_axis=0, concat_axis=0, tiled=True)
    gathered = lax.all_gather(mine, "z", axis=0, tiled=False)
    q = lax.all_to_all(queries, PLANE, split_axis=0, concat_axis=0, tiled=True)
    do = lax.all_to_all(output_gradient, PLANE, split_axis=0, concat_axis=0, tiled=True)

    def decode(rows):
        return rows[..., 0:row_count].astype(jnp.float32) * 128.0 + rows[..., row_count:2 * row_count].astype(jnp.float32)

    key_code = decode(gathered[:, :, row_count, :]).reshape(-1, 128)
    high = decode(mine[:, row_count, :]).reshape(1, -1)
    low = jnp.floor(high * (1.0 / CODE_SPAN)) * CODE_SPAN
    dq, dkv = attention(q, do, gathered, key_code, low, high)

    parts = lax.all_to_all(dkv, "z", split_axis=0, concat_axis=0, tiled=True)
    dkv_own = jnp.sum(parts.astype(jnp.float32), axis=0).astype(jnp.bfloat16)
    heads = KEY_VALUE_HEADS
    out_rows = row_count // heads
    dq_final = lax.all_to_all(dq.reshape(window_count * heads, out_rows, GROUP * HEAD_SIZE), FINAL, 0, 0, tiled=True)
    dkv_final = lax.all_to_all(dkv_own.reshape(window_count * heads, out_rows, 2 * HEAD_SIZE), FINAL, 0, 0, tiled=True)

    def merged(array):
        width = array.shape[-1]
        return array.reshape(window_count, heads, out_rows, width).transpose(0, 2, 1, 3).reshape(window_count, out_rows, heads * width)

    return (
        merged(dq_final),
        merged(dkv_final[..., 0:HEAD_SIZE]),
        merged(dkv_final[..., HEAD_SIZE:2 * HEAD_SIZE]),
    )


def solution(mesh):
    fine = Mesh(mesh.devices.reshape(2, 8, 2, 4, 2), ("xh", "z", "core", "y", "xl"))
    ctx, head = ("xh", "z", "core"), ("y", "xl")
    vectors = P(None, ctx, head)
    out = P(None, ctx + head, None)
    return jax.shard_map(
        on_device,
        mesh=fine,
        in_specs=(vectors, vectors, vectors, vectors, P(None, ctx), P(None, ctx)),
        out_specs=(out, out, out),
        check_vma=False,
    )
```

```python
import math

import jax
import jax.numpy as jnp
from jax import lax
from jax.experimental import pallas as pl
from jax.experimental.pallas import tpu as pltpu
from jax.sharding import Mesh, PartitionSpec as P

QUERY_HEADS = 64
KEY_VALUE_HEADS = 8
HEAD_SIZE = 128
GROUP = QUERY_HEADS // KEY_VALUE_HEADS
NEG_BIG = -1e30
CODE_SPAN = 2048
META_ROWS = 16
SCALE = 1.0 / math.sqrt(HEAD_SIZE)
EXP2_SCALE = SCALE * math.log2(math.e)

NT = (((1,), (1,)), ((), ()))
NN = (((1,), (0,)), ((), ()))


def dot(a, b, dims):
    return lax.dot_general(a, b, dims, preferred_element_type=jnp.float32)


def attention_kernel(place_ref, low_ref, high_ref, *refs):
    qdo_refs = refs[0:4]
    piece_refs = refs[4:14]
    dq_ref, near_ref, far_ref, bias_ref, kt_ref, s_ref, p_ref, dp_ref, acc_ref = refs[14:]
    row_count = qdo_refs[0].shape[1]
    rows = 4 * row_count
    spans = []
    start = 0
    for ref in piece_refs:
        size = ref.shape[0] * row_count
        spans.append((ref, slice(start, start + size), size))
        start += size
    keys = start

    def keys_of(ref, size):
        return ref[:, 0:row_count, 0:HEAD_SIZE].reshape(size, HEAD_SIZE)

    def values_of(ref, size):
        return ref[:, 0:row_count, HEAD_SIZE:2 * HEAD_SIZE].reshape(size, HEAD_SIZE)

    for ref, part, size in spans:
        for b in range(ref.shape[0]):
            digits = ref[b, row_count:row_count + META_ROWS, :].astype(jnp.float32)[0:1, :]
            code = digits[:, 0:128] * 128.0 + digits[:, 128:256]
            column = jnp.broadcast_to(code, (128, 128)).T[0:row_count, :]
            begin = part.start + b * row_count
            for r in range(rows // 128):
                low = low_ref[:, r * 128:(r + 1) * 128]
                high = high_ref[:, r * 128:(r + 1) * 128]
                allowed = (column >= low) & (column <= high)
                bias_ref[begin:begin + row_count, r * 128:(r + 1) * 128] = jnp.where(allowed, 0.0, NEG_BIG)
    for ref, part, size in spans:
        kt_ref[:, part] = keys_of(ref, size).T
    acc_ref[...] = jnp.zeros_like(acc_ref)
    place = place_ref[0]

    def head(h, carry):
        lanes = pl.ds(pl.multiple_of(h * HEAD_SIZE, HEAD_SIZE), HEAD_SIZE)
        q = jnp.concatenate([ref[0, :, lanes] for ref in qdo_refs], axis=0)
        do = jnp.concatenate([ref[1, :, lanes] for ref in qdo_refs], axis=0)
        top = jnp.full((8, rows), NEG_BIG, jnp.float32)
        for ref, part, size in spans:
            s = dot(keys_of(ref, size), q, NT) + bias_ref[part, :]
            s_ref[part, :] = s
            top = jnp.maximum(top, jnp.max(s.reshape(size // 8, 8, rows), axis=0))
        top = jnp.max(top, axis=0, keepdims=True) * EXP2_SCALE
        total = jnp.zeros((8, rows), jnp.float32)
        cross = jnp.zeros((8, rows), jnp.float32)
        for ref, part, size in spans:
            p = jnp.exp2(s_ref[part, :] * EXP2_SCALE - top)
            dp = dot(values_of(ref, size), do, NT)
            total = total + jnp.sum(p.reshape(size // 8, 8, rows), axis=0)
            cross = cross + jnp.sum((p * dp).reshape(size // 8, 8, rows), axis=0)
            p_ref[part, :] = p
            dp_ref[part, :] = dp
        inverse = 1.0 / jnp.sum(total, axis=0, keepdims=True)
        delta = jnp.sum(cross, axis=0, keepdims=True) * inverse
        dqt = jnp.zeros((HEAD_SIZE, rows), jnp.float32)
        for ref, part, size in spans:
            p = p_ref[part, :] * inverse
            ds = (p * (dp_ref[part, :] - delta)).astype(jnp.bfloat16)
            acc_ref[part, HEAD_SIZE:2 * HEAD_SIZE] += dot(p.astype(jnp.bfloat16), do, NN)
            acc_ref[part, 0:HEAD_SIZE] += dot(ds, q, NN)
            dqt = dqt + dot(kt_ref[:, part], ds, NN)
        dq = (dqt * SCALE).T.astype(jnp.bfloat16)
        for r in range(4):
            dq_ref[place ^ r, :, lanes] = dq[r * row_count:(r + 1) * row_count, :]
        return carry

    lax.fori_loop(0, GROUP, head, 0)
    for i, out_ref in enumerate((near_ref, far_ref)):
        for b in range(4):
            shape = (4, row_count, HEAD_SIZE)
            begin = (i * 4 + b) * 4 * row_count
            part = slice(begin, begin + 4 * row_count)
            out_ref[b, :, :, 0:HEAD_SIZE] = (acc_ref[part, 0:HEAD_SIZE] * SCALE).astype(jnp.bfloat16).reshape(shape)
            out_ref[b, :, :, HEAD_SIZE:2 * HEAD_SIZE] = acc_ref[part, HEAD_SIZE:2 * HEAD_SIZE].astype(jnp.bfloat16).reshape(shape)


def attention(place, low, high, qdo, pieces):
    row_count = qdo[0].shape[1]
    rows = 4 * row_count
    keys = 8 * rows
    width = pieces[0].shape[2]
    vmem = pl.BlockSpec(memory_space=pltpu.VMEM)
    smem = pl.BlockSpec(memory_space=pltpu.SMEM)
    grads = jax.ShapeDtypeStruct((4, 4, row_count, width), jnp.bfloat16)
    return pl.pallas_call(
        attention_kernel,
        out_shape=(jax.ShapeDtypeStruct((4, row_count, GROUP * HEAD_SIZE), jnp.bfloat16), grads, grads),
        in_specs=[smem] + [vmem] * 16,
        out_specs=(vmem, vmem, vmem),
        scratch_shapes=[
            pltpu.VMEM((keys, rows), jnp.float32),
            pltpu.VMEM((HEAD_SIZE, keys), jnp.bfloat16),
            pltpu.VMEM((keys, rows), jnp.float32),
            pltpu.VMEM((keys, rows), jnp.float32),
            pltpu.VMEM((keys, rows), jnp.float32),
            pltpu.VMEM((keys, width), jnp.float32),
        ],
        compiler_params=pltpu.CompilerParams(vmem_limit_bytes=48 * 1024 * 1024),
        cost_estimate=pl.CostEstimate(
            flops=10 * keys * rows * HEAD_SIZE * GROUP, bytes_accessed=4 * 1024 * 1024,
            transcendentals=keys * rows * GROUP),
    )(place, low, high, *qdo, *pieces)


PLANE = ("xh", "zp")
FINAL = ("xh", "zp", "y", "xl")
RING = 4


def swapped(array, axes, by, count):
    return lax.ppermute(array, axes, [(i, i ^ by) for i in range(count)])


def turned(array, by):
    return lax.ppermute(array, "zq", [(i, (i + by) % RING) for i in range(RING)])


def on_device(queries, key_vectors, value_vectors, output_gradient, positions, segments):
    window_count, row_count, _ = queries.shape
    across, pair = lax.axis_index("xh"), lax.axis_index("zp")
    place = across * 2 + pair

    code = segments * CODE_SPAN + positions
    room = ((0, 0), (0, HEAD_SIZE - row_count))
    meta = jnp.concatenate([jnp.pad(code // 128, room), jnp.pad(code % 128, room)], axis=1).astype(jnp.bfloat16)
    meta = jnp.pad(meta[:, None, :], ((0, 0), (0, META_ROWS - 1), (0, 0)))
    packed = jnp.concatenate([jnp.concatenate([key_vectors, value_vectors], axis=2), meta], axis=1)

    def window_of(array, r):
        return lax.dynamic_index_in_dim(array, place ^ r, 0, keepdims=False)

    kv_parts = [window_of(packed, 0)] + [swapped(window_of(packed, r), PLANE, r, 4) for r in (1, 2, 3)]
    qdo = [jnp.stack([window_of(queries, r), window_of(output_gradient, r)]) for r in range(4)]
    qdo = [qdo[0]] + [swapped(qdo[r], PLANE, r, 4) for r in (1, 2, 3)]
    own = jnp.stack(kv_parts)
    before = turned(own, 1)
    after = turned(own, -1)
    opposite_a = turned(before[0:2], 1)
    opposite_b = turned(after[2:4], -1)
    near = [own, after, opposite_a, opposite_b, before]
    far = [swapped(piece, "core", 1, 2) for piece in near]
    pieces = near + far

    digits = own[:, row_count, :].astype(jnp.float32)
    high = (digits[:, 0:row_count] * 128.0 + digits[:, HEAD_SIZE:HEAD_SIZE + row_count]).reshape(1, -1)
    low = jnp.floor(high * (1.0 / CODE_SPAN)) * CODE_SPAN
    dq, near_grad, far_grad = attention(place.reshape(1).astype(jnp.int32), low, high, qdo, pieces)

    def plus(*arrays):
        return sum(a.astype(jnp.float32) for a in arrays).astype(jnp.bfloat16)

    half = plus(near_grad, swapped(far_grad, "core", 1, 2))
    up = turned(half[2, 0:2], 1)
    down = turned(half[2, 2:4], -1)
    to_up = jnp.concatenate([plus(half[1, 0:2], up), half[1, 2:4]])
    to_down = jnp.concatenate([half[3, 0:2], plus(half[3, 2:4], down)])
    dkv_own = plus(half[0], turned(to_up, 1), turned(to_down, -1))
    flip = dkv_own.reshape((2, 2) + dkv_own.shape[1:])
    flip = jnp.where(across == 1, flip[::-1], flip)
    flip = jnp.where(pair == 1, flip[:, ::-1], flip)

    heads = KEY_VALUE_HEADS
    out_rows = row_count // heads
    dq_final = lax.all_to_all(dq.reshape(window_count * heads, out_rows, GROUP * HEAD_SIZE), FINAL, 0, 0, tiled=True)
    dkv_final = lax.all_to_all(flip.reshape(window_count * heads, out_rows, 2 * HEAD_SIZE), FINAL, 0, 0, tiled=True)

    def merged(array):
        width = array.shape[-1]
        return array.reshape(window_count, heads, out_rows, width).transpose(0, 2, 1, 3).reshape(window_count, out_rows, heads * width)

    return (
        merged(dq_final),
        merged(dkv_final[..., 0:HEAD_SIZE]),
        merged(dkv_final[..., HEAD_SIZE:2 * HEAD_SIZE]),
    )


def solution(mesh):
    fine = Mesh(mesh.devices.reshape(2, RING, 2, 2, 4, 2), ("xh", "zq", "zp", "core", "y", "xl"))
    ctx, head = ("xh", "zq", "zp", "core"), ("y", "xl")
    vectors = P(None, ctx, head)
    out = P(None, ctx + head, None)
    return jax.shard_map(
        on_device,
        mesh=fine,
        in_specs=(vectors, vectors, vectors, vectors, P(None, ctx), P(None, ctx)),
        out_specs=(out, out, out),
        check_vma=False,
    )
```

```python
import functools
import math

import jax
import jax.numpy as jnp
from jax import lax
from jax.experimental import pallas as pl
from jax.experimental.pallas import tpu as pltpu
from jax.sharding import Mesh, PartitionSpec as P

QUERY_HEADS = 64
KEY_VALUE_HEADS = 8
HEAD_SIZE = 128
GROUP = QUERY_HEADS // KEY_VALUE_HEADS
NEG_BIG = -1e30
CODE_SPAN = 2048
META_ROWS = 16
HEADS_PER_STEP = 2
SCALE = 1.0 / math.sqrt(HEAD_SIZE)
EXP2_SCALE = SCALE * math.log2(math.e)

NT = (((1,), (1,)), ((), ()))
NN = (((1,), (0,)), ((), ()))


def dot(a, b, dims):
    return lax.dot_general(a, b, dims, preferred_element_type=jnp.float32)


def key_spans(piece_refs, row_count):
    spans, start = [], 0
    for ref in piece_refs:
        size = ref.shape[0] * row_count
        spans.append((ref, slice(start, start + size), size))
        start += size
    return spans, start


def keys_of(ref, size, row_count):
    return ref[:, 0:row_count, 0:HEAD_SIZE].reshape(size, HEAD_SIZE)


def values_of(ref, size, row_count):
    return ref[:, 0:row_count, HEAD_SIZE:2 * HEAD_SIZE].reshape(size, HEAD_SIZE)


def fill_bias(bias_ref, spans, low_ref, high_ref, row_count):
    rows = low_ref.shape[1]
    for ref, part, size in spans:
        for b in range(ref.shape[0]):
            digits = ref[b, row_count:row_count + META_ROWS, :].astype(jnp.float32)[0:1, :]
            code = digits[:, 0:128] * 128.0 + digits[:, 128:256]
            column = jnp.broadcast_to(code, (128, 128)).T[0:row_count, :]
            begin = part.start + b * row_count
            for r in range(rows // 128):
                low = low_ref[:, r * 128:(r + 1) * 128]
                high = high_ref[:, r * 128:(r + 1) * 128]
                allowed = (column >= low) & (column <= high)
                bias_ref[begin:begin + row_count, r * 128:(r + 1) * 128] = jnp.where(allowed, 0.0, NEG_BIG)


def rows_of(row_refs, lanes, row_count):
    q = jnp.concatenate([ref[0:row_count, lanes] for ref in row_refs], axis=0)
    do = jnp.concatenate([ref[row_count:2 * row_count, lanes] for ref in row_refs], axis=0)
    return q, do


def stats_kernel(first, count, low_ref, high_ref, *refs):
    row_refs, piece_refs, rest = refs[0:4], refs[4:4 + count], refs[4 + count:]
    if first:
        state_ref, bias_ref = rest
    else:
        before_ref, state_ref, bias_ref = rest
    rows = low_ref.shape[1]
    row_count = rows // 4
    spans, _ = key_spans(piece_refs, row_count)
    fill_bias(bias_ref, spans, low_ref, high_ref, row_count)

    def head(h, carry):
        lanes = pl.ds(pl.multiple_of(h * HEAD_SIZE, HEAD_SIZE), HEAD_SIZE)
        q, do = rows_of(row_refs, lanes, row_count)
        if first:
            top = jnp.full((1, rows), NEG_BIG, jnp.float32)
            total = jnp.zeros((1, rows), jnp.float32)
            cross = jnp.zeros((1, rows), jnp.float32)
        else:
            top, total, cross = before_ref[h, 0:1, :], before_ref[h, 1:2, :], before_ref[h, 2:3, :]
        for ref, part, size in spans:
            s = dot(keys_of(ref, size, row_count), q, NT) * EXP2_SCALE + bias_ref[part, :]
            dp = dot(values_of(ref, size, row_count), do, NT)
            peak = jnp.max(s.reshape(size // 8, 8, rows), axis=0)
            new = jnp.maximum(top, jnp.max(peak, axis=0, keepdims=True))
            p = jnp.exp2(s - new)
            factor = jnp.exp2(top - new)
            part_sum = jnp.sum(p.reshape(size // 8, 8, rows), axis=0)
            part_dot = jnp.sum((p * dp).reshape(size // 8, 8, rows), axis=0)
            total = total * factor + jnp.sum(part_sum, axis=0, keepdims=True)
            cross = cross * factor + jnp.sum(part_dot, axis=0, keepdims=True)
            top = new
        state_ref[h, 0:1, :] = top
        state_ref[h, 1:2, :] = total
        state_ref[h, 2:3, :] = cross
        return carry

    lax.fori_loop(0, GROUP, head, 0)


def grads_kernel(first, last, count, place_ref, low_ref, high_ref, state_ref, *refs):
    row_refs, piece_refs, rest = refs[0:4], refs[4:4 + count], refs[4 + count:]
    if not first:
        before_ref, rest = rest[0], rest[1:]
    dq_ref, near_ref, far_ref, bias_ref, kt_ref, ds_ref, acc_ref = rest
    rows = low_ref.shape[1]
    row_count = rows // 4
    heads = HEADS_PER_STEP
    spans, keys = key_spans(piece_refs, row_count)
    fill_bias(bias_ref, spans, low_ref, high_ref, row_count)
    for ref, part, size in spans:
        kt_ref[:, part] = keys_of(ref, size, row_count).T
    acc_ref[...] = jnp.zeros_like(acc_ref)
    place = place_ref[0]

    def step(g, carry):
        q, do, offsets, deltas, lanes = [], [], [], [], []
        for j in range(heads):
            h = g * heads + j
            lanes.append(pl.ds(pl.multiple_of(h * HEAD_SIZE, HEAD_SIZE), HEAD_SIZE))
            one_q, one_do = rows_of(row_refs, lanes[j], row_count)
            q.append(one_q)
            do.append(one_do)
            total = state_ref[h, 1:2, :]
            offsets.append(state_ref[h, 0:1, :] + jnp.log2(total))
            deltas.append(state_ref[h, 2:3, :] / total)
        q_all, do_all = jnp.concatenate(q, axis=0), jnp.concatenate(do, axis=0)
        for ref, part, size in spans:
            p_low, ds_low = [], []
            for j in range(heads):
                s = dot(keys_of(ref, size, row_count), q[j], NT) * EXP2_SCALE + bias_ref[part, :]
                dp = dot(values_of(ref, size, row_count), do[j], NT)
                p = jnp.exp2(s - offsets[j])
                p_low.append(p.astype(jnp.bfloat16))
                ds_low.append((p * (dp - deltas[j])).astype(jnp.bfloat16))
            p_all, ds_all = jnp.concatenate(p_low, axis=1), jnp.concatenate(ds_low, axis=1)
            ds_ref[part, :] = ds_all
            acc_ref[part, HEAD_SIZE:2 * HEAD_SIZE] += dot(p_all, do_all, NN)
            acc_ref[part, 0:HEAD_SIZE] += dot(ds_all, q_all, NN)
        dqt = dot(kt_ref[...], ds_ref[...], NN)
        for j in range(heads):
            part = dqt[:, j * rows:(j + 1) * rows]
            if not first:
                part = part + before_ref[g * heads + j]
            if last:
                dq = (part * SCALE).T.astype(jnp.bfloat16)
                for r in range(4):
                    dq_ref[place ^ r, :, lanes[j]] = dq[r * row_count:(r + 1) * row_count, :]
            else:
                dq_ref[g * heads + j] = part
        return carry

    lax.fori_loop(0, GROUP // heads, step, 0)
    sources = near_ref.shape[0]
    for i, out_ref in enumerate((near_ref, far_ref)):
        part = slice(i * sources * row_count, (i + 1) * sources * row_count)
        shape = (sources, row_count, HEAD_SIZE)
        out_ref[:, :, 0:HEAD_SIZE] = (acc_ref[part, 0:HEAD_SIZE] * SCALE).astype(jnp.bfloat16).reshape(shape)
        out_ref[:, :, HEAD_SIZE:2 * HEAD_SIZE] = acc_ref[part, HEAD_SIZE:2 * HEAD_SIZE].astype(jnp.bfloat16).reshape(shape)


VMEM = pl.BlockSpec(memory_space=pltpu.VMEM)
SMEM = pl.BlockSpec(memory_space=pltpu.SMEM)


def stats(low, high, row_arrays, pieces, state):
    rows = low.shape[1]
    keys = sum(piece.shape[0] for piece in pieces) * rows // 4
    first = state is None
    inputs = (low, high, *row_arrays, *pieces) + (() if first else (state,))
    return pl.pallas_call(
        functools.partial(stats_kernel, first, len(pieces)),
        out_shape=jax.ShapeDtypeStruct((GROUP, 8, rows), jnp.float32),
        in_specs=[VMEM] * len(inputs),
        out_specs=VMEM,
        scratch_shapes=[pltpu.VMEM((keys, rows), jnp.float32)],
        compiler_params=pltpu.CompilerParams(vmem_limit_bytes=24 * 1024 * 1024),
        cost_estimate=pl.CostEstimate(
            flops=8 * keys * rows * HEAD_SIZE * GROUP, bytes_accessed=1024 * 1024,
            transcendentals=keys * rows * GROUP),
    )(*inputs)


def grads(place, low, high, state, row_arrays, pieces, before, last):
    rows = low.shape[1]
    row_count = rows // 4
    sources = sum(piece.shape[0] for piece in pieces)
    keys = sources * row_count
    width = 2 * HEAD_SIZE
    first = before is None
    inputs = (low, high, state, *row_arrays, *pieces) + (() if first else (before,))
    part = jax.ShapeDtypeStruct((sources // 2, row_count, width), jnp.bfloat16)
    if last:
        dq = jax.ShapeDtypeStruct((4, row_count, GROUP * HEAD_SIZE + width), jnp.bfloat16)
    else:
        dq = jax.ShapeDtypeStruct((GROUP, HEAD_SIZE, rows), jnp.float32)
    return pl.pallas_call(
        functools.partial(grads_kernel, first, last, len(pieces)),
        out_shape=(dq, part, part),
        in_specs=[SMEM] + [VMEM] * len(inputs),
        out_specs=(VMEM, VMEM, VMEM),
        scratch_shapes=[
            pltpu.VMEM((keys, rows), jnp.float32),
            pltpu.VMEM((HEAD_SIZE, keys), jnp.bfloat16),
            pltpu.VMEM((keys, HEADS_PER_STEP * rows), jnp.bfloat16),
            pltpu.VMEM((keys, width), jnp.float32),
        ],
        compiler_params=pltpu.CompilerParams(vmem_limit_bytes=24 * 1024 * 1024),
        cost_estimate=pl.CostEstimate(
            flops=16 * keys * rows * HEAD_SIZE * GROUP, bytes_accessed=2 * 1024 * 1024,
            transcendentals=keys * rows * GROUP),
    )(place, *inputs)


def pack_kernel(place_ref, code_ref, q_ref, do_ref, k_ref, v_ref, *out_refs):
    row_count = q_ref.shape[1]
    wide = q_ref.shape[2]
    fold = wide // (2 * HEAD_SIZE)
    lines = row_count // fold
    half = fold * HEAD_SIZE
    place = place_ref[0]
    for r, out_ref in enumerate(out_refs):
        w = place ^ r
        out_ref[0:row_count, :] = q_ref[w]
        out_ref[row_count:2 * row_count, :] = do_ref[w]
        begin = 2 * row_count
        for g in range(fold):
            from_rows = slice(g * lines, (g + 1) * lines)
            out_ref[begin:begin + lines, g * HEAD_SIZE:(g + 1) * HEAD_SIZE] = k_ref[w, from_rows, :]
            out_ref[begin:begin + lines, half + g * HEAD_SIZE:half + (g + 1) * HEAD_SIZE] = v_ref[w, from_rows, :]
        code = code_ref[pl.ds(w, 1), :]
        begin += lines
        for i, digit in enumerate((code >> 7, code & 127)):
            spread = jnp.broadcast_to(digit.astype(jnp.float32), (META_ROWS, 128)).astype(jnp.bfloat16)
            out_ref[begin:begin + META_ROWS, i * 128:(i + 1) * 128] = spread
        out_ref[begin:begin + META_ROWS, 256:] = jnp.zeros((META_ROWS, wide - 256), jnp.bfloat16)


def unpack_kernel(*refs):
    load_refs, (own_ref, low_ref, high_ref) = refs[0:4], refs[4:]
    row_count = own_ref.shape[1] - META_ROWS
    wide = load_refs[0].shape[1]
    fold = wide // (2 * HEAD_SIZE)
    lines = row_count // fold
    half = fold * HEAD_SIZE
    codes = []
    for r, ref in enumerate(load_refs):
        begin = 2 * row_count
        for g in range(fold):
            to_rows = slice(g * lines, (g + 1) * lines)
            own_ref[r, to_rows, 0:HEAD_SIZE] = ref[begin:begin + lines, g * HEAD_SIZE:(g + 1) * HEAD_SIZE]
            own_ref[r, to_rows, HEAD_SIZE:] = ref[begin:begin + lines, half + g * HEAD_SIZE:half + (g + 1) * HEAD_SIZE]
        meta = ref[begin + lines:begin + lines + META_ROWS, 0:256]
        own_ref[r, row_count:, :] = meta
        digits = meta.astype(jnp.float32)[0:8, :]
        codes.append(digits[:, 0:128] * 128.0 + digits[:, 128:256])
    lane = lax.broadcasted_iota(jnp.int32, (8, 128), 1)
    for i in range(2):
        code = jnp.where(lane < row_count, codes[2 * i], pltpu.roll(codes[2 * i + 1], row_count, 1))[0:1, :]
        high_ref[:, i * 128:(i + 1) * 128] = code
        low_ref[:, i * 128:(i + 1) * 128] = jnp.floor(code * (1.0 / CODE_SPAN)) * CODE_SPAN


def pack(place, code, queries, output_gradient, key_vectors, value_vectors):
    row_count, wide = queries.shape[1:]
    load = jax.ShapeDtypeStruct((2 * row_count + row_count * 2 * HEAD_SIZE // wide + META_ROWS, wide), jnp.bfloat16)
    return pl.pallas_call(
        pack_kernel,
        out_shape=(load,) * 4,
        in_specs=[SMEM] + [VMEM] * 5,
        out_specs=(VMEM,) * 4,
        compiler_params=pltpu.CompilerParams(vmem_limit_bytes=24 * 1024 * 1024),
    )(place, code, queries, output_gradient, key_vectors, value_vectors)


def unpack(loads, row_count):
    row = jax.ShapeDtypeStruct((1, 4 * row_count), jnp.float32)
    own = jax.ShapeDtypeStruct((4, row_count + META_ROWS, 2 * HEAD_SIZE), jnp.bfloat16)
    return pl.pallas_call(
        unpack_kernel,
        out_shape=(own, row, row),
        in_specs=[VMEM] * 4,
        out_specs=(VMEM,) * 3,
        compiler_params=pltpu.CompilerParams(vmem_limit_bytes=24 * 1024 * 1024),
    )(*loads)


PLANE = ("xh", "zp")
FINAL = ("xh", "zp", "y", "xl")
RING = 4


def swapped(array, axes, by, count):
    return lax.ppermute(array, axes, [(i, i ^ by) for i in range(count)])


def other_core(array):
    return swapped(array, "core", 1, 2)


def turned(array, by):
    return lax.ppermute(array, "zq", [(i, (i + by) % RING) for i in range(RING)])


def plus(*arrays):
    return sum(a.astype(jnp.float32) for a in arrays).astype(jnp.bfloat16)


def on_device(queries, key_vectors, value_vectors, output_gradient, positions, segments):
    window_count, row_count, _ = queries.shape
    across, pair = lax.axis_index("xh"), lax.axis_index("zp")
    place = across * 2 + pair

    spot = place.reshape(1).astype(jnp.int32)
    code = jnp.pad(segments * CODE_SPAN + positions, ((0, 0), (0, 128 - row_count)))
    loads = pack(spot, code, queries, output_gradient, key_vectors, value_vectors)
    row_arrays = [loads[0]] + [swapped(loads[r], PLANE, r, 4) for r in (1, 2, 3)]
    own, low, high = unpack(row_arrays, row_count)

    tied = lax.optimization_barrier
    before = turned(own, 1)
    after = turned(own, -1)
    far_own = other_core(own)
    state = stats(low, high, row_arrays, [own], None)
    state, before, after = tied((state, before, after))
    opposite = (turned(before[0:2], 1), turned(after[2:4], -1))
    far_after, far_before = other_core(after), other_core(before)
    state = stats(low, high, row_arrays, [after, before, far_own, far_after, far_before], state)
    state, opposite = tied((state, opposite))
    far_opposite = tuple(other_core(piece) for piece in opposite)
    state = stats(low, high, row_arrays, [*opposite, *far_opposite], state)

    dq, near_2, far_2 = grads(spot, low, high, state, row_arrays, [*opposite, *far_opposite], None, False)
    sum_2 = plus(near_2, other_core(far_2))
    spot, dq, first_up, first_down = tied((spot, dq, sum_2[0:2], sum_2[2:4]))
    up, down = turned(first_up, 1), turned(first_down, -1)
    dq, near_1, far_1 = grads(spot, low, high, state, row_arrays, [after, before, far_after, far_before], dq, False)
    dq, near_1, far_1, up, down = tied((dq, near_1, far_1, up, down))
    sum_1 = plus(near_1, other_core(far_1))
    next_up = jnp.concatenate([plus(sum_1[0:2], up), sum_1[2:4]])
    next_down = jnp.concatenate([sum_1[4:6], plus(sum_1[6:8], down)])
    spot, dq, next_up, next_down = tied((spot, dq, next_up, next_down))
    to_up, to_down = turned(next_up, 1), turned(next_down, -1)
    dq, near_0, far_0 = grads(spot, low, high, state, row_arrays, [own, far_own], dq, True)
    dq, near_0, far_0, to_up, to_down = tied((dq, near_0, far_0, to_up, to_down))
    dkv_own = plus(near_0, other_core(far_0), to_up, to_down)

    flip = dkv_own.reshape((2, 2) + dkv_own.shape[1:])
    flip = jnp.where(across == 1, flip[::-1], flip)
    flip = jnp.where(pair == 1, flip[:, ::-1], flip)

    heads = KEY_VALUE_HEADS
    out_rows = row_count // heads
    split = GROUP * HEAD_SIZE
    leaving = dq.at[:, :, split:].set(flip.reshape(dkv_own.shape)).reshape(window_count * heads, out_rows, split + 2 * HEAD_SIZE)
    final = lax.all_to_all(leaving, FINAL, 0, 0, tiled=True)

    def merged(array):
        width = array.shape[-1]
        return array.reshape(window_count, heads, out_rows, width).transpose(0, 2, 1, 3).reshape(window_count, out_rows, heads * width)

    return (
        merged(final[..., 0:split]),
        merged(final[..., split:split + HEAD_SIZE]),
        merged(final[..., split + HEAD_SIZE:]),
    )


def solution(mesh):
    fine = Mesh(mesh.devices.reshape(2, RING, 2, 2, 4, 2), ("xh", "zq", "zp", "core", "y", "xl"))
    ctx, head = ("xh", "zq", "zp", "core"), ("y", "xl")
    vectors = P(None, ctx, head)
    out = P(None, ctx + head, None)
    return jax.shard_map(
        on_device,
        mesh=fine,
        in_specs=(vectors, vectors, vectors, vectors, P(None, ctx), P(None, ctx)),
        out_specs=(out, out, out),
        check_vma=False,
    )
```

```python
import functools
import math

import jax
import jax.numpy as jnp
from jax import lax
from jax.experimental import pallas as pl
from jax.experimental.pallas import tpu as pltpu
from jax.sharding import Mesh, PartitionSpec as P

QUERY_HEADS = 64
KEY_VALUE_HEADS = 8
HEAD_SIZE = 128
GROUP = QUERY_HEADS // KEY_VALUE_HEADS
NEG_BIG = -1e30
CODE_SPAN = 2048
META_ROWS = 16
HEADS_PER_STEP = 4
SCALE = 1.0 / math.sqrt(HEAD_SIZE)
EXP2_SCALE = SCALE * math.log2(math.e)

NT = (((1,), (1,)), ((), ()))
NN = (((1,), (0,)), ((), ()))


def dot(a, b, dims):
    return lax.dot_general(a, b, dims, preferred_element_type=jnp.float32)


def key_spans(piece_refs, row_count):
    spans, start = [], 0
    for ref in piece_refs:
        size = ref.shape[0] * row_count
        spans.append((ref, slice(start, start + size), size))
        start += size
    return spans, start


def keys_of(ref, size, row_count):
    return ref[:, 0:row_count, 0:HEAD_SIZE].reshape(size, HEAD_SIZE)


def values_of(ref, size, row_count):
    return ref[:, 0:row_count, HEAD_SIZE:2 * HEAD_SIZE].reshape(size, HEAD_SIZE)


def fill_bias(bias_ref, spans, low_ref, high_ref, row_count):
    rows = low_ref.shape[1]
    for ref, part, size in spans:
        for b in range(ref.shape[0]):
            digits = ref[b, row_count:row_count + META_ROWS, :].astype(jnp.float32)[0:1, :]
            code = digits[:, 0:128] * 128.0 + digits[:, 128:256]
            column = jnp.broadcast_to(code, (128, 128)).T[0:row_count, :]
            begin = part.start + b * row_count
            for r in range(rows // 128):
                low = low_ref[:, r * 128:(r + 1) * 128]
                high = high_ref[:, r * 128:(r + 1) * 128]
                allowed = (column >= low) & (column <= high)
                bias_ref[begin:begin + row_count, r * 128:(r + 1) * 128] = jnp.where(allowed, 0.0, NEG_BIG)


def rows_of(row_refs, lanes, row_count):
    q = jnp.concatenate([ref[0:row_count, lanes] for ref in row_refs], axis=0)
    do = jnp.concatenate([ref[row_count:2 * row_count, lanes] for ref in row_refs], axis=0)
    return q, do


def absorbed(top, total, cross, scores, softmax_grads):
    rows = top.shape[1]
    new = top
    for s in scores:
        peak = jnp.max(s.reshape(s.shape[0] // 8, 8, rows), axis=0)
        new = jnp.maximum(new, jnp.max(peak, axis=0, keepdims=True))
    factor = jnp.exp2(top - new)
    total, cross = total * factor, cross * factor
    weights = [jnp.exp2(s - new) for s in scores]
    for p, dp in zip(weights, softmax_grads):
        part_sum = jnp.sum(p.reshape(p.shape[0] // 8, 8, rows), axis=0)
        part_dot = jnp.sum((p * dp).reshape(p.shape[0] // 8, 8, rows), axis=0)
        total = total + jnp.sum(part_sum, axis=0, keepdims=True)
        cross = cross + jnp.sum(part_dot, axis=0, keepdims=True)
    return new, total, cross, weights


def stats_kernel(count, low_ref, high_ref, *refs):
    row_refs, piece_refs, (state_ref, bias_ref) = refs[0:4], refs[4:4 + count], refs[4 + count:]
    rows = low_ref.shape[1]
    row_count = rows // 4
    spans, _ = key_spans(piece_refs, row_count)
    fill_bias(bias_ref, spans, low_ref, high_ref, row_count)

    def step(g, carry):
        for j in range(HEADS_PER_STEP):
            h = g * HEADS_PER_STEP + j
            lanes = pl.ds(pl.multiple_of(h * HEAD_SIZE, HEAD_SIZE), HEAD_SIZE)
            q, do = rows_of(row_refs, lanes, row_count)
            top = jnp.full((1, rows), NEG_BIG, jnp.float32)
            total = jnp.zeros((1, rows), jnp.float32)
            cross = jnp.zeros((1, rows), jnp.float32)
            for ref, part, size in spans:
                s = dot(keys_of(ref, size, row_count), q, NT) * EXP2_SCALE + bias_ref[part, :]
                dp = dot(values_of(ref, size, row_count), do, NT)
                top, total, cross = absorbed(top, total, cross, [s], [dp])[0:3]
            state_ref[h, 0:1, :] = top
            state_ref[h, 1:2, :] = total
            state_ref[h, 2:3, :] = cross
        return carry

    lax.fori_loop(0, GROUP // HEADS_PER_STEP, step, 0)


def grads_kernel(first, last, count, place_ref, low_ref, high_ref, state_ref, *refs):
    row_refs, piece_refs, rest = refs[0:4], refs[4:4 + count], refs[4 + count:]
    if first:
        dq_ref, near_ref, far_ref, final_ref, bias_ref, kt_ref, ds_ref, acc_ref = rest
    else:
        before_ref, dq_ref, near_ref, far_ref, bias_ref, kt_ref, ds_ref, acc_ref = rest
    rows = low_ref.shape[1]
    row_count = rows // 4
    heads = HEADS_PER_STEP
    spans, keys = key_spans(piece_refs, row_count)
    fill_bias(bias_ref, spans, low_ref, high_ref, row_count)
    for ref, part, size in spans:
        kt_ref[:, part] = keys_of(ref, size, row_count).T
    acc_ref[...] = jnp.zeros_like(acc_ref)
    place = place_ref[0]

    def step(g, carry):
        q, do, lanes, p_low, ds_low = [], [], [], [], []
        for j in range(heads):
            h = g * heads + j
            lanes.append(pl.ds(pl.multiple_of(h * HEAD_SIZE, HEAD_SIZE), HEAD_SIZE))
            one_q, one_do = rows_of(row_refs, lanes[j], row_count)
            q.append(one_q)
            do.append(one_do)

            def products(ref, part, size):
                s = dot(keys_of(ref, size, row_count), one_q, NT) * EXP2_SCALE + bias_ref[part, :]
                return s, dot(values_of(ref, size, row_count), one_do, NT)

            if first:
                pairs = [products(*span) for span in spans]
                top, total, cross, weights = absorbed(
                    state_ref[h, 0:1, :], state_ref[h, 1:2, :], state_ref[h, 2:3, :],
                    [s for s, _ in pairs], [dp for _, dp in pairs])
                inverse = 1.0 / total
                delta = cross * inverse
                final_ref[h, 0:1, :] = top + jnp.log2(total)
                final_ref[h, 1:2, :] = delta
                softmax = [p * inverse for p in weights]
                softmax_grads = [dp for _, dp in pairs]
            else:
                offset, delta = state_ref[h, 0:1, :], state_ref[h, 1:2, :]
                softmax, softmax_grads = [], []
                for span in spans:
                    s, dp = products(*span)
                    softmax.append(jnp.exp2(s - offset))
                    softmax_grads.append(dp)
            p_low.append([p.astype(jnp.bfloat16) for p in softmax])
            ds_low.append([(p * (dp - delta)).astype(jnp.bfloat16) for p, dp in zip(softmax, softmax_grads)])
        q_all, do_all = jnp.concatenate(q, axis=0), jnp.concatenate(do, axis=0)
        for i, (ref, part, size) in enumerate(spans):
            p_all = jnp.concatenate([p_low[j][i] for j in range(heads)], axis=1)
            ds_all = jnp.concatenate([ds_low[j][i] for j in range(heads)], axis=1)
            ds_ref[part, :] = ds_all
            acc_ref[part, HEAD_SIZE:2 * HEAD_SIZE] += dot(p_all, do_all, NN)
            acc_ref[part, 0:HEAD_SIZE] += dot(ds_all, q_all, NN)
        dqt = dot(kt_ref[...], ds_ref[...], NN)
        for j in range(heads):
            part = dqt[:, j * rows:(j + 1) * rows]
            if not first:
                part = part + before_ref[g * heads + j]
            if last:
                dq = (part * SCALE).T.astype(jnp.bfloat16)
                for r in range(4):
                    dq_ref[place ^ r, :, lanes[j]] = dq[r * row_count:(r + 1) * row_count, :]
            else:
                dq_ref[g * heads + j] = part
        return carry

    lax.fori_loop(0, GROUP // heads, step, 0)
    sources = near_ref.shape[0]
    for i, out_ref in enumerate((near_ref, far_ref)):
        part = slice(i * sources * row_count, (i + 1) * sources * row_count)
        shape = (sources, row_count, HEAD_SIZE)
        out_ref[:, :, 0:HEAD_SIZE] = (acc_ref[part, 0:HEAD_SIZE] * SCALE).astype(jnp.bfloat16).reshape(shape)
        out_ref[:, :, HEAD_SIZE:2 * HEAD_SIZE] = acc_ref[part, HEAD_SIZE:2 * HEAD_SIZE].astype(jnp.bfloat16).reshape(shape)


VMEM = pl.BlockSpec(memory_space=pltpu.VMEM)
SMEM = pl.BlockSpec(memory_space=pltpu.SMEM)
ANY = pl.BlockSpec(memory_space=pltpu.HBM)


def stats(low, high, row_arrays, pieces):
    rows = low.shape[1]
    keys = sum(piece.shape[0] for piece in pieces) * rows // 4
    inputs = (low, high, *row_arrays, *pieces)
    return pl.pallas_call(
        functools.partial(stats_kernel, len(pieces)),
        out_shape=jax.ShapeDtypeStruct((GROUP, 8, rows), jnp.float32),
        in_specs=[VMEM] * len(inputs),
        out_specs=VMEM,
        scratch_shapes=[pltpu.VMEM((keys, rows), jnp.float32)],
        compiler_params=pltpu.CompilerParams(vmem_limit_bytes=32 * 1024 * 1024),
        cost_estimate=pl.CostEstimate(
            flops=8 * keys * rows * HEAD_SIZE * GROUP, bytes_accessed=1024 * 1024,
            transcendentals=keys * rows * GROUP),
    )(*inputs)


def grads(place, low, high, state, row_arrays, pieces, before, last):
    rows = low.shape[1]
    row_count = rows // 4
    sources = sum(piece.shape[0] for piece in pieces)
    keys = sources * row_count
    width = 2 * HEAD_SIZE
    first = before is None
    inputs = (low, high, state, *row_arrays, *pieces) + (() if first else (before,))
    part = jax.ShapeDtypeStruct((sources // 2, row_count, width), jnp.bfloat16)
    extra = (jax.ShapeDtypeStruct((GROUP, 8, rows), jnp.float32),) if first else ()
    if last:
        dq = jax.ShapeDtypeStruct((4, row_count, GROUP * HEAD_SIZE + width), jnp.bfloat16)
    else:
        dq = jax.ShapeDtypeStruct((GROUP, HEAD_SIZE, rows), jnp.float32)
    return pl.pallas_call(
        functools.partial(grads_kernel, first, last, len(pieces)),
        out_shape=(dq, part, part) + extra,
        in_specs=[SMEM] + [VMEM] * len(inputs),
        out_specs=(VMEM,) * (3 + len(extra)),
        scratch_shapes=[
            pltpu.VMEM((keys, rows), jnp.float32),
            pltpu.VMEM((HEAD_SIZE, keys), jnp.bfloat16),
            pltpu.VMEM((keys, HEADS_PER_STEP * rows), jnp.bfloat16),
            pltpu.VMEM((keys, width), jnp.float32),
        ],
        compiler_params=pltpu.CompilerParams(vmem_limit_bytes=32 * 1024 * 1024),
        cost_estimate=pl.CostEstimate(
            flops=16 * keys * rows * HEAD_SIZE * GROUP, bytes_accessed=2 * 1024 * 1024,
            transcendentals=keys * rows * GROUP),
    )(place, *inputs)


def copies(pairs, sems):
    started = [pltpu.make_async_copy(source, target, sems.at[i]) for i, (source, target) in enumerate(pairs)]
    for copy in started:
        copy.start()
    for copy in started:
        copy.wait()


def pack_keys_kernel(place_ref, code_ref, k_ref, v_ref, self_ref, pair_ref, across_ref, sems):
    row_count = k_ref.shape[1]
    place = place_ref[0]
    targets = ((0, self_ref), (1, pair_ref.at[0]), (3, pair_ref.at[1]), (2, across_ref))
    pairs = []
    for r, target in targets:
        pairs.append((k_ref.at[place ^ r], target.at[0:row_count, 0:HEAD_SIZE]))
        pairs.append((v_ref.at[place ^ r], target.at[0:row_count, HEAD_SIZE:2 * HEAD_SIZE]))
    for r, target in targets:
        code = code_ref[pl.ds(place ^ r, 1), :]
        for i, digit in enumerate((code >> 7, code & 127)):
            spread = jnp.broadcast_to(digit.astype(jnp.float32), (META_ROWS, 128)).astype(jnp.bfloat16)
            target[row_count:row_count + META_ROWS, i * 128:(i + 1) * 128] = spread
    copies(pairs, sems)


def pack_rows_kernel(place_ref, q_ref, do_ref, *refs):
    out_refs, sems = refs[0:4], refs[4]
    row_count = q_ref.shape[1]
    place = place_ref[0]
    pairs = []
    for r, target in enumerate(out_refs):
        pairs.append((q_ref.at[place ^ r], target.at[0:row_count]))
        pairs.append((do_ref.at[place ^ r], target.at[row_count:2 * row_count]))
    copies(pairs, sems)


def own_kernel(self_ref, pair_ref, across_ref, own_ref, low_ref, high_ref):
    row_count = self_ref.shape[0] - META_ROWS
    codes = []
    for r, value in enumerate((self_ref[...], pair_ref[0], across_ref[0], across_ref[1])):
        own_ref[r] = value
        digits = value[row_count:, :].astype(jnp.float32)[0:8, :]
        codes.append(digits[:, 0:128] * 128.0 + digits[:, 128:256])
    lane = lax.broadcasted_iota(jnp.int32, (8, 128), 1)
    for i in range(2):
        code = jnp.where(lane < row_count, codes[2 * i], pltpu.roll(codes[2 * i + 1], row_count, 1))[0:1, :]
        high_ref[:, i * 128:(i + 1) * 128] = code
        low_ref[:, i * 128:(i + 1) * 128] = jnp.floor(code * (1.0 / CODE_SPAN)) * CODE_SPAN


def pack_keys(place, code, key_vectors, value_vectors):
    lines = key_vectors.shape[1] + META_ROWS
    one = jax.ShapeDtypeStruct((lines, 2 * HEAD_SIZE), jnp.bfloat16)
    two = jax.ShapeDtypeStruct((2, lines, 2 * HEAD_SIZE), jnp.bfloat16)
    return pl.pallas_call(
        pack_keys_kernel,
        out_shape=(one, two, one),
        in_specs=[SMEM, VMEM, ANY, ANY],
        out_specs=(VMEM,) * 3,
        scratch_shapes=[pltpu.SemaphoreType.DMA((8,))],
        compiler_params=pltpu.CompilerParams(vmem_limit_bytes=32 * 1024 * 1024),
    )(place, code, key_vectors, value_vectors)


def pack_rows(place, queries, output_gradient):
    row_count, wide = queries.shape[1:]
    return pl.pallas_call(
        pack_rows_kernel,
        out_shape=(jax.ShapeDtypeStruct((2 * row_count, wide), jnp.bfloat16),) * 4,
        in_specs=[SMEM, ANY, ANY],
        out_specs=(VMEM,) * 4,
        scratch_shapes=[pltpu.SemaphoreType.DMA((8,))],
        compiler_params=pltpu.CompilerParams(vmem_limit_bytes=32 * 1024 * 1024),
    )(place, queries, output_gradient)


def own_keys(mine, paired, crossed):
    rows = 4 * (mine.shape[0] - META_ROWS)
    row = jax.ShapeDtypeStruct((1, rows), jnp.float32)
    own = jax.ShapeDtypeStruct((4,) + mine.shape, jnp.bfloat16)
    return pl.pallas_call(
        own_kernel,
        out_shape=(own, row, row),
        in_specs=[VMEM] * 3,
        out_specs=(VMEM,) * 3,
        compiler_params=pltpu.CompilerParams(vmem_limit_bytes=32 * 1024 * 1024),
    )(mine, paired, crossed)


PLANE = ("xh", "zp")
FINAL = ("xh", "zp", "y", "xl")
RING = 4


def swapped(array, axes, by, count):
    return lax.ppermute(array, axes, [(i, i ^ by) for i in range(count)])


def other_core(array):
    return swapped(array, "core", 1, 2)


def turned(array, by):
    return lax.ppermute(array, "zq", [(i, (i + by) % RING) for i in range(RING)])


def plus(*arrays):
    return sum(a.astype(jnp.float32) for a in arrays).astype(jnp.bfloat16)


def on_device(queries, key_vectors, value_vectors, output_gradient, positions, segments):
    window_count, row_count, _ = queries.shape
    across, pair = lax.axis_index("xh"), lax.axis_index("zp")
    place = across * 2 + pair

    spot = place.reshape(1).astype(jnp.int32)
    code = jnp.pad(segments * CODE_SPAN + positions, ((0, 0), (0, 128 - row_count)))
    tied = lax.optimization_barrier
    mine, to_pair, across_part = pack_keys(spot, code, key_vectors, value_vectors)
    paired = swapped(to_pair, PLANE, 1, 4)
    spot, to_pair = tied((spot, to_pair))
    loads = pack_rows(spot, queries, output_gradient)
    row_arrays = [loads[0]] + [swapped(loads[r], PLANE, r, 4) for r in (1, 2, 3)]
    crossed = swapped(jnp.stack([across_part, paired[1]]), PLANE, 2, 4)
    own, low, high = own_keys(mine, paired, crossed)

    before = turned(own, 1)
    after = turned(own, -1)
    far_own = other_core(own)
    opposite = turned(before, 1)
    far_after, far_before = other_core(after), other_core(before)
    state = stats(low, high, row_arrays, [own, far_own, after, far_after, before, far_before])
    state, opposite = tied((state, opposite))
    far_opposite = other_core(opposite)

    dq, near_2, far_2, state = grads(spot, low, high, state, row_arrays, [opposite, far_opposite], None, False)
    sum_2 = plus(near_2, other_core(far_2))
    spot, dq, sum_2 = tied((spot, dq, sum_2))
    passed = turned(sum_2, 1)
    dq, near_1, far_1 = grads(spot, low, high, state, row_arrays, [after, before, far_after, far_before], dq, False)
    dq, near_1, far_1, passed = tied((dq, near_1, far_1, passed))
    beside = other_core(far_1)
    next_up = plus(near_1[0:4], beside[0:4], passed)
    next_down = plus(near_1[4:8], beside[4:8])
    spot, dq, next_up, next_down = tied((spot, dq, next_up, next_down))
    to_up, to_down = turned(next_up, 1), turned(next_down, -1)
    dq, near_0, far_0 = grads(spot, low, high, state, row_arrays, [own, far_own], dq, True)
    dq, near_0, far_0, to_up, to_down = tied((dq, near_0, far_0, to_up, to_down))
    dkv_own = plus(near_0, other_core(far_0), to_up, to_down)

    flip = dkv_own.reshape((2, 2) + dkv_own.shape[1:])
    flip = jnp.where(across == 1, flip[::-1], flip)
    flip = jnp.where(pair == 1, flip[:, ::-1], flip)

    heads = KEY_VALUE_HEADS
    out_rows = row_count // heads
    split = GROUP * HEAD_SIZE
    leaving = dq.at[:, :, split:].set(flip.reshape(dkv_own.shape)).reshape(window_count * heads, out_rows, split + 2 * HEAD_SIZE)
    final = lax.all_to_all(leaving, FINAL, 0, 0, tiled=True)

    def merged(array):
        width = array.shape[-1]
        return array.reshape(window_count, heads, out_rows, width).transpose(0, 2, 1, 3).reshape(window_count, out_rows, heads * width)

    return (
        merged(final[..., 0:split]),
        merged(final[..., split:split + HEAD_SIZE]),
        merged(final[..., split + HEAD_SIZE:]),
    )


def solution(mesh):
    fine = Mesh(mesh.devices.reshape(2, RING, 2, 2, 4, 2), ("xh", "zq", "zp", "core", "y", "xl"))
    ctx, head = ("xh", "zq", "zp", "core"), ("y", "xl")
    vectors = P(None, ctx, head)
    out = P(None, ctx + head, None)
    return jax.shard_map(
        on_device,
        mesh=fine,
        in_specs=(vectors, vectors, vectors, vectors, P(None, ctx), P(None, ctx)),
        out_specs=(out, out, out),
        check_vma=False,
    )
```

```python
import functools
import math

import jax
import jax.numpy as jnp
from jax import lax
from jax.experimental import pallas as pl
from jax.experimental.pallas import tpu as pltpu
from jax.sharding import Mesh, PartitionSpec as P

QUERY_HEADS = 64
KEY_VALUE_HEADS = 8
HEAD_SIZE = 128
GROUP = QUERY_HEADS // KEY_VALUE_HEADS
NEG_BIG = -1e30
CODE_SPAN = 2048
META_ROWS = 16
HEADS_PER_STEP = 4
SCALE = 1.0 / math.sqrt(HEAD_SIZE)
EXP2_SCALE = SCALE * math.log2(math.e)

NT = (((1,), (1,)), ((), ()))
NN = (((1,), (0,)), ((), ()))


def dot(a, b, dims):
    return lax.dot_general(a, b, dims, preferred_element_type=jnp.float32)


def key_spans(piece_refs, row_count):
    spans, start = [], 0
    for ref in piece_refs:
        size = ref.shape[0] * row_count
        spans.append((ref, slice(start, start + size), size))
        start += size
    return spans, start


def keys_of(ref, size, row_count):
    return ref[:, 0:row_count, 0:HEAD_SIZE].reshape(size, HEAD_SIZE)


def values_of(ref, size, row_count):
    return ref[:, 0:row_count, HEAD_SIZE:2 * HEAD_SIZE].reshape(size, HEAD_SIZE)


def fill_bias(bias_ref, spans, low_ref, high_ref, row_count):
    rows = low_ref.shape[1]
    for ref, part, size in spans:
        for b in range(ref.shape[0]):
            digits = ref[b, row_count:row_count + META_ROWS, :].astype(jnp.float32)[0:1, :]
            code = digits[:, 0:128] * 128.0 + digits[:, 128:256]
            column = jnp.broadcast_to(code, (128, 128)).T[0:row_count, :]
            begin = part.start + b * row_count
            for r in range(rows // 128):
                low = low_ref[:, r * 128:(r + 1) * 128]
                high = high_ref[:, r * 128:(r + 1) * 128]
                allowed = (column >= low) & (column <= high)
                bias_ref[begin:begin + row_count, r * 128:(r + 1) * 128] = jnp.where(allowed, 0.0, NEG_BIG)


def rows_of(row_refs, lanes, row_count):
    q = jnp.concatenate([ref[0:row_count, lanes] for ref in row_refs], axis=0)
    do = jnp.concatenate([ref[row_count:2 * row_count, lanes] for ref in row_refs], axis=0)
    return q, do


def absorbed(top, total, cross, scores, softmax_grads):
    rows = top.shape[1]
    new = top
    for s in scores:
        peak = jnp.max(s.reshape(s.shape[0] // 8, 8, rows), axis=0)
        new = jnp.maximum(new, jnp.max(peak, axis=0, keepdims=True))
    factor = jnp.exp2(top - new)
    total, cross = total * factor, cross * factor
    weights = [jnp.exp2(s - new) for s in scores]
    for p, dp in zip(weights, softmax_grads):
        part_sum = jnp.sum(p.reshape(p.shape[0] // 8, 8, rows), axis=0)
        part_dot = jnp.sum((p * dp).reshape(p.shape[0] // 8, 8, rows), axis=0)
        total = total + jnp.sum(part_sum, axis=0, keepdims=True)
        cross = cross + jnp.sum(part_dot, axis=0, keepdims=True)
    return new, total, cross, weights


def stats_kernel(count, low_ref, high_ref, *refs):
    row_refs, piece_refs, (state_ref, bias_ref) = refs[0:4], refs[4:4 + count], refs[4 + count:]
    rows = low_ref.shape[1]
    row_count = rows // 4
    spans, _ = key_spans(piece_refs, row_count)
    fill_bias(bias_ref, spans, low_ref, high_ref, row_count)

    def step(g, carry):
        for j in range(HEADS_PER_STEP):
            h = g * HEADS_PER_STEP + j
            lanes = pl.ds(pl.multiple_of(h * HEAD_SIZE, HEAD_SIZE), HEAD_SIZE)
            q, do = rows_of(row_refs, lanes, row_count)
            top = jnp.full((1, rows), NEG_BIG, jnp.float32)
            total = jnp.zeros((1, rows), jnp.float32)
            cross = jnp.zeros((1, rows), jnp.float32)
            for ref, part, size in spans:
                s = dot(keys_of(ref, size, row_count), q, NT) * EXP2_SCALE + bias_ref[part, :]
                dp = dot(values_of(ref, size, row_count), do, NT)
                top, total, cross = absorbed(top, total, cross, [s], [dp])[0:3]
            state_ref[h, 0:1, :] = top
            state_ref[h, 1:2, :] = total
            state_ref[h, 2:3, :] = cross
        return carry

    lax.fori_loop(0, GROUP // HEADS_PER_STEP, step, 0)


def grads_kernel(first, last, count, place_ref, low_ref, high_ref, state_ref, *refs):
    row_refs, piece_refs, rest = refs[0:4], refs[4:4 + count], refs[4 + count:]
    if first:
        dq_ref, near_ref, far_ref, final_ref, bias_ref, kt_ref, ds_ref, acc_ref = rest
    else:
        before_ref, dq_ref, near_ref, far_ref, bias_ref, kt_ref, ds_ref, acc_ref = rest
    rows = low_ref.shape[1]
    row_count = rows // 4
    heads = HEADS_PER_STEP
    spans, keys = key_spans(piece_refs, row_count)
    fill_bias(bias_ref, spans, low_ref, high_ref, row_count)
    for ref, part, size in spans:
        kt_ref[:, part] = keys_of(ref, size, row_count).T
    acc_ref[...] = jnp.zeros_like(acc_ref)
    place = place_ref[0]

    def step(g, carry):
        q, do, lanes, p_low, ds_low = [], [], [], [], []
        for j in range(heads):
            h = g * heads + j
            lanes.append(pl.ds(pl.multiple_of(h * HEAD_SIZE, HEAD_SIZE), HEAD_SIZE))
            one_q, one_do = rows_of(row_refs, lanes[j], row_count)
            q.append(one_q)
            do.append(one_do)

            def products(ref, part, size):
                s = dot(keys_of(ref, size, row_count), one_q, NT) * EXP2_SCALE + bias_ref[part, :]
                return s, dot(values_of(ref, size, row_count), one_do, NT)

            if first:
                pairs = [products(*span) for span in spans]
                top, total, cross, weights = absorbed(
                    state_ref[h, 0:1, :], state_ref[h, 1:2, :], state_ref[h, 2:3, :],
                    [s for s, _ in pairs], [dp for _, dp in pairs])
                inverse = 1.0 / total
                delta = cross * inverse
                final_ref[h, 0:1, :] = top + jnp.log2(total)
                final_ref[h, 1:2, :] = delta
                softmax = [p * inverse for p in weights]
                softmax_grads = [dp for _, dp in pairs]
            else:
                offset, delta = state_ref[h, 0:1, :], state_ref[h, 1:2, :]
                softmax, softmax_grads = [], []
                for span in spans:
                    s, dp = products(*span)
                    softmax.append(jnp.exp2(s - offset))
                    softmax_grads.append(dp)
            p_low.append([p.astype(jnp.bfloat16) for p in softmax])
            ds_low.append([(p * (dp - delta)).astype(jnp.bfloat16) for p, dp in zip(softmax, softmax_grads)])
        q_all, do_all = jnp.concatenate(q, axis=0), jnp.concatenate(do, axis=0)
        for i, (ref, part, size) in enumerate(spans):
            p_all = jnp.concatenate([p_low[j][i] for j in range(heads)], axis=1)
            ds_all = jnp.concatenate([ds_low[j][i] for j in range(heads)], axis=1)
            ds_ref[part, :] = ds_all
            acc_ref[part, HEAD_SIZE:2 * HEAD_SIZE] += dot(p_all, do_all, NN)
            acc_ref[part, 0:HEAD_SIZE] += dot(ds_all, q_all, NN)
        dqt = dot(kt_ref[...], ds_ref[...], NN)
        for j in range(heads):
            part = dqt[:, j * rows:(j + 1) * rows]
            if not first:
                part = part + before_ref[g * heads + j]
            if last:
                dq = (part * SCALE).T.astype(jnp.bfloat16)
                for r in range(4):
                    dq_ref[place ^ r, :, lanes[j]] = dq[r * row_count:(r + 1) * row_count, :]
            else:
                dq_ref[g * heads + j] = part
        return carry

    lax.fori_loop(0, GROUP // heads, step, 0)
    sources = near_ref.shape[0]
    for i, out_ref in enumerate((near_ref, far_ref)):
        part = slice(i * sources * row_count, (i + 1) * sources * row_count)
        shape = (sources, row_count, HEAD_SIZE)
        out_ref[:, :, 0:HEAD_SIZE] = (acc_ref[part, 0:HEAD_SIZE] * SCALE).astype(jnp.bfloat16).reshape(shape)
        out_ref[:, :, HEAD_SIZE:2 * HEAD_SIZE] = acc_ref[part, HEAD_SIZE:2 * HEAD_SIZE].astype(jnp.bfloat16).reshape(shape)


VMEM = pl.BlockSpec(memory_space=pltpu.VMEM)
SMEM = pl.BlockSpec(memory_space=pltpu.SMEM)
ANY = pl.BlockSpec(memory_space=pltpu.HBM)


def stats(low, high, row_arrays, pieces):
    rows = low.shape[1]
    keys = sum(piece.shape[0] for piece in pieces) * rows // 4
    inputs = (low, high, *row_arrays, *pieces)
    return pl.pallas_call(
        functools.partial(stats_kernel, len(pieces)),
        out_shape=jax.ShapeDtypeStruct((GROUP, 8, rows), jnp.float32),
        in_specs=[VMEM] * len(inputs),
        out_specs=VMEM,
        scratch_shapes=[pltpu.VMEM((keys, rows), jnp.float32)],
        compiler_params=pltpu.CompilerParams(vmem_limit_bytes=32 * 1024 * 1024),
        cost_estimate=pl.CostEstimate(
            flops=8 * keys * rows * HEAD_SIZE * GROUP, bytes_accessed=1024 * 1024,
            transcendentals=keys * rows * GROUP),
    )(*inputs)


def grads(place, low, high, state, row_arrays, pieces, before, last):
    rows = low.shape[1]
    row_count = rows // 4
    sources = sum(piece.shape[0] for piece in pieces)
    keys = sources * row_count
    width = 2 * HEAD_SIZE
    first = before is None
    inputs = (low, high, state, *row_arrays, *pieces) + (() if first else (before,))
    part = jax.ShapeDtypeStruct((sources // 2, row_count, width), jnp.bfloat16)
    extra = (jax.ShapeDtypeStruct((GROUP, 8, rows), jnp.float32),) if first else ()
    if last:
        dq = jax.ShapeDtypeStruct((4, row_count, GROUP * HEAD_SIZE), jnp.bfloat16)
    else:
        dq = jax.ShapeDtypeStruct((GROUP, HEAD_SIZE, rows), jnp.float32)
    return pl.pallas_call(
        functools.partial(grads_kernel, first, last, len(pieces)),
        out_shape=(dq, part, part) + extra,
        in_specs=[SMEM] + [VMEM] * len(inputs),
        out_specs=(VMEM,) * (3 + len(extra)),
        scratch_shapes=[
            pltpu.VMEM((keys, rows), jnp.float32),
            pltpu.VMEM((HEAD_SIZE, keys), jnp.bfloat16),
            pltpu.VMEM((keys, HEADS_PER_STEP * rows), jnp.bfloat16),
            pltpu.VMEM((keys, width), jnp.float32),
        ],
        compiler_params=pltpu.CompilerParams(vmem_limit_bytes=32 * 1024 * 1024),
        cost_estimate=pl.CostEstimate(
            flops=16 * keys * rows * HEAD_SIZE * GROUP, bytes_accessed=2 * 1024 * 1024,
            transcendentals=keys * rows * GROUP),
    )(place, *inputs)


def copies(pairs, sems):
    started = [pltpu.make_async_copy(source, target, sems.at[i]) for i, (source, target) in enumerate(pairs)]
    for copy in started:
        copy.start()
    for copy in started:
        copy.wait()


def pack_keys_kernel(place_ref, code_ref, k_ref, v_ref, self_ref, pair_ref, across_ref, sems):
    row_count = k_ref.shape[1]
    place = place_ref[0]
    targets = ((0, self_ref), (1, pair_ref.at[0]), (3, pair_ref.at[1]), (2, across_ref))
    pairs = []
    for r, target in targets:
        pairs.append((k_ref.at[place ^ r], target.at[0:row_count, 0:HEAD_SIZE]))
        pairs.append((v_ref.at[place ^ r], target.at[0:row_count, HEAD_SIZE:2 * HEAD_SIZE]))
    for r, target in targets:
        code = code_ref[pl.ds(place ^ r, 1), :]
        for i, digit in enumerate((code >> 7, code & 127)):
            spread = jnp.broadcast_to(digit.astype(jnp.float32), (META_ROWS, 128)).astype(jnp.bfloat16)
            target[row_count:row_count + META_ROWS, i * 128:(i + 1) * 128] = spread
    copies(pairs, sems)


def pack_rows_kernel(place_ref, q_ref, do_ref, *refs):
    out_refs, sems = refs[0:4], refs[4]
    row_count = q_ref.shape[1]
    place = place_ref[0]
    pairs = []
    for r, target in enumerate(out_refs):
        pairs.append((q_ref.at[place ^ r], target.at[0:row_count]))
        pairs.append((do_ref.at[place ^ r], target.at[row_count:2 * row_count]))
    copies(pairs, sems)


def own_kernel(self_ref, pair_ref, across_ref, own_ref, low_ref, high_ref):
    row_count = self_ref.shape[0] - META_ROWS
    codes = []
    for r, value in enumerate((self_ref[...], pair_ref[0], across_ref[0], across_ref[1])):
        own_ref[r] = value
        digits = value[row_count:, :].astype(jnp.float32)[0:8, :]
        codes.append(digits[:, 0:128] * 128.0 + digits[:, 128:256])
    lane = lax.broadcasted_iota(jnp.int32, (8, 128), 1)
    for i in range(2):
        code = jnp.where(lane < row_count, codes[2 * i], pltpu.roll(codes[2 * i + 1], row_count, 1))[0:1, :]
        high_ref[:, i * 128:(i + 1) * 128] = code
        low_ref[:, i * 128:(i + 1) * 128] = jnp.floor(code * (1.0 / CODE_SPAN)) * CODE_SPAN


def pack_keys(place, code, key_vectors, value_vectors):
    lines = key_vectors.shape[1] + META_ROWS
    one = jax.ShapeDtypeStruct((lines, 2 * HEAD_SIZE), jnp.bfloat16)
    two = jax.ShapeDtypeStruct((2, lines, 2 * HEAD_SIZE), jnp.bfloat16)
    return pl.pallas_call(
        pack_keys_kernel,
        out_shape=(one, two, one),
        in_specs=[SMEM, VMEM, ANY, ANY],
        out_specs=(VMEM,) * 3,
        scratch_shapes=[pltpu.SemaphoreType.DMA((8,))],
        compiler_params=pltpu.CompilerParams(vmem_limit_bytes=32 * 1024 * 1024),
    )(place, code, key_vectors, value_vectors)


def pack_rows(place, queries, output_gradient):
    row_count, wide = queries.shape[1:]
    return pl.pallas_call(
        pack_rows_kernel,
        out_shape=(jax.ShapeDtypeStruct((2 * row_count, wide), jnp.bfloat16),) * 4,
        in_specs=[SMEM, ANY, ANY],
        out_specs=(VMEM,) * 4,
        scratch_shapes=[pltpu.SemaphoreType.DMA((8,))],
        compiler_params=pltpu.CompilerParams(vmem_limit_bytes=32 * 1024 * 1024),
    )(place, queries, output_gradient)


def own_keys(mine, paired, crossed):
    rows = 4 * (mine.shape[0] - META_ROWS)
    row = jax.ShapeDtypeStruct((1, rows), jnp.float32)
    own = jax.ShapeDtypeStruct((4,) + mine.shape, jnp.bfloat16)
    return pl.pallas_call(
        own_kernel,
        out_shape=(own, row, row),
        in_specs=[VMEM] * 3,
        out_specs=(VMEM,) * 3,
        compiler_params=pltpu.CompilerParams(vmem_limit_bytes=32 * 1024 * 1024),
    )(mine, paired, crossed)


PLANE = ("xh", "zp")
FINAL = ("xh", "zp", "y", "xl")
RING = 4


def swapped(array, axes, by, count):
    return lax.ppermute(array, axes, [(i, i ^ by) for i in range(count)])


def other_core(array):
    return swapped(array, "core", 1, 2)


def turned(array, by):
    return lax.ppermute(array, "zq", [(i, (i + by) % RING) for i in range(RING)])


def plus(*arrays):
    return sum(a.astype(jnp.float32) for a in arrays).astype(jnp.bfloat16)


def on_device(queries, key_vectors, value_vectors, output_gradient, positions, segments):
    window_count, row_count, _ = queries.shape
    across, pair = lax.axis_index("xh"), lax.axis_index("zp")
    place = across * 2 + pair

    spot = place.reshape(1).astype(jnp.int32)
    code = jnp.pad(segments * CODE_SPAN + positions, ((0, 0), (0, 128 - row_count)))
    tied = lax.optimization_barrier
    mine, to_pair, across_part = pack_keys(spot, code, key_vectors, value_vectors)
    paired = swapped(to_pair, PLANE, 1, 4)
    spot, to_pair = tied((spot, to_pair))
    loads = pack_rows(spot, queries, output_gradient)
    row_arrays = [loads[0]] + [swapped(loads[r], PLANE, r, 4) for r in (1, 2, 3)]
    crossed = swapped(jnp.stack([across_part, paired[1]]), PLANE, 2, 4)
    own, low, high = own_keys(mine, paired, crossed)

    before = turned(own, 1)
    after = turned(own, -1)
    far_own = other_core(own)
    before, row_arrays = tied((before, row_arrays))
    opposite = turned(before, 1)
    far_after, far_before = other_core(after), other_core(before)
    state = stats(low, high, row_arrays, [own, far_own, after, far_after, before, far_before])
    state, opposite = tied((state, opposite))
    far_opposite = other_core(opposite)

    dq, near_2, far_2, state = grads(spot, low, high, state, row_arrays, [opposite, far_opposite], None, False)
    sum_2 = plus(near_2, other_core(far_2))
    spot, dq, sum_2 = tied((spot, dq, sum_2))
    passed = turned(sum_2, 1)
    dq, near_1, far_1 = grads(spot, low, high, state, row_arrays, [after, before, far_after, far_before], dq, False)
    dq, near_1, far_1, passed = tied((dq, near_1, far_1, passed))
    beside = other_core(far_1)
    dq, near_0, far_0 = grads(spot, low, high, state, row_arrays, [own, far_own], dq, True)
    dq, near_0, far_0, beside = tied((dq, near_0, far_0, beside))

    heads = KEY_VALUE_HEADS
    out_rows = row_count // heads

    def delivered(array):
        return lax.all_to_all(array.reshape(window_count * heads, out_rows, array.shape[-1]), FINAL, 0, 0, tiled=True)

    dq_final = delivered(dq)
    next_up = plus(near_1[0:4], beside[0:4], passed)
    next_down = plus(near_1[4:8], beside[4:8])
    to_up, to_down = turned(next_up, 1), turned(next_down, -1)
    dkv_own = plus(near_0, other_core(far_0), to_up, to_down)
    flip = dkv_own.reshape((2, 2) + dkv_own.shape[1:])
    flip = jnp.where(across == 1, flip[::-1], flip)
    flip = jnp.where(pair == 1, flip[:, ::-1], flip)
    flip, dq_final = tied((flip, dq_final))
    dkv_final = delivered(flip.reshape(dkv_own.shape))

    def merged(array):
        width = array.shape[-1]
        return array.reshape(window_count, heads, out_rows, width).transpose(0, 2, 1, 3).reshape(window_count, out_rows, heads * width)

    return (
        merged(dq_final),
        merged(dkv_final[..., 0:HEAD_SIZE]),
        merged(dkv_final[..., HEAD_SIZE:]),
    )


def solution(mesh):
    fine = Mesh(mesh.devices.reshape(2, RING, 2, 2, 4, 2), ("xh", "zq", "zp", "core", "y", "xl"))
    ctx, head = ("xh", "zq", "zp", "core"), ("y", "xl")
    vectors = P(None, ctx, head)
    out = P(None, ctx + head, None)
    return jax.shard_map(
        on_device,
        mesh=fine,
        in_specs=(vectors, vectors, vectors, vectors, P(None, ctx), P(None, ctx)),
        out_specs=(out, out, out),
        check_vma=False,
    )
```

```python
import functools
import math

import jax
import jax.numpy as jnp
from jax import lax
from jax.experimental import pallas as pl
from jax.experimental.pallas import tpu as pltpu
from jax.sharding import Mesh, PartitionSpec as P

QUERY_HEADS = 64
KEY_VALUE_HEADS = 8
HEAD_SIZE = 128
GROUP = QUERY_HEADS // KEY_VALUE_HEADS
NEG_BIG = -1e30
CODE_SPAN = 2048
META_ROWS = 16
HEADS_PER_STEP = 4
SCALE = 1.0 / math.sqrt(HEAD_SIZE)
EXP2_SCALE = SCALE * math.log2(math.e)

NT = (((1,), (1,)), ((), ()))
NN = (((1,), (0,)), ((), ()))


def dot(a, b, dims):
    return lax.dot_general(a, b, dims, preferred_element_type=jnp.float32)


def key_spans(piece_refs, row_count):
    spans, start = [], 0
    for ref in piece_refs:
        size = ref.shape[0] * row_count
        spans.append((ref, slice(start, start + size), size))
        start += size
    return spans, start


def keys_of(ref, size, row_count):
    return ref[:, 0:row_count, 0:HEAD_SIZE].reshape(size, HEAD_SIZE)


def values_of(ref, size, row_count):
    return ref[:, 0:row_count, HEAD_SIZE:2 * HEAD_SIZE].reshape(size, HEAD_SIZE)


def fill_bias(bias_ref, spans, low_ref, high_ref, row_count):
    rows = low_ref.shape[1]
    for ref, part, size in spans:
        for b in range(ref.shape[0]):
            digits = ref[b, row_count:row_count + META_ROWS, :].astype(jnp.float32)[0:1, :]
            code = digits[:, 0:128] * 128.0 + digits[:, 128:256]
            column = jnp.broadcast_to(code, (128, 128)).T[0:row_count, :]
            begin = part.start + b * row_count
            for r in range(rows // 128):
                low = low_ref[:, r * 128:(r + 1) * 128]
                high = high_ref[:, r * 128:(r + 1) * 128]
                allowed = (column >= low) & (column <= high)
                bias_ref[begin:begin + row_count, r * 128:(r + 1) * 128] = jnp.where(allowed, 0.0, NEG_BIG)


def rows_of(row_refs, lanes, row_count):
    q = jnp.concatenate([ref[0:row_count, lanes] for ref in row_refs], axis=0)
    do = jnp.concatenate([ref[row_count:2 * row_count, lanes] for ref in row_refs], axis=0)
    return q, do


def absorbed(top, total, cross, scores, softmax_grads):
    rows = top.shape[1]
    new = top
    for s in scores:
        peak = jnp.max(s.reshape(s.shape[0] // 8, 8, rows), axis=0)
        new = jnp.maximum(new, jnp.max(peak, axis=0, keepdims=True))
    factor = jnp.exp2(top - new)
    total, cross = total * factor, cross * factor
    weights = [jnp.exp2(s - new) for s in scores]
    for p, dp in zip(weights, softmax_grads):
        part_sum = jnp.sum(p.reshape(p.shape[0] // 8, 8, rows), axis=0)
        part_dot = jnp.sum((p * dp).reshape(p.shape[0] // 8, 8, rows), axis=0)
        total = total + jnp.sum(part_sum, axis=0, keepdims=True)
        cross = cross + jnp.sum(part_dot, axis=0, keepdims=True)
    return new, total, cross, weights


def stats_kernel(count, low_ref, high_ref, *refs):
    row_refs, piece_refs, (state_ref, bias_ref) = refs[0:4], refs[4:4 + count], refs[4 + count:]
    rows = low_ref.shape[1]
    row_count = rows // 4
    spans, _ = key_spans(piece_refs, row_count)
    fill_bias(bias_ref, spans, low_ref, high_ref, row_count)

    def step(g, carry):
        for j in range(HEADS_PER_STEP):
            h = g * HEADS_PER_STEP + j
            lanes = pl.ds(pl.multiple_of(h * HEAD_SIZE, HEAD_SIZE), HEAD_SIZE)
            q, do = rows_of(row_refs, lanes, row_count)
            top = jnp.full((1, rows), NEG_BIG, jnp.float32)
            total = jnp.zeros((1, rows), jnp.float32)
            cross = jnp.zeros((1, rows), jnp.float32)
            for ref, part, size in spans:
                s = dot(keys_of(ref, size, row_count), q, NT) * EXP2_SCALE + bias_ref[part, :]
                dp = dot(values_of(ref, size, row_count), do, NT)
                top, total, cross = absorbed(top, total, cross, [s], [dp])[0:3]
            state_ref[h, 0:1, :] = top
            state_ref[h, 1:2, :] = total
            state_ref[h, 2:3, :] = cross
        return carry

    lax.fori_loop(0, GROUP // HEADS_PER_STEP, step, 0)


def grads_kernel(first, last, count, place_ref, low_ref, high_ref, state_ref, *refs):
    row_refs, piece_refs, rest = refs[0:4], refs[4:4 + count], refs[4 + count:]
    if first:
        dq_ref, near_ref, far_ref, final_ref, bias_ref, kt_ref, ds_ref, acc_ref = rest
    else:
        before_ref, dq_ref, near_ref, far_ref, bias_ref, kt_ref, ds_ref, acc_ref = rest
    rows = low_ref.shape[1]
    row_count = rows // 4
    heads = HEADS_PER_STEP
    spans, keys = key_spans(piece_refs, row_count)
    fill_bias(bias_ref, spans, low_ref, high_ref, row_count)
    for ref, part, size in spans:
        kt_ref[:, part] = keys_of(ref, size, row_count).T
    acc_ref[...] = jnp.zeros_like(acc_ref)
    place = place_ref[0]

    def step(g, carry):
        q, do, lanes, p_low, ds_low = [], [], [], [], []
        for j in range(heads):
            h = g * heads + j
            lanes.append(pl.ds(pl.multiple_of(h * HEAD_SIZE, HEAD_SIZE), HEAD_SIZE))
            one_q, one_do = rows_of(row_refs, lanes[j], row_count)
            q.append(one_q)
            do.append(one_do)

            def products(ref, part, size):
                s = dot(keys_of(ref, size, row_count), one_q, NT) * EXP2_SCALE + bias_ref[part, :]
                return s, dot(values_of(ref, size, row_count), one_do, NT)

            if first:
                pairs = [products(*span) for span in spans]
                top, total, cross, weights = absorbed(
                    state_ref[h, 0:1, :], state_ref[h, 1:2, :], state_ref[h, 2:3, :],
                    [s for s, _ in pairs], [dp for _, dp in pairs])
                inverse = 1.0 / total
                delta = cross * inverse
                final_ref[h, 0:1, :] = top + jnp.log2(total)
                final_ref[h, 1:2, :] = delta
                softmax = [p * inverse for p in weights]
                softmax_grads = [dp for _, dp in pairs]
            else:
                offset, delta = state_ref[h, 0:1, :], state_ref[h, 1:2, :]
                softmax, softmax_grads = [], []
                for span in spans:
                    s, dp = products(*span)
                    softmax.append(jnp.exp2(s - offset))
                    softmax_grads.append(dp)
            p_low.append([p.astype(jnp.bfloat16) for p in softmax])
            ds_low.append([(p * (dp - delta)).astype(jnp.bfloat16) for p, dp in zip(softmax, softmax_grads)])
        q_all, do_all = jnp.concatenate(q, axis=0), jnp.concatenate(do, axis=0)
        for i, (ref, part, size) in enumerate(spans):
            p_all = jnp.concatenate([p_low[j][i] for j in range(heads)], axis=1)
            ds_all = jnp.concatenate([ds_low[j][i] for j in range(heads)], axis=1)
            ds_ref[part, :] = ds_all
            acc_ref[part, HEAD_SIZE:2 * HEAD_SIZE] += dot(p_all, do_all, NN)
            acc_ref[part, 0:HEAD_SIZE] += dot(ds_all, q_all, NN)
        dqt = dot(kt_ref[...], ds_ref[...], NN)
        for j in range(heads):
            part = dqt[:, j * rows:(j + 1) * rows]
            if not first:
                part = part + before_ref[g * heads + j]
            if last:
                dq = (part * SCALE).T.astype(jnp.bfloat16)
                for r in range(4):
                    dq_ref[place ^ r, :, lanes[j]] = dq[r * row_count:(r + 1) * row_count, :]
            else:
                dq_ref[g * heads + j] = part
        return carry

    lax.fori_loop(0, GROUP // heads, step, 0)
    sources = near_ref.shape[0]
    for i, out_ref in enumerate((near_ref, far_ref)):
        part = slice(i * sources * row_count, (i + 1) * sources * row_count)
        shape = (sources, row_count, HEAD_SIZE)
        out_ref[:, :, 0:HEAD_SIZE] = (acc_ref[part, 0:HEAD_SIZE] * SCALE).astype(jnp.bfloat16).reshape(shape)
        out_ref[:, :, HEAD_SIZE:2 * HEAD_SIZE] = acc_ref[part, HEAD_SIZE:2 * HEAD_SIZE].astype(jnp.bfloat16).reshape(shape)


VMEM = pl.BlockSpec(memory_space=pltpu.VMEM)
SMEM = pl.BlockSpec(memory_space=pltpu.SMEM)
ANY = pl.BlockSpec(memory_space=pltpu.HBM)


def stats(low, high, row_arrays, pieces):
    rows = low.shape[1]
    keys = sum(piece.shape[0] for piece in pieces) * rows // 4
    inputs = (low, high, *row_arrays, *pieces)
    return pl.pallas_call(
        functools.partial(stats_kernel, len(pieces)),
        out_shape=jax.ShapeDtypeStruct((GROUP, 8, rows), jnp.float32),
        in_specs=[VMEM] * len(inputs),
        out_specs=VMEM,
        scratch_shapes=[pltpu.VMEM((keys, rows), jnp.float32)],
        compiler_params=pltpu.CompilerParams(vmem_limit_bytes=32 * 1024 * 1024),
        cost_estimate=pl.CostEstimate(
            flops=8 * keys * rows * HEAD_SIZE * GROUP, bytes_accessed=1024 * 1024,
            transcendentals=keys * rows * GROUP),
    )(*inputs)


def grads(place, low, high, state, row_arrays, pieces, before, last):
    rows = low.shape[1]
    row_count = rows // 4
    sources = sum(piece.shape[0] for piece in pieces)
    keys = sources * row_count
    width = 2 * HEAD_SIZE
    first = before is None
    inputs = (low, high, state, *row_arrays, *pieces) + (() if first else (before,))
    part = jax.ShapeDtypeStruct((sources // 2, row_count, width), jnp.bfloat16)
    extra = (jax.ShapeDtypeStruct((GROUP, 8, rows), jnp.float32),) if first else ()
    if last:
        dq = jax.ShapeDtypeStruct((4, row_count, GROUP * HEAD_SIZE + width), jnp.bfloat16)
    else:
        dq = jax.ShapeDtypeStruct((GROUP, HEAD_SIZE, rows), jnp.float32)
    return pl.pallas_call(
        functools.partial(grads_kernel, first, last, len(pieces)),
        out_shape=(dq, part, part) + extra,
        in_specs=[SMEM] + [VMEM] * len(inputs),
        out_specs=(VMEM,) * (3 + len(extra)),
        scratch_shapes=[
            pltpu.VMEM((keys, rows), jnp.float32),
            pltpu.VMEM((HEAD_SIZE, keys), jnp.bfloat16),
            pltpu.VMEM((keys, HEADS_PER_STEP * rows), jnp.bfloat16),
            pltpu.VMEM((keys, width), jnp.float32),
        ],
        compiler_params=pltpu.CompilerParams(vmem_limit_bytes=32 * 1024 * 1024),
        cost_estimate=pl.CostEstimate(
            flops=16 * keys * rows * HEAD_SIZE * GROUP, bytes_accessed=2 * 1024 * 1024,
            transcendentals=keys * rows * GROUP),
    )(place, *inputs)


def copies(pairs, sems):
    started = [pltpu.make_async_copy(source, target, sems.at[i]) for i, (source, target) in enumerate(pairs)]
    for copy in started:
        copy.start()
    for copy in started:
        copy.wait()


def pack_keys_kernel(place_ref, code_ref, k_ref, v_ref, self_ref, pair_ref, across_ref, sems):
    row_count = k_ref.shape[1]
    place = place_ref[0]
    targets = ((0, self_ref), (1, pair_ref.at[0]), (3, pair_ref.at[1]), (2, across_ref))
    pairs = []
    for r, target in targets:
        pairs.append((k_ref.at[place ^ r], target.at[0:row_count, 0:HEAD_SIZE]))
        pairs.append((v_ref.at[place ^ r], target.at[0:row_count, HEAD_SIZE:2 * HEAD_SIZE]))
    for r, target in targets:
        code = code_ref[pl.ds(place ^ r, 1), :]
        for i, digit in enumerate((code >> 7, code & 127)):
            spread = jnp.broadcast_to(digit.astype(jnp.float32), (META_ROWS, 128)).astype(jnp.bfloat16)
            target[row_count:row_count + META_ROWS, i * 128:(i + 1) * 128] = spread
    copies(pairs, sems)


def pack_rows_kernel(place_ref, q_ref, do_ref, *refs):
    out_refs, sems = refs[0:4], refs[4]
    row_count = q_ref.shape[1]
    place = place_ref[0]
    pairs = []
    for r, target in enumerate(out_refs):
        pairs.append((q_ref.at[place ^ r], target.at[0:row_count]))
        pairs.append((do_ref.at[place ^ r], target.at[row_count:2 * row_count]))
    copies(pairs, sems)


def own_kernel(self_ref, pair_ref, across_ref, own_ref, low_ref, high_ref):
    row_count = self_ref.shape[0] - META_ROWS
    codes = []
    for r, value in enumerate((self_ref[...], pair_ref[0], across_ref[0], across_ref[1])):
        own_ref[r] = value
        digits = value[row_count:, :].astype(jnp.float32)[0:8, :]
        codes.append(digits[:, 0:128] * 128.0 + digits[:, 128:256])
    lane = lax.broadcasted_iota(jnp.int32, (8, 128), 1)
    for i in range(2):
        code = jnp.where(lane < row_count, codes[2 * i], pltpu.roll(codes[2 * i + 1], row_count, 1))[0:1, :]
        high_ref[:, i * 128:(i + 1) * 128] = code
        low_ref[:, i * 128:(i + 1) * 128] = jnp.floor(code * (1.0 / CODE_SPAN)) * CODE_SPAN


def pack_keys(place, code, key_vectors, value_vectors):
    lines = key_vectors.shape[1] + META_ROWS
    one = jax.ShapeDtypeStruct((lines, 2 * HEAD_SIZE), jnp.bfloat16)
    two = jax.ShapeDtypeStruct((2, lines, 2 * HEAD_SIZE), jnp.bfloat16)
    return pl.pallas_call(
        pack_keys_kernel,
        out_shape=(one, two, one),
        in_specs=[SMEM, VMEM, ANY, ANY],
        out_specs=(VMEM,) * 3,
        scratch_shapes=[pltpu.SemaphoreType.DMA((8,))],
        compiler_params=pltpu.CompilerParams(vmem_limit_bytes=32 * 1024 * 1024),
    )(place, code, key_vectors, value_vectors)


def pack_rows(place, queries, output_gradient):
    row_count, wide = queries.shape[1:]
    return pl.pallas_call(
        pack_rows_kernel,
        out_shape=(jax.ShapeDtypeStruct((2 * row_count, wide), jnp.bfloat16),) * 4,
        in_specs=[SMEM, ANY, ANY],
        out_specs=(VMEM,) * 4,
        scratch_shapes=[pltpu.SemaphoreType.DMA((8,))],
        compiler_params=pltpu.CompilerParams(vmem_limit_bytes=32 * 1024 * 1024),
    )(place, queries, output_gradient)


def own_keys(mine, paired, crossed):
    rows = 4 * (mine.shape[0] - META_ROWS)
    row = jax.ShapeDtypeStruct((1, rows), jnp.float32)
    own = jax.ShapeDtypeStruct((4,) + mine.shape, jnp.bfloat16)
    return pl.pallas_call(
        own_kernel,
        out_shape=(own, row, row),
        in_specs=[VMEM] * 3,
        out_specs=(VMEM,) * 3,
        compiler_params=pltpu.CompilerParams(vmem_limit_bytes=32 * 1024 * 1024),
    )(mine, paired, crossed)


PLANE = ("xh", "zp")
FINAL = ("xh", "zp", "y", "xl")
RING = 4


def swapped(array, axes, by, count):
    return lax.ppermute(array, axes, [(i, i ^ by) for i in range(count)])


def other_core(array):
    return swapped(array, "core", 1, 2)


def turned(array, by):
    return lax.ppermute(array, "zq", [(i, (i + by) % RING) for i in range(RING)])


def plus(*arrays):
    return sum(a.astype(jnp.float32) for a in arrays).astype(jnp.bfloat16)


def on_device(queries, key_vectors, value_vectors, output_gradient, positions, segments):
    window_count, row_count, _ = queries.shape
    across, pair = lax.axis_index("xh"), lax.axis_index("zp")
    place = across * 2 + pair

    spot = place.reshape(1).astype(jnp.int32)
    code = jnp.pad(segments * CODE_SPAN + positions, ((0, 0), (0, 128 - row_count)))
    tied = lax.optimization_barrier
    mine, to_pair, across_part = pack_keys(spot, code, key_vectors, value_vectors)
    paired = swapped(to_pair, PLANE, 1, 4)
    spot, to_pair = tied((spot, to_pair))
    loads = pack_rows(spot, queries, output_gradient)
    crossed = swapped(jnp.stack([across_part, paired[1]]), PLANE, 2, 4)
    crossed, far_rows = tied((crossed, loads[2:4]))
    row_arrays = [loads[0], swapped(loads[1], PLANE, 1, 4)] + [swapped(far_rows[r - 2], PLANE, r, 4) for r in (2, 3)]
    own, low, high = own_keys(mine, paired, crossed)

    before = turned(own, 1)
    after = turned(own, -1)
    far_own = other_core(own)
    before, row_arrays = tied((before, row_arrays))
    opposite = turned(before, 1)
    far_after, far_before = other_core(after), other_core(before)
    state = stats(low, high, row_arrays, [own, far_own, after, far_after, before, far_before])
    state, opposite = tied((state, opposite))
    far_opposite = other_core(opposite)

    dq, near_2, far_2, state = grads(spot, low, high, state, row_arrays, [opposite, far_opposite], None, False)
    sum_2 = plus(near_2, other_core(far_2))
    spot, dq, sum_2 = tied((spot, dq, sum_2))
    passed = turned(sum_2, 1)
    dq, near_1, far_1 = grads(spot, low, high, state, row_arrays, [after, before, far_after, far_before], dq, False)
    dq, near_1, far_1, passed = tied((dq, near_1, far_1, passed))
    beside = other_core(far_1)
    next_up = plus(near_1[0:4], beside[0:4], passed)
    next_down = plus(near_1[4:8], beside[4:8])
    spot, dq, next_up, next_down = tied((spot, dq, next_up, next_down))
    to_up, to_down = turned(next_up, 1), turned(next_down, -1)
    dq, near_0, far_0 = grads(spot, low, high, state, row_arrays, [own, far_own], dq, True)
    dq, to_up, to_down = tied((dq, to_up, to_down))
    dkv_own = plus(near_0, other_core(far_0), to_up, to_down)

    flip = dkv_own.reshape((2, 2) + dkv_own.shape[1:])
    flip = jnp.where(across == 1, flip[::-1], flip)
    flip = jnp.where(pair == 1, flip[:, ::-1], flip)

    heads = KEY_VALUE_HEADS
    out_rows = row_count // heads
    split = GROUP * HEAD_SIZE
    leaving = dq.at[:, :, split:].set(flip.reshape(dkv_own.shape)).reshape(window_count * heads, out_rows, split + 2 * HEAD_SIZE)
    final = lax.all_to_all(leaving, FINAL, 0, 0, tiled=True)

    def merged(array):
        width = array.shape[-1]
        return array.reshape(window_count, heads, out_rows, width).transpose(0, 2, 1, 3).reshape(window_count, out_rows, heads * width)

    return (
        merged(final[..., 0:split]),
        merged(final[..., split:split + HEAD_SIZE]),
        merged(final[..., split + HEAD_SIZE:]),
    )


def solution(mesh):
    fine = Mesh(mesh.devices.reshape(2, RING, 2, 2, 4, 2), ("xh", "zq", "zp", "core", "y", "xl"))
    ctx, head = ("xh", "zq", "zp", "core"), ("y", "xl")
    vectors = P(None, ctx, head)
    out = P(None, ctx + head, None)
    return jax.shard_map(
        on_device,
        mesh=fine,
        in_specs=(vectors, vectors, vectors, vectors, P(None, ctx), P(None, ctx)),
        out_specs=(out, out, out),
        check_vma=False,
    )
```

```python
import functools
import math

import jax
import jax.numpy as jnp
from jax import lax
from jax.experimental import pallas as pl
from jax.experimental.pallas import tpu as pltpu
from jax.sharding import Mesh, PartitionSpec as P

QUERY_HEADS = 64
KEY_VALUE_HEADS = 8
HEAD_SIZE = 128
GROUP = QUERY_HEADS // KEY_VALUE_HEADS
NEG_BIG = -1e30
CODE_SPAN = 2048
META_ROWS = 16
HEADS_PER_STEP = 4
SCALE = 1.0 / math.sqrt(HEAD_SIZE)
EXP2_SCALE = SCALE * math.log2(math.e)

NT = (((1,), (1,)), ((), ()))
NN = (((1,), (0,)), ((), ()))


def dot(a, b, dims):
    return lax.dot_general(a, b, dims, preferred_element_type=jnp.float32)


def key_spans(piece_refs, row_count):
    spans, start = [], 0
    for ref in piece_refs:
        size = ref.shape[0] * row_count
        spans.append((ref, slice(start, start + size), size))
        start += size
    return spans, start


def keys_of(ref, size, row_count):
    return ref[:, 0:row_count, 0:HEAD_SIZE].reshape(size, HEAD_SIZE)


def values_of(ref, size, row_count):
    return ref[:, 0:row_count, HEAD_SIZE:2 * HEAD_SIZE].reshape(size, HEAD_SIZE)


def fill_bias(bias_ref, spans, low_ref, high_ref, row_count):
    rows = low_ref.shape[1]
    for ref, part, size in spans:
        for b in range(ref.shape[0]):
            digits = ref[b, row_count:row_count + META_ROWS, :].astype(jnp.float32)[0:1, :]
            code = digits[:, 0:128] * 128.0 + digits[:, 128:256]
            column = jnp.broadcast_to(code, (128, 128)).T[0:row_count, :]
            begin = part.start + b * row_count
            for r in range(rows // 128):
                low = low_ref[:, r * 128:(r + 1) * 128]
                high = high_ref[:, r * 128:(r + 1) * 128]
                allowed = (column >= low) & (column <= high)
                bias_ref[begin:begin + row_count, r * 128:(r + 1) * 128] = jnp.where(allowed, 0.0, NEG_BIG)


def rows_of(row_refs, lanes, row_count):
    q = jnp.concatenate([ref[0:row_count, lanes] for ref in row_refs], axis=0)
    do = jnp.concatenate([ref[row_count:2 * row_count, lanes] for ref in row_refs], axis=0)
    return q, do


def absorbed(top, total, cross, scores, softmax_grads):
    rows = top.shape[1]
    new = top
    for s in scores:
        peak = jnp.max(s.reshape(s.shape[0] // 8, 8, rows), axis=0)
        new = jnp.maximum(new, jnp.max(peak, axis=0, keepdims=True))
    factor = jnp.exp2(top - new)
    total, cross = total * factor, cross * factor
    weights = [jnp.exp2(s - new) for s in scores]
    for p, dp in zip(weights, softmax_grads):
        part_sum = jnp.sum(p.reshape(p.shape[0] // 8, 8, rows), axis=0)
        part_dot = jnp.sum((p * dp).reshape(p.shape[0] // 8, 8, rows), axis=0)
        total = total + jnp.sum(part_sum, axis=0, keepdims=True)
        cross = cross + jnp.sum(part_dot, axis=0, keepdims=True)
    return new, total, cross, weights


def stats_kernel(first, count, low_ref, high_ref, *refs):
    row_refs, piece_refs, rest = refs[0:4], refs[4:4 + count], refs[4 + count:]
    state_ref, bias_ref = rest[-2:]
    rows = low_ref.shape[1]
    row_count = rows // 4
    spans, _ = key_spans(piece_refs, row_count)
    fill_bias(bias_ref, spans, low_ref, high_ref, row_count)

    def step(g, carry):
        for j in range(HEADS_PER_STEP):
            h = g * HEADS_PER_STEP + j
            lanes = pl.ds(pl.multiple_of(h * HEAD_SIZE, HEAD_SIZE), HEAD_SIZE)
            q, do = rows_of(row_refs, lanes, row_count)
            if first:
                top = jnp.full((1, rows), NEG_BIG, jnp.float32)
                total = jnp.zeros((1, rows), jnp.float32)
                cross = jnp.zeros((1, rows), jnp.float32)
            else:
                top, total, cross = rest[0][h, 0:1, :], rest[0][h, 1:2, :], rest[0][h, 2:3, :]
            for ref, part, size in spans:
                s = dot(keys_of(ref, size, row_count), q, NT) * EXP2_SCALE + bias_ref[part, :]
                dp = dot(values_of(ref, size, row_count), do, NT)
                top, total, cross = absorbed(top, total, cross, [s], [dp])[0:3]
            state_ref[h, 0:1, :] = top
            state_ref[h, 1:2, :] = total
            state_ref[h, 2:3, :] = cross
        return carry

    lax.fori_loop(0, GROUP // HEADS_PER_STEP, step, 0)


def grads_kernel(first, last, count, place_ref, low_ref, high_ref, state_ref, *refs):
    row_refs, piece_refs, rest = refs[0:4], refs[4:4 + count], refs[4 + count:]
    if not first:
        before_ref, rest = rest[0], rest[1:]
    dq_ref, out_refs, rest = rest[0], rest[1:1 + count], rest[1 + count:]
    if first:
        final_ref, rest = rest[0], rest[1:]
    bias_ref, kt_ref, ds_ref, acc_ref = rest
    rows = low_ref.shape[1]
    row_count = rows // 4
    heads = HEADS_PER_STEP
    spans, keys = key_spans(piece_refs, row_count)
    fill_bias(bias_ref, spans, low_ref, high_ref, row_count)
    for ref, part, size in spans:
        kt_ref[:, part] = keys_of(ref, size, row_count).T
    acc_ref[...] = jnp.zeros_like(acc_ref)
    place = place_ref[0]

    def step(g, carry):
        q, do, lanes, p_low, ds_low = [], [], [], [], []
        for j in range(heads):
            h = g * heads + j
            lanes.append(pl.ds(pl.multiple_of(h * HEAD_SIZE, HEAD_SIZE), HEAD_SIZE))
            one_q, one_do = rows_of(row_refs, lanes[j], row_count)
            q.append(one_q)
            do.append(one_do)

            def products(ref, part, size):
                s = dot(keys_of(ref, size, row_count), one_q, NT) * EXP2_SCALE + bias_ref[part, :]
                return s, dot(values_of(ref, size, row_count), one_do, NT)

            if first:
                pairs = [products(*span) for span in spans]
                top, total, cross, weights = absorbed(
                    state_ref[h, 0:1, :], state_ref[h, 1:2, :], state_ref[h, 2:3, :],
                    [s for s, _ in pairs], [dp for _, dp in pairs])
                inverse = 1.0 / total
                delta = cross * inverse
                final_ref[h, 0:1, :] = top + jnp.log2(total)
                final_ref[h, 1:2, :] = delta
                softmax = [p * inverse for p in weights]
                softmax_grads = [dp for _, dp in pairs]
            else:
                offset, delta = state_ref[h, 0:1, :], state_ref[h, 1:2, :]
                softmax, softmax_grads = [], []
                for span in spans:
                    s, dp = products(*span)
                    softmax.append(jnp.exp2(s - offset))
                    softmax_grads.append(dp)
            p_low.append([p.astype(jnp.bfloat16) for p in softmax])
            ds_low.append([(p * (dp - delta)).astype(jnp.bfloat16) for p, dp in zip(softmax, softmax_grads)])
        q_all, do_all = jnp.concatenate(q, axis=0), jnp.concatenate(do, axis=0)
        for i, (ref, part, size) in enumerate(spans):
            p_all = jnp.concatenate([p_low[j][i] for j in range(heads)], axis=1)
            ds_all = jnp.concatenate([ds_low[j][i] for j in range(heads)], axis=1)
            ds_ref[part, :] = ds_all
            acc_ref[part, HEAD_SIZE:2 * HEAD_SIZE] += dot(p_all, do_all, NN)
            acc_ref[part, 0:HEAD_SIZE] += dot(ds_all, q_all, NN)
        dqt = dot(kt_ref[...], ds_ref[...], NN)
        for j in range(heads):
            part = dqt[:, j * rows:(j + 1) * rows]
            if not first:
                part = part + before_ref[g * heads + j]
            if last:
                dq = (part * SCALE).T.astype(jnp.bfloat16)
                for r in range(4):
                    dq_ref[place ^ r, :, lanes[j]] = dq[r * row_count:(r + 1) * row_count, :]
            else:
                dq_ref[g * heads + j] = part
        return carry

    lax.fori_loop(0, GROUP // heads, step, 0)
    for out_ref, (_, part, size) in zip(out_refs, spans):
        shape = (size // row_count, row_count, HEAD_SIZE)
        out_ref[:, :, 0:HEAD_SIZE] = (acc_ref[part, 0:HEAD_SIZE] * SCALE).astype(jnp.bfloat16).reshape(shape)
        out_ref[:, :, HEAD_SIZE:2 * HEAD_SIZE] = acc_ref[part, HEAD_SIZE:2 * HEAD_SIZE].astype(jnp.bfloat16).reshape(shape)


VMEM = pl.BlockSpec(memory_space=pltpu.VMEM)
SMEM = pl.BlockSpec(memory_space=pltpu.SMEM)
ANY = pl.BlockSpec(memory_space=pltpu.HBM)


def stats(low, high, row_arrays, pieces, state):
    rows = low.shape[1]
    keys = sum(piece.shape[0] for piece in pieces) * rows // 4
    first = state is None
    inputs = (low, high, *row_arrays, *pieces) + (() if first else (state,))
    return pl.pallas_call(
        functools.partial(stats_kernel, first, len(pieces)),
        out_shape=jax.ShapeDtypeStruct((GROUP, 8, rows), jnp.float32),
        in_specs=[VMEM] * len(inputs),
        out_specs=VMEM,
        scratch_shapes=[pltpu.VMEM((keys, rows), jnp.float32)],
        compiler_params=pltpu.CompilerParams(vmem_limit_bytes=32 * 1024 * 1024),
        cost_estimate=pl.CostEstimate(
            flops=8 * keys * rows * HEAD_SIZE * GROUP, bytes_accessed=1024 * 1024,
            transcendentals=keys * rows * GROUP),
    )(*inputs)


def grads(place, low, high, state, row_arrays, pieces, before, last):
    rows = low.shape[1]
    row_count = rows // 4
    sources = sum(piece.shape[0] for piece in pieces)
    keys = sources * row_count
    width = 2 * HEAD_SIZE
    first = before is None
    inputs = (low, high, state, *row_arrays, *pieces) + (() if first else (before,))
    parts = tuple(jax.ShapeDtypeStruct((piece.shape[0], row_count, width), jnp.bfloat16) for piece in pieces)
    extra = (jax.ShapeDtypeStruct((GROUP, 8, rows), jnp.float32),) if first else ()
    if last:
        dq = jax.ShapeDtypeStruct((4, row_count, GROUP * HEAD_SIZE + width), jnp.bfloat16)
    else:
        dq = jax.ShapeDtypeStruct((GROUP, HEAD_SIZE, rows), jnp.float32)
    return pl.pallas_call(
        functools.partial(grads_kernel, first, last, len(pieces)),
        out_shape=(dq,) + parts + extra,
        in_specs=[SMEM] + [VMEM] * len(inputs),
        out_specs=(VMEM,) * (1 + len(parts) + len(extra)),
        scratch_shapes=[
            pltpu.VMEM((keys, rows), jnp.float32),
            pltpu.VMEM((HEAD_SIZE, keys), jnp.bfloat16),
            pltpu.VMEM((keys, HEADS_PER_STEP * rows), jnp.bfloat16),
            pltpu.VMEM((keys, width), jnp.float32),
        ],
        compiler_params=pltpu.CompilerParams(vmem_limit_bytes=32 * 1024 * 1024),
        cost_estimate=pl.CostEstimate(
            flops=16 * keys * rows * HEAD_SIZE * GROUP, bytes_accessed=2 * 1024 * 1024,
            transcendentals=keys * rows * GROUP),
    )(place, *inputs)


def copies(pairs, sems):
    started = [pltpu.make_async_copy(source, target, sems.at[i]) for i, (source, target) in enumerate(pairs)]
    for copy in started:
        copy.start()
    for copy in started:
        copy.wait()


def pack_keys_kernel(place_ref, code_ref, k_ref, v_ref, self_ref, pair_ref, across_ref, sems):
    row_count = k_ref.shape[1]
    place = place_ref[0]
    targets = ((0, self_ref), (1, pair_ref.at[0]), (3, pair_ref.at[1]), (2, across_ref))
    pairs = []
    for r, target in targets:
        pairs.append((k_ref.at[place ^ r], target.at[0:row_count, 0:HEAD_SIZE]))
        pairs.append((v_ref.at[place ^ r], target.at[0:row_count, HEAD_SIZE:2 * HEAD_SIZE]))
    for r, target in targets:
        code = code_ref[pl.ds(place ^ r, 1), :]
        for i, digit in enumerate((code >> 7, code & 127)):
            spread = jnp.broadcast_to(digit.astype(jnp.float32), (META_ROWS, 128)).astype(jnp.bfloat16)
            target[row_count:row_count + META_ROWS, i * 128:(i + 1) * 128] = spread
    copies(pairs, sems)


def pack_rows_kernel(place_ref, q_ref, do_ref, *refs):
    out_refs, sems = refs[0:4], refs[4]
    row_count = q_ref.shape[1]
    place = place_ref[0]
    pairs = []
    for r, target in enumerate(out_refs):
        pairs.append((q_ref.at[place ^ r], target.at[0:row_count]))
        pairs.append((do_ref.at[place ^ r], target.at[row_count:2 * row_count]))
    copies(pairs, sems)


def own_kernel(self_ref, pair_ref, across_ref, own_ref, low_ref, high_ref):
    row_count = self_ref.shape[0] - META_ROWS
    codes = []
    for r, value in enumerate((self_ref[...], pair_ref[0], across_ref[0], across_ref[1])):
        own_ref[r] = value
        digits = value[row_count:, :].astype(jnp.float32)[0:8, :]
        codes.append(digits[:, 0:128] * 128.0 + digits[:, 128:256])
    lane = lax.broadcasted_iota(jnp.int32, (8, 128), 1)
    for i in range(2):
        code = jnp.where(lane < row_count, codes[2 * i], pltpu.roll(codes[2 * i + 1], row_count, 1))[0:1, :]
        high_ref[:, i * 128:(i + 1) * 128] = code
        low_ref[:, i * 128:(i + 1) * 128] = jnp.floor(code * (1.0 / CODE_SPAN)) * CODE_SPAN


def pack_keys(place, code, key_vectors, value_vectors):
    lines = key_vectors.shape[1] + META_ROWS
    one = jax.ShapeDtypeStruct((lines, 2 * HEAD_SIZE), jnp.bfloat16)
    two = jax.ShapeDtypeStruct((2, lines, 2 * HEAD_SIZE), jnp.bfloat16)
    return pl.pallas_call(
        pack_keys_kernel,
        out_shape=(one, two, one),
        in_specs=[SMEM, VMEM, ANY, ANY],
        out_specs=(VMEM,) * 3,
        scratch_shapes=[pltpu.SemaphoreType.DMA((8,))],
        compiler_params=pltpu.CompilerParams(vmem_limit_bytes=32 * 1024 * 1024),
    )(place, code, key_vectors, value_vectors)


def pack_rows(place, queries, output_gradient):
    row_count, wide = queries.shape[1:]
    return pl.pallas_call(
        pack_rows_kernel,
        out_shape=(jax.ShapeDtypeStruct((2 * row_count, wide), jnp.bfloat16),) * 4,
        in_specs=[SMEM, ANY, ANY],
        out_specs=(VMEM,) * 4,
        scratch_shapes=[pltpu.SemaphoreType.DMA((8,))],
        compiler_params=pltpu.CompilerParams(vmem_limit_bytes=32 * 1024 * 1024),
    )(place, queries, output_gradient)


def own_keys(mine, paired, crossed):
    rows = 4 * (mine.shape[0] - META_ROWS)
    row = jax.ShapeDtypeStruct((1, rows), jnp.float32)
    own = jax.ShapeDtypeStruct((4,) + mine.shape, jnp.bfloat16)
    return pl.pallas_call(
        own_kernel,
        out_shape=(own, row, row),
        in_specs=[VMEM] * 3,
        out_specs=(VMEM,) * 3,
        compiler_params=pltpu.CompilerParams(vmem_limit_bytes=32 * 1024 * 1024),
    )(mine, paired, crossed)


PLANE = ("xh", "core")
FINAL = ("xh", "core", "y", "xl")
RING = 8


def swapped(array, axes, by, count):
    return lax.ppermute(array, axes, [(i, i ^ by) for i in range(count)])


def turned(array, by):
    return lax.ppermute(array, "z", [(i, (i + by) % RING) for i in range(RING)])


def plus(*arrays):
    return sum(a.astype(jnp.float32) for a in arrays).astype(jnp.bfloat16)


def on_device(queries, key_vectors, value_vectors, output_gradient, positions, segments):
    window_count, row_count, _ = queries.shape
    across, pair = lax.axis_index("xh"), lax.axis_index("core")
    place = across * 2 + pair

    spot = place.reshape(1).astype(jnp.int32)
    code = jnp.pad(segments * CODE_SPAN + positions, ((0, 0), (0, 128 - row_count)))
    tied = lax.optimization_barrier
    mine, to_pair, across_part = pack_keys(spot, code, key_vectors, value_vectors)
    paired = swapped(to_pair, PLANE, 1, 4)
    spot, to_pair = tied((spot, to_pair))
    loads = pack_rows(spot, queries, output_gradient)
    crossed = swapped(jnp.stack([across_part, paired[1]]), PLANE, 2, 4)
    crossed, far_rows = tied((crossed, loads[2:4]))
    row_arrays = [loads[0], swapped(loads[1], PLANE, 1, 4)] + [swapped(far_rows[r - 2], PLANE, r, 4) for r in (2, 3)]
    own, low, high = own_keys(mine, paired, crossed)

    below, above = [own], [own]
    for _ in range(2):
        below.append(turned(below[-1], 1))
        above.append(turned(above[-1], -1))
    below.append(turned(below[2], 1))
    above.append(turned(above[2], -1))
    state = stats(low, high, row_arrays, [own, below[1], above[1]], None)
    state, below[3], above[3] = tied((state, below[3], above[3]))
    opposite = turned(below[3], 1)
    state = stats(low, high, row_arrays, [below[2], above[2], below[3], above[3]], state)
    state, opposite = tied((state, opposite))

    def gradients(pieces, before, last=False):
        return grads(spot, low, high, state, row_arrays, pieces, before, last)

    dq, to_up, state = gradients([opposite], None)
    spot, dq, to_up = tied((spot, dq, to_up))
    up = turned(to_up, 1)
    dq, up_grad, down_grad = gradients([above[3], below[3]], dq)
    dq, up_grad, down_grad, up = tied((dq, up_grad, down_grad, up))
    to_up, to_down = plus(up_grad, up), down_grad
    for k in (2, 1, 0):
        spot, dq, to_up, to_down = tied((spot, dq, to_up, to_down))
        up, down = turned(to_up, 1), turned(to_down, -1)
        if k:
            dq, up_grad, down_grad = gradients([above[k], below[k]], dq)
            dq, up_grad, down_grad, up, down = tied((dq, up_grad, down_grad, up, down))
            to_up, to_down = plus(up_grad, up), plus(down_grad, down)
    dq, own_grad = gradients([own], dq, True)
    dq, own_grad, up, down = tied((dq, own_grad, up, down))
    dkv_own = plus(own_grad, up, down)

    flip = dkv_own.reshape((2, 2) + dkv_own.shape[1:])
    flip = jnp.where(across == 1, flip[::-1], flip)
    flip = jnp.where(pair == 1, flip[:, ::-1], flip)

    heads = KEY_VALUE_HEADS
    out_rows = row_count // heads
    split = GROUP * HEAD_SIZE
    leaving = dq.at[:, :, split:].set(flip.reshape(dkv_own.shape)).reshape(window_count * heads, out_rows, split + 2 * HEAD_SIZE)
    final = lax.all_to_all(leaving, FINAL, 0, 0, tiled=True)

    def merged(array):
        width = array.shape[-1]
        return array.reshape(window_count, heads, out_rows, width).transpose(0, 2, 1, 3).reshape(window_count, out_rows, heads * width)

    return (
        merged(final[..., 0:split]),
        merged(final[..., split:split + HEAD_SIZE]),
        merged(final[..., split + HEAD_SIZE:]),
    )


def solution(mesh):
    fine = Mesh(mesh.devices.reshape(2, RING, 2, 4, 2), ("xh", "z", "core", "y", "xl"))
    ctx, head = ("xh", "z", "core"), ("y", "xl")
    vectors = P(None, ctx, head)
    out = P(None, ctx + head, None)
    return jax.shard_map(
        on_device,
        mesh=fine,
        in_specs=(vectors, vectors, vectors, vectors, P(None, ctx), P(None, ctx)),
        out_specs=(out, out, out),
        check_vma=False,
    )
```

```python
import functools
import math

import jax
import jax.numpy as jnp
from jax import lax
from jax.experimental import pallas as pl
from jax.experimental.pallas import tpu as pltpu
from jax.sharding import Mesh, PartitionSpec as P

QUERY_HEADS = 64
KEY_VALUE_HEADS = 8
HEAD_SIZE = 128
GROUP = QUERY_HEADS // KEY_VALUE_HEADS
NEG_BIG = -1e30
CODE_SPAN = 2048
META_ROWS = 16
HEADS_PER_STEP = 4
SCALE = 1.0 / math.sqrt(HEAD_SIZE)
EXP2_SCALE = SCALE * math.log2(math.e)

NT = (((1,), (1,)), ((), ()))
NN = (((1,), (0,)), ((), ()))


def dot(a, b, dims):
    return lax.dot_general(a, b, dims, preferred_element_type=jnp.float32)


def key_spans(piece_refs):
    spans, start = [], 0
    for ref in piece_refs:
        size = ref.shape[0] - META_ROWS
        spans.append((ref, slice(start, start + size), size))
        start += size
    return spans, start


def keys_of(ref, size):
    return ref[0:size, 0:HEAD_SIZE]


def values_of(ref, size):
    return ref[0:size, HEAD_SIZE:2 * HEAD_SIZE]


def fill_bias(bias_ref, spans, low_ref, high_ref, row_count):
    rows = low_ref.shape[1]
    for ref, part, size in spans:
        digits = ref[size:size + META_ROWS, :].astype(jnp.float32)
        codes = digits[:, 0:128] * 128.0 + digits[:, 128:256]
        for b in range(size // row_count):
            column = jnp.broadcast_to(codes[b:b + 1, :], (128, 128)).T[0:row_count, :]
            begin = part.start + b * row_count
            for r in range(rows // 128):
                low = low_ref[:, r * 128:(r + 1) * 128]
                high = high_ref[:, r * 128:(r + 1) * 128]
                allowed = (column >= low) & (column <= high)
                bias_ref[begin:begin + row_count, r * 128:(r + 1) * 128] = jnp.where(allowed, 0.0, NEG_BIG)


def rows_of(row_refs, lanes, row_count):
    q = jnp.concatenate([ref[0:row_count, lanes] for ref in row_refs], axis=0)
    do = jnp.concatenate([ref[row_count:2 * row_count, lanes] for ref in row_refs], axis=0)
    return q, do


def absorbed(top, total, cross, scores, softmax_grads):
    rows = top.shape[1]
    new = top
    for s in scores:
        peak = jnp.max(s.reshape(s.shape[0] // 8, 8, rows), axis=0)
        new = jnp.maximum(new, jnp.max(peak, axis=0, keepdims=True))
    factor = jnp.exp2(top - new)
    total, cross = total * factor, cross * factor
    weights = [jnp.exp2(s - new) for s in scores]
    for p, dp in zip(weights, softmax_grads):
        part_sum = jnp.sum(p.reshape(p.shape[0] // 8, 8, rows), axis=0)
        part_dot = jnp.sum((p * dp).reshape(p.shape[0] // 8, 8, rows), axis=0)
        total = total + jnp.sum(part_sum, axis=0, keepdims=True)
        cross = cross + jnp.sum(part_dot, axis=0, keepdims=True)
    return new, total, cross, weights


def stats_kernel(first, count, low_ref, high_ref, *refs):
    row_refs, piece_refs, rest = refs[0:4], refs[4:4 + count], refs[4 + count:]
    state_ref, bias_ref = rest[-2:]
    rows = low_ref.shape[1]
    row_count = rows // 4
    spans, _ = key_spans(piece_refs)
    fill_bias(bias_ref, spans, low_ref, high_ref, row_count)

    def step(g, carry):
        for j in range(HEADS_PER_STEP):
            h = g * HEADS_PER_STEP + j
            lanes = pl.ds(pl.multiple_of(h * HEAD_SIZE, HEAD_SIZE), HEAD_SIZE)
            q, do = rows_of(row_refs, lanes, row_count)
            if first:
                top = jnp.full((1, rows), NEG_BIG, jnp.float32)
                total = jnp.zeros((1, rows), jnp.float32)
                cross = jnp.zeros((1, rows), jnp.float32)
            else:
                top, total, cross = rest[0][h, 0:1, :], rest[0][h, 1:2, :], rest[0][h, 2:3, :]
            for ref, part, size in spans:
                s = dot(keys_of(ref, size), q, NT) * EXP2_SCALE + bias_ref[part, :]
                dp = dot(values_of(ref, size), do, NT)
                top, total, cross = absorbed(top, total, cross, [s], [dp])[0:3]
            state_ref[h, 0:1, :] = top
            state_ref[h, 1:2, :] = total
            state_ref[h, 2:3, :] = cross
        return carry

    lax.fori_loop(0, GROUP // HEADS_PER_STEP, step, 0)


def grads_kernel(first, last, count, place_ref, low_ref, high_ref, state_ref, *refs):
    row_refs, piece_refs, rest = refs[0:4], refs[4:4 + count], refs[4 + count:]
    if not first:
        before_ref, rest = rest[0], rest[1:]
    dq_ref, out_refs, rest = rest[0], rest[1:1 + count], rest[1 + count:]
    if first:
        final_ref, rest = rest[0], rest[1:]
    bias_ref, kt_ref, ds_ref, acc_ref = rest
    rows = low_ref.shape[1]
    row_count = rows // 4
    heads = HEADS_PER_STEP
    spans, keys = key_spans(piece_refs)
    fill_bias(bias_ref, spans, low_ref, high_ref, row_count)
    for ref, part, size in spans:
        kt_ref[:, part] = keys_of(ref, size).T
    acc_ref[...] = jnp.zeros_like(acc_ref)
    place = place_ref[0]

    def step(g, carry):
        q, do, lanes, p_low, ds_low = [], [], [], [], []
        for j in range(heads):
            h = g * heads + j
            lanes.append(pl.ds(pl.multiple_of(h * HEAD_SIZE, HEAD_SIZE), HEAD_SIZE))
            one_q, one_do = rows_of(row_refs, lanes[j], row_count)
            q.append(one_q)
            do.append(one_do)

            def products(ref, part, size):
                s = dot(keys_of(ref, size), one_q, NT) * EXP2_SCALE + bias_ref[part, :]
                return s, dot(values_of(ref, size), one_do, NT)

            if first:
                pairs = [products(*span) for span in spans]
                top, total, cross, weights = absorbed(
                    state_ref[h, 0:1, :], state_ref[h, 1:2, :], state_ref[h, 2:3, :],
                    [s for s, _ in pairs], [dp for _, dp in pairs])
                inverse = 1.0 / total
                delta = cross * inverse
                final_ref[h, 0:1, :] = top + jnp.log2(total)
                final_ref[h, 1:2, :] = delta
                softmax = [p * inverse for p in weights]
                softmax_grads = [dp for _, dp in pairs]
            else:
                offset, delta = state_ref[h, 0:1, :], state_ref[h, 1:2, :]
                softmax, softmax_grads = [], []
                for span in spans:
                    s, dp = products(*span)
                    softmax.append(jnp.exp2(s - offset))
                    softmax_grads.append(dp)
            p_low.append([p.astype(jnp.bfloat16) for p in softmax])
            ds_low.append([(p * (dp - delta)).astype(jnp.bfloat16) for p, dp in zip(softmax, softmax_grads)])
        q_all, do_all = jnp.concatenate(q, axis=0), jnp.concatenate(do, axis=0)
        for i, (ref, part, size) in enumerate(spans):
            p_all = jnp.concatenate([p_low[j][i] for j in range(heads)], axis=1)
            ds_all = jnp.concatenate([ds_low[j][i] for j in range(heads)], axis=1)
            ds_ref[part, :] = ds_all
            acc_ref[part, HEAD_SIZE:2 * HEAD_SIZE] += dot(p_all, do_all, NN)
            acc_ref[part, 0:HEAD_SIZE] += dot(ds_all, q_all, NN)
        dqt = dot(kt_ref[...], ds_ref[...], NN)
        for j in range(heads):
            part = dqt[:, j * rows:(j + 1) * rows]
            if not first:
                part = part + before_ref[g * heads + j]
            if last:
                dq = (part * SCALE).T.astype(jnp.bfloat16)
                for r in range(4):
                    dq_ref[place ^ r, :, lanes[j]] = dq[r * row_count:(r + 1) * row_count, :]
            else:
                dq_ref[g * heads + j] = part
        return carry

    lax.fori_loop(0, GROUP // heads, step, 0)
    for out_ref, (_, part, size) in zip(out_refs, spans):
        shape = (size // row_count, row_count, HEAD_SIZE)
        out_ref[:, :, 0:HEAD_SIZE] = (acc_ref[part, 0:HEAD_SIZE] * SCALE).astype(jnp.bfloat16).reshape(shape)
        out_ref[:, :, HEAD_SIZE:2 * HEAD_SIZE] = acc_ref[part, HEAD_SIZE:2 * HEAD_SIZE].astype(jnp.bfloat16).reshape(shape)


VMEM = pl.BlockSpec(memory_space=pltpu.VMEM)
SMEM = pl.BlockSpec(memory_space=pltpu.SMEM)
ANY = pl.BlockSpec(memory_space=pltpu.HBM)


def stats(low, high, row_arrays, pieces, state):
    rows = low.shape[1]
    keys = sum(piece.shape[0] - META_ROWS for piece in pieces)
    first = state is None
    inputs = (low, high, *row_arrays, *pieces) + (() if first else (state,))
    return pl.pallas_call(
        functools.partial(stats_kernel, first, len(pieces)),
        out_shape=jax.ShapeDtypeStruct((GROUP, 8, rows), jnp.float32),
        in_specs=[VMEM] * len(inputs),
        out_specs=VMEM,
        scratch_shapes=[pltpu.VMEM((keys, rows), jnp.float32)],
        compiler_params=pltpu.CompilerParams(vmem_limit_bytes=32 * 1024 * 1024),
        cost_estimate=pl.CostEstimate(
            flops=8 * keys * rows * HEAD_SIZE * GROUP, bytes_accessed=1024 * 1024,
            transcendentals=keys * rows * GROUP),
    )(*inputs)


def grads(place, low, high, state, row_arrays, pieces, before, last):
    rows = low.shape[1]
    row_count = rows // 4
    keys = sum(piece.shape[0] - META_ROWS for piece in pieces)
    width = 2 * HEAD_SIZE
    first = before is None
    inputs = (low, high, state, *row_arrays, *pieces) + (() if first else (before,))
    parts = tuple(jax.ShapeDtypeStruct((4, row_count, width), jnp.bfloat16) for piece in pieces)
    extra = (jax.ShapeDtypeStruct((GROUP, 8, rows), jnp.float32),) if first else ()
    if last:
        dq = jax.ShapeDtypeStruct((4, row_count, GROUP * HEAD_SIZE + width), jnp.bfloat16)
    else:
        dq = jax.ShapeDtypeStruct((GROUP, HEAD_SIZE, rows), jnp.float32)
    return pl.pallas_call(
        functools.partial(grads_kernel, first, last, len(pieces)),
        out_shape=(dq,) + parts + extra,
        in_specs=[SMEM] + [VMEM] * len(inputs),
        out_specs=(VMEM,) * (1 + len(parts) + len(extra)),
        scratch_shapes=[
            pltpu.VMEM((keys, rows), jnp.float32),
            pltpu.VMEM((HEAD_SIZE, keys), jnp.bfloat16),
            pltpu.VMEM((keys, HEADS_PER_STEP * rows), jnp.bfloat16),
            pltpu.VMEM((keys, width), jnp.float32),
        ],
        compiler_params=pltpu.CompilerParams(vmem_limit_bytes=32 * 1024 * 1024),
        cost_estimate=pl.CostEstimate(
            flops=16 * keys * rows * HEAD_SIZE * GROUP, bytes_accessed=2 * 1024 * 1024,
            transcendentals=keys * rows * GROUP),
    )(place, *inputs)


def copies(pairs, sems):
    started = [pltpu.make_async_copy(source, target, sems.at[i]) for i, (source, target) in enumerate(pairs)]
    for copy in started:
        copy.start()
    for copy in started:
        copy.wait()


def pack_keys_kernel(place_ref, code_ref, k_ref, v_ref, self_ref, pair_ref, across_ref, sems):
    row_count = k_ref.shape[1]
    place = place_ref[0]
    targets = ((0, self_ref), (1, pair_ref.at[0]), (3, pair_ref.at[1]), (2, across_ref))
    pairs = []
    for r, target in targets:
        pairs.append((k_ref.at[place ^ r], target.at[0:row_count, 0:HEAD_SIZE]))
        pairs.append((v_ref.at[place ^ r], target.at[0:row_count, HEAD_SIZE:2 * HEAD_SIZE]))
    for r, target in targets:
        code = code_ref[pl.ds(place ^ r, 1), :]
        for i, digit in enumerate((code >> 7, code & 127)):
            spread = jnp.broadcast_to(digit.astype(jnp.float32), (META_ROWS, 128)).astype(jnp.bfloat16)
            target[row_count:row_count + META_ROWS, i * 128:(i + 1) * 128] = spread
    copies(pairs, sems)


def pack_rows_kernel(place_ref, q_ref, do_ref, *refs):
    out_refs, sems = refs[0:4], refs[4]
    row_count = q_ref.shape[1]
    place = place_ref[0]
    pairs = []
    for r, target in enumerate(out_refs):
        pairs.append((q_ref.at[place ^ r], target.at[0:row_count]))
        pairs.append((do_ref.at[place ^ r], target.at[row_count:2 * row_count]))
    copies(pairs, sems)


def own_kernel(self_ref, pair_ref, across_ref, own_ref, low_ref, high_ref):
    row_count = self_ref.shape[0] - META_ROWS
    line = lax.broadcasted_iota(jnp.int32, (META_ROWS, 2 * HEAD_SIZE), 0)
    meta = jnp.zeros((META_ROWS, 2 * HEAD_SIZE), jnp.float32)
    codes = []
    for r, value in enumerate((self_ref[...], pair_ref[0], across_ref[0], across_ref[1])):
        own_ref[r * row_count:(r + 1) * row_count, :] = value[0:row_count, :]
        digits = value[row_count:, :].astype(jnp.float32)
        meta = jnp.where(line == r, digits, meta)
        codes.append(digits[0:8, 0:128] * 128.0 + digits[0:8, 128:256])
    own_ref[4 * row_count:, :] = meta.astype(jnp.bfloat16)
    lane = lax.broadcasted_iota(jnp.int32, (8, 128), 1)
    for i in range(2):
        code = jnp.where(lane < row_count, codes[2 * i], pltpu.roll(codes[2 * i + 1], row_count, 1))[0:1, :]
        high_ref[:, i * 128:(i + 1) * 128] = code
        low_ref[:, i * 128:(i + 1) * 128] = jnp.floor(code * (1.0 / CODE_SPAN)) * CODE_SPAN


def pack_keys(place, code, key_vectors, value_vectors):
    lines = key_vectors.shape[1] + META_ROWS
    one = jax.ShapeDtypeStruct((lines, 2 * HEAD_SIZE), jnp.bfloat16)
    two = jax.ShapeDtypeStruct((2, lines, 2 * HEAD_SIZE), jnp.bfloat16)
    return pl.pallas_call(
        pack_keys_kernel,
        out_shape=(one, two, one),
        in_specs=[SMEM, VMEM, ANY, ANY],
        out_specs=(VMEM,) * 3,
        scratch_shapes=[pltpu.SemaphoreType.DMA((8,))],
        compiler_params=pltpu.CompilerParams(vmem_limit_bytes=32 * 1024 * 1024),
    )(place, code, key_vectors, value_vectors)


def pack_rows(place, queries, output_gradient):
    row_count, wide = queries.shape[1:]
    return pl.pallas_call(
        pack_rows_kernel,
        out_shape=(jax.ShapeDtypeStruct((2 * row_count, wide), jnp.bfloat16),) * 4,
        in_specs=[SMEM, ANY, ANY],
        out_specs=(VMEM,) * 4,
        scratch_shapes=[pltpu.SemaphoreType.DMA((8,))],
        compiler_params=pltpu.CompilerParams(vmem_limit_bytes=32 * 1024 * 1024),
    )(place, queries, output_gradient)


def own_keys(mine, paired, crossed):
    rows = 4 * (mine.shape[0] - META_ROWS)
    row = jax.ShapeDtypeStruct((1, rows), jnp.float32)
    own = jax.ShapeDtypeStruct((rows + META_ROWS, mine.shape[1]), jnp.bfloat16)
    return pl.pallas_call(
        own_kernel,
        out_shape=(own, row, row),
        in_specs=[VMEM] * 3,
        out_specs=(VMEM,) * 3,
        compiler_params=pltpu.CompilerParams(vmem_limit_bytes=32 * 1024 * 1024),
    )(mine, paired, crossed)


PLANE = ("xh", "core")
FINAL = ("xh", "core", "y", "xl")
RING = 8


def swapped(array, axes, by, count):
    return lax.ppermute(array, axes, [(i, i ^ by) for i in range(count)])


def turned(array, by):
    return lax.ppermute(array, "z", [(i, (i + by) % RING) for i in range(RING)])


def plus(*arrays):
    return sum(a.astype(jnp.float32) for a in arrays).astype(jnp.bfloat16)


def on_device(queries, key_vectors, value_vectors, output_gradient, positions, segments):
    window_count, row_count, _ = queries.shape
    across, pair = lax.axis_index("xh"), lax.axis_index("core")
    place = across * 2 + pair

    spot = place.reshape(1).astype(jnp.int32)
    code = jnp.pad(segments * CODE_SPAN + positions, ((0, 0), (0, 128 - row_count)))
    tied = lax.optimization_barrier
    mine, to_pair, across_part = pack_keys(spot, code, key_vectors, value_vectors)
    paired = swapped(to_pair, PLANE, 1, 4)
    spot, to_pair = tied((spot, to_pair))
    loads = pack_rows(spot, queries, output_gradient)
    crossed = swapped(jnp.stack([across_part, paired[1]]), PLANE, 2, 4)
    crossed, far_rows = tied((crossed, loads[2:4]))
    row_arrays = [loads[0], swapped(loads[1], PLANE, 1, 4)] + [swapped(far_rows[r - 2], PLANE, r, 4) for r in (2, 3)]
    own, low, high = own_keys(mine, paired, crossed)

    below, above = [own], [own]
    for _ in range(2):
        below.append(turned(below[-1], 1))
        above.append(turned(above[-1], -1))
    below.append(turned(below[2], 1))
    above.append(turned(above[2], -1))
    state = stats(low, high, row_arrays, [own, below[1], above[1], below[2], above[2]], None)
    state, below[3], above[3] = tied((state, below[3], above[3]))
    opposite = turned(below[3], 1)
    state = stats(low, high, row_arrays, [below[3], above[3]], state)
    state, opposite = tied((state, opposite))

    def gradients(pieces, before, last=False):
        return grads(spot, low, high, state, row_arrays, pieces, before, last)

    dq, to_up, state = gradients([opposite], None)
    spot, dq, to_up = tied((spot, dq, to_up))
    up = turned(to_up, 1)
    dq, up_grad, down_grad = gradients([above[3], below[3]], dq)
    dq, up_grad, down_grad, up = tied((dq, up_grad, down_grad, up))
    to_up, to_down = plus(up_grad, up), down_grad
    for k in (2, 1, 0):
        spot, dq, to_up, to_down = tied((spot, dq, to_up, to_down))
        up, down = turned(to_up, 1), turned(to_down, -1)
        if k:
            dq, up_grad, down_grad = gradients([above[k], below[k]], dq)
            dq, up_grad, down_grad, up, down = tied((dq, up_grad, down_grad, up, down))
            to_up, to_down = plus(up_grad, up), plus(down_grad, down)
    dq, own_grad = gradients([own], dq, True)
    dq, own_grad, up, down = tied((dq, own_grad, up, down))
    dkv_own = plus(own_grad, up, down)

    flip = dkv_own.reshape((2, 2) + dkv_own.shape[1:])
    flip = jnp.where(across == 1, flip[::-1], flip)
    flip = jnp.where(pair == 1, flip[:, ::-1], flip)

    heads = KEY_VALUE_HEADS
    out_rows = row_count // heads
    split = GROUP * HEAD_SIZE
    leaving = dq.at[:, :, split:].set(flip.reshape(dkv_own.shape)).reshape(window_count * heads, out_rows, split + 2 * HEAD_SIZE)
    final = lax.all_to_all(leaving, FINAL, 0, 0, tiled=True)

    def merged(array):
        width = array.shape[-1]
        return array.reshape(window_count, heads, out_rows, width).transpose(0, 2, 1, 3).reshape(window_count, out_rows, heads * width)

    return (
        merged(final[..., 0:split]),
        merged(final[..., split:split + HEAD_SIZE]),
        merged(final[..., split + HEAD_SIZE:]),
    )


def solution(mesh):
    fine = Mesh(mesh.devices.reshape(2, RING, 2, 4, 2), ("xh", "z", "core", "y", "xl"))
    ctx, head = ("xh", "z", "core"), ("y", "xl")
    vectors = P(None, ctx, head)
    out = P(None, ctx + head, None)
    return jax.shard_map(
        on_device,
        mesh=fine,
        in_specs=(vectors, vectors, vectors, vectors, P(None, ctx), P(None, ctx)),
        out_specs=(out, out, out),
        check_vma=False,
    )
```

```python
import functools
import math

import jax
import jax.numpy as jnp
from jax import lax
from jax.experimental import pallas as pl
from jax.experimental.pallas import tpu as pltpu
from jax.sharding import Mesh, PartitionSpec as P

QUERY_HEADS = 64
KEY_VALUE_HEADS = 8
HEAD_SIZE = 128
GROUP = QUERY_HEADS // KEY_VALUE_HEADS
NEG_BIG = -1e30
CODE_SPAN = 2048
META_ROWS = 16
HEADS_PER_STEP = 4
SCALE = 1.0 / math.sqrt(HEAD_SIZE)
EXP2_SCALE = SCALE * math.log2(math.e)

NT = (((1,), (1,)), ((), ()))
NN = (((1,), (0,)), ((), ()))


def dot(a, b, dims):
    return lax.dot_general(a, b, dims, preferred_element_type=jnp.float32)


def key_spans(piece_refs):
    spans, start = [], 0
    for ref in piece_refs:
        size = ref.shape[0] - META_ROWS
        spans.append((ref, slice(start, start + size), size))
        start += size
    return spans, start


def keys_of(ref, size):
    return ref[0:size, 0:HEAD_SIZE]


def values_of(ref, size):
    return ref[0:size, HEAD_SIZE:2 * HEAD_SIZE]


def fill_bias(bias_ref, spans, low_ref, high_ref, row_count):
    rows = low_ref.shape[1]
    for ref, part, size in spans:
        digits = ref[size:size + META_ROWS, :].astype(jnp.float32)
        codes = digits[:, 0:128] * 128.0 + digits[:, 128:256]
        for b in range(size // row_count):
            column = jnp.broadcast_to(codes[b:b + 1, :], (128, 128)).T[0:row_count, :]
            begin = part.start + b * row_count
            for r in range(rows // 128):
                low = low_ref[:, r * 128:(r + 1) * 128]
                high = high_ref[:, r * 128:(r + 1) * 128]
                allowed = (column >= low) & (column <= high)
                bias_ref[begin:begin + row_count, r * 128:(r + 1) * 128] = jnp.where(allowed, 0.0, NEG_BIG)


def rows_of(row_refs, lanes, row_count):
    q = jnp.concatenate([ref[0:row_count, lanes] for ref in row_refs], axis=0)
    do = jnp.concatenate([ref[row_count:2 * row_count, lanes] for ref in row_refs], axis=0)
    return q, do


def absorbed(top, total, cross, scores, softmax_grads):
    rows = top.shape[1]
    new = top
    for s in scores:
        peak = jnp.max(s.reshape(s.shape[0] // 8, 8, rows), axis=0)
        new = jnp.maximum(new, jnp.max(peak, axis=0, keepdims=True))
    factor = jnp.exp2(top - new)
    total, cross = total * factor, cross * factor
    weights = [jnp.exp2(s - new) for s in scores]
    for p, dp in zip(weights, softmax_grads):
        part_sum = jnp.sum(p.reshape(p.shape[0] // 8, 8, rows), axis=0)
        part_dot = jnp.sum((p * dp).reshape(p.shape[0] // 8, 8, rows), axis=0)
        total = total + jnp.sum(part_sum, axis=0, keepdims=True)
        cross = cross + jnp.sum(part_dot, axis=0, keepdims=True)
    return new, total, cross, weights


def stats_kernel(first, count, low_ref, high_ref, *refs):
    row_refs, piece_refs, rest = refs[0:4], refs[4:4 + count], refs[4 + count:]
    state_ref, bias_ref = rest[-2:]
    rows = low_ref.shape[1]
    row_count = rows // 4
    spans, _ = key_spans(piece_refs)
    fill_bias(bias_ref, spans, low_ref, high_ref, row_count)

    def step(g, carry):
        for j in range(HEADS_PER_STEP):
            h = g * HEADS_PER_STEP + j
            lanes = pl.ds(pl.multiple_of(h * HEAD_SIZE, HEAD_SIZE), HEAD_SIZE)
            q, do = rows_of(row_refs, lanes, row_count)
            if first:
                top = jnp.full((1, rows), NEG_BIG, jnp.float32)
                total = jnp.zeros((1, rows), jnp.float32)
                cross = jnp.zeros((1, rows), jnp.float32)
            else:
                top, total, cross = rest[0][h, 0:1, :], rest[0][h, 1:2, :], rest[0][h, 2:3, :]
            for ref, part, size in spans:
                s = dot(keys_of(ref, size), q, NT) * EXP2_SCALE + bias_ref[part, :]
                dp = dot(values_of(ref, size), do, NT)
                top, total, cross = absorbed(top, total, cross, [s], [dp])[0:3]
            state_ref[h, 0:1, :] = top
            state_ref[h, 1:2, :] = total
            state_ref[h, 2:3, :] = cross
        return carry

    lax.fori_loop(0, GROUP // HEADS_PER_STEP, step, 0)


def grads_kernel(first, last, count, place_ref, low_ref, high_ref, state_ref, *refs):
    row_refs, piece_refs, rest = refs[0:4], refs[4:4 + count], refs[4 + count:]
    if not first:
        before_ref, rest = rest[0], rest[1:]
    dq_ref, out_refs, rest = rest[0], rest[1:1 + count], rest[1 + count:]
    if first:
        final_ref, rest = rest[0], rest[1:]
    bias_ref, kt_ref, ds_ref, acc_ref = rest
    rows = low_ref.shape[1]
    row_count = rows // 4
    heads = HEADS_PER_STEP
    spans, keys = key_spans(piece_refs)
    fill_bias(bias_ref, spans, low_ref, high_ref, row_count)
    for ref, part, size in spans:
        kt_ref[:, part] = keys_of(ref, size).T
    acc_ref[...] = jnp.zeros_like(acc_ref)
    place = place_ref[0]

    def step(g, carry):
        q, do, lanes, p_low, ds_low = [], [], [], [], []
        for j in range(heads):
            h = g * heads + j
            lanes.append(pl.ds(pl.multiple_of(h * HEAD_SIZE, HEAD_SIZE), HEAD_SIZE))
            one_q, one_do = rows_of(row_refs, lanes[j], row_count)
            q.append(one_q)
            do.append(one_do)

            def products(ref, part, size):
                s = dot(keys_of(ref, size), one_q, NT) * EXP2_SCALE + bias_ref[part, :]
                return s, dot(values_of(ref, size), one_do, NT)

            if first:
                pairs = [products(*span) for span in spans]
                top, total, cross, weights = absorbed(
                    state_ref[h, 0:1, :], state_ref[h, 1:2, :], state_ref[h, 2:3, :],
                    [s for s, _ in pairs], [dp for _, dp in pairs])
                inverse = 1.0 / total
                delta = cross * inverse
                final_ref[h, 0:1, :] = top + jnp.log2(total)
                final_ref[h, 1:2, :] = delta
                softmax = [p * inverse for p in weights]
                softmax_grads = [dp for _, dp in pairs]
            else:
                offset, delta = state_ref[h, 0:1, :], state_ref[h, 1:2, :]
                softmax, softmax_grads = [], []
                for span in spans:
                    s, dp = products(*span)
                    softmax.append(jnp.exp2(s - offset))
                    softmax_grads.append(dp)
            p_low.append([p.astype(jnp.bfloat16) for p in softmax])
            ds_low.append([(p * (dp - delta)).astype(jnp.bfloat16) for p, dp in zip(softmax, softmax_grads)])
        q_all, do_all = jnp.concatenate(q, axis=0), jnp.concatenate(do, axis=0)
        for i, (ref, part, size) in enumerate(spans):
            p_all = jnp.concatenate([p_low[j][i] for j in range(heads)], axis=1)
            ds_all = jnp.concatenate([ds_low[j][i] for j in range(heads)], axis=1)
            ds_ref[part, :] = ds_all
            acc_ref[part, HEAD_SIZE:2 * HEAD_SIZE] += dot(p_all, do_all, NN)
            acc_ref[part, 0:HEAD_SIZE] += dot(ds_all, q_all, NN)
        dqt = dot(kt_ref[...], ds_ref[...], NN)
        for j in range(heads):
            part = dqt[:, j * rows:(j + 1) * rows]
            if not first:
                part = part + before_ref[g * heads + j]
            if last:
                dq = (part * SCALE).T.astype(jnp.bfloat16)
                for r in range(4):
                    dq_ref[place ^ r, :, lanes[j]] = dq[r * row_count:(r + 1) * row_count, :]
            else:
                dq_ref[g * heads + j] = part
        return carry

    lax.fori_loop(0, GROUP // heads, step, 0)
    for out_ref, (_, part, size) in zip(out_refs, spans):
        shape = (size // row_count, row_count, HEAD_SIZE)
        out_ref[:, :, 0:HEAD_SIZE] = (acc_ref[part, 0:HEAD_SIZE] * SCALE).astype(jnp.bfloat16).reshape(shape)
        out_ref[:, :, HEAD_SIZE:2 * HEAD_SIZE] = acc_ref[part, HEAD_SIZE:2 * HEAD_SIZE].astype(jnp.bfloat16).reshape(shape)


VMEM = pl.BlockSpec(memory_space=pltpu.VMEM)
SMEM = pl.BlockSpec(memory_space=pltpu.SMEM)
ANY = pl.BlockSpec(memory_space=pltpu.HBM)


def stats(low, high, row_arrays, pieces, state):
    rows = low.shape[1]
    keys = sum(piece.shape[0] - META_ROWS for piece in pieces)
    first = state is None
    inputs = (low, high, *row_arrays, *pieces) + (() if first else (state,))
    return pl.pallas_call(
        functools.partial(stats_kernel, first, len(pieces)),
        out_shape=jax.ShapeDtypeStruct((GROUP, 8, rows), jnp.float32),
        in_specs=[VMEM] * len(inputs),
        out_specs=VMEM,
        scratch_shapes=[pltpu.VMEM((keys, rows), jnp.float32)],
        compiler_params=pltpu.CompilerParams(vmem_limit_bytes=32 * 1024 * 1024),
        cost_estimate=pl.CostEstimate(
            flops=8 * keys * rows * HEAD_SIZE * GROUP, bytes_accessed=1024 * 1024,
            transcendentals=keys * rows * GROUP),
    )(*inputs)


def grads(place, low, high, state, row_arrays, pieces, before, last):
    rows = low.shape[1]
    row_count = rows // 4
    keys = sum(piece.shape[0] - META_ROWS for piece in pieces)
    width = 2 * HEAD_SIZE
    first = before is None
    inputs = (low, high, state, *row_arrays, *pieces) + (() if first else (before,))
    parts = tuple(jax.ShapeDtypeStruct((4, row_count, width), jnp.bfloat16) for piece in pieces)
    extra = (jax.ShapeDtypeStruct((GROUP, 8, rows), jnp.float32),) if first else ()
    if last:
        dq = jax.ShapeDtypeStruct((4, row_count, GROUP * HEAD_SIZE + width), jnp.bfloat16)
    else:
        dq = jax.ShapeDtypeStruct((GROUP, HEAD_SIZE, rows), jnp.float32)
    return pl.pallas_call(
        functools.partial(grads_kernel, first, last, len(pieces)),
        out_shape=(dq,) + parts + extra,
        in_specs=[SMEM] + [VMEM] * len(inputs),
        out_specs=(VMEM,) * (1 + len(parts) + len(extra)),
        scratch_shapes=[
            pltpu.VMEM((keys, rows), jnp.float32),
            pltpu.VMEM((HEAD_SIZE, keys), jnp.bfloat16),
            pltpu.VMEM((keys, HEADS_PER_STEP * rows), jnp.bfloat16),
            pltpu.VMEM((keys, width), jnp.float32),
        ],
        compiler_params=pltpu.CompilerParams(vmem_limit_bytes=32 * 1024 * 1024),
        cost_estimate=pl.CostEstimate(
            flops=16 * keys * rows * HEAD_SIZE * GROUP, bytes_accessed=2 * 1024 * 1024,
            transcendentals=keys * rows * GROUP),
    )(place, *inputs)


def copies(pairs, sems):
    started = [pltpu.make_async_copy(source, target, sems.at[i]) for i, (source, target) in enumerate(pairs)]
    for copy in started:
        copy.start()
    for copy in started:
        copy.wait()


def pack_keys_kernel(place_ref, code_ref, k_ref, v_ref, self_ref, pair_ref, across_ref, sems):
    row_count = k_ref.shape[1]
    place = place_ref[0]
    targets = ((0, self_ref), (1, pair_ref.at[0]), (3, pair_ref.at[1]), (2, across_ref))
    pairs = []
    for r, target in targets:
        pairs.append((k_ref.at[place ^ r], target.at[0:row_count, 0:HEAD_SIZE]))
        pairs.append((v_ref.at[place ^ r], target.at[0:row_count, HEAD_SIZE:2 * HEAD_SIZE]))
    for r, target in targets:
        code = code_ref[pl.ds(place ^ r, 1), :]
        for i, digit in enumerate((code >> 7, code & 127)):
            spread = jnp.broadcast_to(digit.astype(jnp.float32), (META_ROWS, 128)).astype(jnp.bfloat16)
            target[row_count:row_count + META_ROWS, i * 128:(i + 1) * 128] = spread
    copies(pairs, sems)


def pack_rows_kernel(place_ref, q_ref, do_ref, *refs):
    out_refs, sems = refs[0:4], refs[4]
    row_count = q_ref.shape[1]
    place = place_ref[0]
    pairs = []
    for r, target in enumerate(out_refs):
        pairs.append((q_ref.at[place ^ r], target.at[0:row_count]))
        pairs.append((do_ref.at[place ^ r], target.at[row_count:2 * row_count]))
    copies(pairs, sems)


def own_kernel(self_ref, pair_ref, across_ref, own_ref, low_ref, high_ref):
    row_count = self_ref.shape[0] - META_ROWS
    line = lax.broadcasted_iota(jnp.int32, (META_ROWS, 2 * HEAD_SIZE), 0)
    meta = jnp.zeros((META_ROWS, 2 * HEAD_SIZE), jnp.float32)
    codes = []
    for r, value in enumerate((self_ref[...], pair_ref[0], across_ref[0], across_ref[1])):
        own_ref[r * row_count:(r + 1) * row_count, :] = value[0:row_count, :]
        digits = value[row_count:, :].astype(jnp.float32)
        meta = jnp.where(line == r, digits, meta)
        codes.append(digits[0:8, 0:128] * 128.0 + digits[0:8, 128:256])
    own_ref[4 * row_count:, :] = meta.astype(jnp.bfloat16)
    lane = lax.broadcasted_iota(jnp.int32, (8, 128), 1)
    for i in range(2):
        code = jnp.where(lane < row_count, codes[2 * i], pltpu.roll(codes[2 * i + 1], row_count, 1))[0:1, :]
        high_ref[:, i * 128:(i + 1) * 128] = code
        low_ref[:, i * 128:(i + 1) * 128] = jnp.floor(code * (1.0 / CODE_SPAN)) * CODE_SPAN


def pack_keys(place, code, key_vectors, value_vectors):
    lines = key_vectors.shape[1] + META_ROWS
    one = jax.ShapeDtypeStruct((lines, 2 * HEAD_SIZE), jnp.bfloat16)
    two = jax.ShapeDtypeStruct((2, lines, 2 * HEAD_SIZE), jnp.bfloat16)
    return pl.pallas_call(
        pack_keys_kernel,
        out_shape=(one, two, one),
        in_specs=[SMEM, VMEM, ANY, ANY],
        out_specs=(VMEM,) * 3,
        scratch_shapes=[pltpu.SemaphoreType.DMA((8,))],
        compiler_params=pltpu.CompilerParams(vmem_limit_bytes=32 * 1024 * 1024),
    )(place, code, key_vectors, value_vectors)


def pack_rows(place, queries, output_gradient):
    row_count, wide = queries.shape[1:]
    return pl.pallas_call(
        pack_rows_kernel,
        out_shape=(jax.ShapeDtypeStruct((2 * row_count, wide), jnp.bfloat16),) * 4,
        in_specs=[SMEM, ANY, ANY],
        out_specs=(VMEM,) * 4,
        scratch_shapes=[pltpu.SemaphoreType.DMA((8,))],
        compiler_params=pltpu.CompilerParams(vmem_limit_bytes=32 * 1024 * 1024),
    )(place, queries, output_gradient)


def own_keys(mine, paired, crossed):
    rows = 4 * (mine.shape[0] - META_ROWS)
    row = jax.ShapeDtypeStruct((1, rows), jnp.float32)
    own = jax.ShapeDtypeStruct((rows + META_ROWS, mine.shape[1]), jnp.bfloat16)
    return pl.pallas_call(
        own_kernel,
        out_shape=(own, row, row),
        in_specs=[VMEM] * 3,
        out_specs=(VMEM,) * 3,
        compiler_params=pltpu.CompilerParams(vmem_limit_bytes=32 * 1024 * 1024),
    )(mine, paired, crossed)


PLANE = ("xh", "core")
FINAL = ("xh", "core", "y", "xl")
RING = 8


def swapped(array, axes, by, count):
    return lax.ppermute(array, axes, [(i, i ^ by) for i in range(count)])


def turned(array, by):
    return lax.ppermute(array, "z", [(i, (i + by) % RING) for i in range(RING)])


def plus(*arrays):
    return sum(a.astype(jnp.float32) for a in arrays).astype(jnp.bfloat16)


def on_device(queries, key_vectors, value_vectors, output_gradient, positions, segments):
    window_count, row_count, _ = queries.shape
    across, pair = lax.axis_index("xh"), lax.axis_index("core")
    place = across * 2 + pair

    spot = place.reshape(1).astype(jnp.int32)
    code = jnp.pad(segments * CODE_SPAN + positions, ((0, 0), (0, 128 - row_count)))
    tied = lax.optimization_barrier
    mine, to_pair, across_part = pack_keys(spot, code, key_vectors, value_vectors)
    paired = swapped(to_pair, PLANE, 1, 4)
    spot, to_pair = tied((spot, to_pair))
    loads = pack_rows(spot, queries, output_gradient)
    crossed = swapped(jnp.stack([across_part, paired[1]]), PLANE, 2, 4)
    crossed, far_rows = tied((crossed, loads[2:4]))
    row_arrays = [loads[0], swapped(loads[1], PLANE, 1, 4)] + [swapped(far_rows[r - 2], PLANE, r, 4) for r in (2, 3)]
    own, low, high = own_keys(mine, paired, crossed)

    below, above = [own], [own]
    for _ in range(2):
        below.append(turned(below[-1], 1))
        above.append(turned(above[-1], -1))
    below.append(turned(below[2], 1))
    above.append(turned(above[2], -1))
    state = stats(low, high, row_arrays, [own, below[1], above[1], below[2], above[2]], None)
    state, below[3], above[3] = tied((state, below[3], above[3]))
    opposite = turned(below[3], 1)
    state = stats(low, high, row_arrays, [below[3], above[3]], state)
    state, opposite = tied((state, opposite))

    def gradients(pieces, before, last=False):
        return grads(spot, low, high, state, row_arrays, pieces, before, last)

    dq, to_up, state = gradients([opposite], None)
    spot, dq, to_up = tied((spot, dq, to_up))
    up = turned(to_up, 1)
    dq, to_down = gradients([below[3]], dq)
    spot, dq, to_down = tied((spot, dq, to_down))
    down = turned(to_down, -1)
    dq, up_grad = gradients([above[3]], dq)
    dq, up_grad, up = tied((dq, up_grad, up))
    to_up = plus(up_grad, up)
    for k in (2, 1, 0):
        if k == 2:
            spot, dq, to_up = tied((spot, dq, to_up))
        else:
            spot, dq, to_up, to_down = tied((spot, dq, to_up, to_down))
            down = turned(to_down, -1)
        up = turned(to_up, 1)
        if k:
            dq, up_grad, down_grad = gradients([above[k], below[k]], dq)
            dq, up_grad, down_grad, up, down = tied((dq, up_grad, down_grad, up, down))
            to_up, to_down = plus(up_grad, up), plus(down_grad, down)
    dq, own_grad = gradients([own], dq, True)
    dq, own_grad, up, down = tied((dq, own_grad, up, down))
    dkv_own = plus(own_grad, up, down)

    flip = dkv_own.reshape((2, 2) + dkv_own.shape[1:])
    flip = jnp.where(across == 1, flip[::-1], flip)
    flip = jnp.where(pair == 1, flip[:, ::-1], flip)

    heads = KEY_VALUE_HEADS
    out_rows = row_count // heads
    split = GROUP * HEAD_SIZE
    leaving = dq.at[:, :, split:].set(flip.reshape(dkv_own.shape)).reshape(window_count * heads, out_rows, split + 2 * HEAD_SIZE)
    final = lax.all_to_all(leaving, FINAL, 0, 0, tiled=True)

    def merged(array):
        width = array.shape[-1]
        return array.reshape(window_count, heads, out_rows, width).transpose(0, 2, 1, 3).reshape(window_count, out_rows, heads * width)

    return (
        merged(final[..., 0:split]),
        merged(final[..., split:split + HEAD_SIZE]),
        merged(final[..., split + HEAD_SIZE:]),
    )


def solution(mesh):
    fine = Mesh(mesh.devices.reshape(2, RING, 2, 4, 2), ("xh", "z", "core", "y", "xl"))
    ctx, head = ("xh", "z", "core"), ("y", "xl")
    vectors = P(None, ctx, head)
    out = P(None, ctx + head, None)
    return jax.shard_map(
        on_device,
        mesh=fine,
        in_specs=(vectors, vectors, vectors, vectors, P(None, ctx), P(None, ctx)),
        out_specs=(out, out, out),
        check_vma=False,
    )
```

```python
import functools
import math

import jax
import jax.numpy as jnp
from jax import lax
from jax.experimental import pallas as pl
from jax.experimental.pallas import tpu as pltpu
from jax.sharding import Mesh, PartitionSpec as P

QUERY_HEADS = 64
KEY_VALUE_HEADS = 8
HEAD_SIZE = 128
GROUP = QUERY_HEADS // KEY_VALUE_HEADS
NEG_BIG = -1e30
CODE_SPAN = 2048
META_ROWS = 16
HEADS_PER_STEP = 4
SCALE = 1.0 / math.sqrt(HEAD_SIZE)
EXP2_SCALE = SCALE * math.log2(math.e)

NT = (((1,), (1,)), ((), ()))
NN = (((1,), (0,)), ((), ()))


def dot(a, b, dims):
    return lax.dot_general(a, b, dims, preferred_element_type=jnp.float32)


def key_spans(piece_refs):
    spans, start = [], 0
    for ref in piece_refs:
        size = ref.shape[0] - META_ROWS
        spans.append((ref, slice(start, start + size), size))
        start += size
    return spans, start


def keys_of(ref, size):
    return ref[0:size, 0:HEAD_SIZE]


def values_of(ref, size):
    return ref[0:size, HEAD_SIZE:2 * HEAD_SIZE]


def fill_bias(bias_ref, spans, low_ref, high_ref, row_count):
    rows = low_ref.shape[1]
    for ref, part, size in spans:
        digits = ref[size:size + META_ROWS, :].astype(jnp.float32)
        codes = digits[:, 0:128] * 128.0 + digits[:, 128:256]
        for b in range(size // row_count):
            column = jnp.broadcast_to(codes[b:b + 1, :], (128, 128)).T[0:row_count, :]
            begin = part.start + b * row_count
            for r in range(rows // 128):
                low = low_ref[:, r * 128:(r + 1) * 128]
                high = high_ref[:, r * 128:(r + 1) * 128]
                allowed = (column >= low) & (column <= high)
                bias_ref[begin:begin + row_count, r * 128:(r + 1) * 128] = jnp.where(allowed, 0.0, NEG_BIG)


def rows_of(row_refs, lanes, row_count):
    q = jnp.concatenate([ref[0:row_count, lanes] for ref in row_refs], axis=0)
    do = jnp.concatenate([ref[row_count:2 * row_count, lanes] for ref in row_refs], axis=0)
    return q, do


def absorbed(top, total, cross, scores, softmax_grads):
    rows = top.shape[1]
    new = top
    for s in scores:
        peak = jnp.max(s.reshape(s.shape[0] // 8, 8, rows), axis=0)
        new = jnp.maximum(new, jnp.max(peak, axis=0, keepdims=True))
    factor = jnp.exp2(top - new)
    total, cross = total * factor, cross * factor
    weights = [jnp.exp2(s - new) for s in scores]
    for p, dp in zip(weights, softmax_grads):
        part_sum = jnp.sum(p.reshape(p.shape[0] // 8, 8, rows), axis=0)
        part_dot = jnp.sum((p * dp).reshape(p.shape[0] // 8, 8, rows), axis=0)
        total = total + jnp.sum(part_sum, axis=0, keepdims=True)
        cross = cross + jnp.sum(part_dot, axis=0, keepdims=True)
    return new, total, cross, weights


def stats_kernel(first, count, low_ref, high_ref, *refs):
    row_refs, piece_refs, rest = refs[0:4], refs[4:4 + count], refs[4 + count:]
    state_ref, bias_ref = rest[-2:]
    rows = low_ref.shape[1]
    row_count = rows // 4
    spans, _ = key_spans(piece_refs)
    fill_bias(bias_ref, spans, low_ref, high_ref, row_count)

    def step(g, carry):
        for j in range(HEADS_PER_STEP):
            h = g * HEADS_PER_STEP + j
            lanes = pl.ds(pl.multiple_of(h * HEAD_SIZE, HEAD_SIZE), HEAD_SIZE)
            q, do = rows_of(row_refs, lanes, row_count)
            if first:
                top = jnp.full((1, rows), NEG_BIG, jnp.float32)
                total = jnp.zeros((1, rows), jnp.float32)
                cross = jnp.zeros((1, rows), jnp.float32)
            else:
                top, total, cross = rest[0][h, 0:1, :], rest[0][h, 1:2, :], rest[0][h, 2:3, :]
            for ref, part, size in spans:
                s = dot(keys_of(ref, size), q, NT) * EXP2_SCALE + bias_ref[part, :]
                dp = dot(values_of(ref, size), do, NT)
                top, total, cross = absorbed(top, total, cross, [s], [dp])[0:3]
            state_ref[h, 0:1, :] = top
            state_ref[h, 1:2, :] = total
            state_ref[h, 2:3, :] = cross
        return carry

    lax.fori_loop(0, GROUP // HEADS_PER_STEP, step, 0)


def grads_kernel(first, last, count, place_ref, low_ref, high_ref, state_ref, *refs):
    row_refs, piece_refs, rest = refs[0:4], refs[4:4 + count], refs[4 + count:]
    if not first:
        before_ref, rest = rest[0], rest[1:]
    dq_ref, out_refs, rest = rest[0], rest[1:1 + count], rest[1 + count:]
    if first:
        final_ref, rest = rest[0], rest[1:]
    bias_ref, kt_ref, ds_ref, acc_ref = rest
    rows = low_ref.shape[1]
    row_count = rows // 4
    heads = HEADS_PER_STEP
    spans, keys = key_spans(piece_refs)
    fill_bias(bias_ref, spans, low_ref, high_ref, row_count)
    for ref, part, size in spans:
        kt_ref[:, part] = keys_of(ref, size).T
    acc_ref[...] = jnp.zeros_like(acc_ref)
    place = place_ref[0]

    def step(g, carry):
        q, do, lanes, p_low, ds_low = [], [], [], [], []
        for j in range(heads):
            h = g * heads + j
            lanes.append(pl.ds(pl.multiple_of(h * HEAD_SIZE, HEAD_SIZE), HEAD_SIZE))
            one_q, one_do = rows_of(row_refs, lanes[j], row_count)
            q.append(one_q)
            do.append(one_do)

            def products(ref, part, size):
                s = dot(keys_of(ref, size), one_q, NT) * EXP2_SCALE + bias_ref[part, :]
                return s, dot(values_of(ref, size), one_do, NT)

            if first:
                pairs = [products(*span) for span in spans]
                top, total, cross, weights = absorbed(
                    state_ref[h, 0:1, :], state_ref[h, 1:2, :], state_ref[h, 2:3, :],
                    [s for s, _ in pairs], [dp for _, dp in pairs])
                inverse = 1.0 / total
                delta = cross * inverse
                final_ref[h, 0:1, :] = top + jnp.log2(total)
                final_ref[h, 1:2, :] = delta
                softmax = [p * inverse for p in weights]
                softmax_grads = [dp for _, dp in pairs]
            else:
                offset, delta = state_ref[h, 0:1, :], state_ref[h, 1:2, :]
                softmax, softmax_grads = [], []
                for span in spans:
                    s, dp = products(*span)
                    softmax.append(jnp.exp2(s - offset))
                    softmax_grads.append(dp)
            p_low.append([p.astype(jnp.bfloat16) for p in softmax])
            ds_low.append([(p * (dp - delta)).astype(jnp.bfloat16) for p, dp in zip(softmax, softmax_grads)])
        q_all, do_all = jnp.concatenate(q, axis=0), jnp.concatenate(do, axis=0)
        for i, (ref, part, size) in enumerate(spans):
            p_all = jnp.concatenate([p_low[j][i] for j in range(heads)], axis=1)
            ds_all = jnp.concatenate([ds_low[j][i] for j in range(heads)], axis=1)
            ds_ref[part, :] = ds_all
            acc_ref[part, HEAD_SIZE:2 * HEAD_SIZE] += dot(p_all, do_all, NN)
            acc_ref[part, 0:HEAD_SIZE] += dot(ds_all, q_all, NN)
        dqt = dot(kt_ref[...], ds_ref[...], NN)
        for j in range(heads):
            part = dqt[:, j * rows:(j + 1) * rows]
            if not first:
                part = part + before_ref[g * heads + j]
            if last:
                dq = (part * SCALE).T.astype(jnp.bfloat16)
                for r in range(4):
                    dq_ref[place ^ r, :, lanes[j]] = dq[r * row_count:(r + 1) * row_count, :]
            else:
                dq_ref[g * heads + j] = part
        return carry

    lax.fori_loop(0, GROUP // heads, step, 0)
    for out_ref, (_, part, size) in zip(out_refs, spans):
        shape = (size // row_count, row_count, HEAD_SIZE)
        out_ref[:, :, 0:HEAD_SIZE] = (acc_ref[part, 0:HEAD_SIZE] * SCALE).astype(jnp.bfloat16).reshape(shape)
        out_ref[:, :, HEAD_SIZE:2 * HEAD_SIZE] = acc_ref[part, HEAD_SIZE:2 * HEAD_SIZE].astype(jnp.bfloat16).reshape(shape)


VMEM = pl.BlockSpec(memory_space=pltpu.VMEM)
SMEM = pl.BlockSpec(memory_space=pltpu.SMEM)
ANY = pl.BlockSpec(memory_space=pltpu.HBM)


def stats(low, high, row_arrays, pieces, state):
    rows = low.shape[1]
    keys = sum(piece.shape[0] - META_ROWS for piece in pieces)
    first = state is None
    inputs = (low, high, *row_arrays, *pieces) + (() if first else (state,))
    return pl.pallas_call(
        functools.partial(stats_kernel, first, len(pieces)),
        out_shape=jax.ShapeDtypeStruct((GROUP, 8, rows), jnp.float32),
        in_specs=[VMEM] * len(inputs),
        out_specs=VMEM,
        scratch_shapes=[pltpu.VMEM((keys, rows), jnp.float32)],
        compiler_params=pltpu.CompilerParams(vmem_limit_bytes=32 * 1024 * 1024),
        cost_estimate=pl.CostEstimate(
            flops=8 * keys * rows * HEAD_SIZE * GROUP, bytes_accessed=1024 * 1024,
            transcendentals=keys * rows * GROUP),
    )(*inputs)


def grads(place, low, high, state, row_arrays, pieces, before, last):
    rows = low.shape[1]
    row_count = rows // 4
    keys = sum(piece.shape[0] - META_ROWS for piece in pieces)
    width = 2 * HEAD_SIZE
    first = before is None
    inputs = (low, high, state, *row_arrays, *pieces) + (() if first else (before,))
    parts = tuple(jax.ShapeDtypeStruct((4, row_count, width), jnp.bfloat16) for piece in pieces)
    extra = (jax.ShapeDtypeStruct((GROUP, 8, rows), jnp.float32),) if first else ()
    if last:
        dq = jax.ShapeDtypeStruct((4, row_count, GROUP * HEAD_SIZE + width), jnp.bfloat16)
    else:
        dq = jax.ShapeDtypeStruct((GROUP, HEAD_SIZE, rows), jnp.float32)
    return pl.pallas_call(
        functools.partial(grads_kernel, first, last, len(pieces)),
        out_shape=(dq,) + parts + extra,
        in_specs=[SMEM] + [VMEM] * len(inputs),
        out_specs=(VMEM,) * (1 + len(parts) + len(extra)),
        scratch_shapes=[
            pltpu.VMEM((keys, rows), jnp.float32),
            pltpu.VMEM((HEAD_SIZE, keys), jnp.bfloat16),
            pltpu.VMEM((keys, HEADS_PER_STEP * rows), jnp.bfloat16),
            pltpu.VMEM((keys, width), jnp.float32),
        ],
        compiler_params=pltpu.CompilerParams(vmem_limit_bytes=32 * 1024 * 1024),
        cost_estimate=pl.CostEstimate(
            flops=16 * keys * rows * HEAD_SIZE * GROUP, bytes_accessed=2 * 1024 * 1024,
            transcendentals=keys * rows * GROUP),
    )(place, *inputs)


def copies(pairs, sems):
    started = [pltpu.make_async_copy(source, target, sems.at[i]) for i, (source, target) in enumerate(pairs)]
    for copy in started:
        copy.start()
    for copy in started:
        copy.wait()


def pack_keys_kernel(place_ref, code_ref, k_ref, v_ref, self_ref, pair_ref, across_ref, sems):
    row_count = k_ref.shape[1]
    place = place_ref[0]
    targets = ((0, self_ref), (1, pair_ref.at[0]), (3, pair_ref.at[1]), (2, across_ref))
    pairs = []
    for r, target in targets:
        pairs.append((k_ref.at[place ^ r], target.at[0:row_count, 0:HEAD_SIZE]))
        pairs.append((v_ref.at[place ^ r], target.at[0:row_count, HEAD_SIZE:2 * HEAD_SIZE]))
    for r, target in targets:
        code = code_ref[pl.ds(place ^ r, 1), :]
        for i, digit in enumerate((code >> 7, code & 127)):
            spread = jnp.broadcast_to(digit.astype(jnp.float32), (META_ROWS, 128)).astype(jnp.bfloat16)
            target[row_count:row_count + META_ROWS, i * 128:(i + 1) * 128] = spread
    copies(pairs, sems)


def pack_rows_kernel(place_ref, q_ref, do_ref, *refs):
    out_refs, sems = refs[0:4], refs[4]
    row_count = q_ref.shape[1]
    place = place_ref[0]
    pairs = []
    for r, target in enumerate(out_refs):
        pairs.append((q_ref.at[place ^ r], target.at[0:row_count]))
        pairs.append((do_ref.at[place ^ r], target.at[row_count:2 * row_count]))
    copies(pairs, sems)


def own_kernel(self_ref, pair_ref, across_ref, own_ref, low_ref, high_ref):
    row_count = self_ref.shape[0] - META_ROWS
    line = lax.broadcasted_iota(jnp.int32, (META_ROWS, 2 * HEAD_SIZE), 0)
    meta = jnp.zeros((META_ROWS, 2 * HEAD_SIZE), jnp.float32)
    codes = []
    for r, value in enumerate((self_ref[...], pair_ref[0], across_ref[0], across_ref[1])):
        own_ref[r * row_count:(r + 1) * row_count, :] = value[0:row_count, :]
        digits = value[row_count:, :].astype(jnp.float32)
        meta = jnp.where(line == r, digits, meta)
        codes.append(digits[0:8, 0:128] * 128.0 + digits[0:8, 128:256])
    own_ref[4 * row_count:, :] = meta.astype(jnp.bfloat16)
    lane = lax.broadcasted_iota(jnp.int32, (8, 128), 1)
    for i in range(2):
        code = jnp.where(lane < row_count, codes[2 * i], pltpu.roll(codes[2 * i + 1], row_count, 1))[0:1, :]
        high_ref[:, i * 128:(i + 1) * 128] = code
        low_ref[:, i * 128:(i + 1) * 128] = jnp.floor(code * (1.0 / CODE_SPAN)) * CODE_SPAN


def pack_keys(place, code, key_vectors, value_vectors):
    lines = key_vectors.shape[1] + META_ROWS
    one = jax.ShapeDtypeStruct((lines, 2 * HEAD_SIZE), jnp.bfloat16)
    two = jax.ShapeDtypeStruct((2, lines, 2 * HEAD_SIZE), jnp.bfloat16)
    return pl.pallas_call(
        pack_keys_kernel,
        out_shape=(one, two, one),
        in_specs=[SMEM, VMEM, ANY, ANY],
        out_specs=(VMEM,) * 3,
        scratch_shapes=[pltpu.SemaphoreType.DMA((8,))],
        compiler_params=pltpu.CompilerParams(vmem_limit_bytes=32 * 1024 * 1024),
    )(place, code, key_vectors, value_vectors)


def pack_rows(place, queries, output_gradient):
    row_count, wide = queries.shape[1:]
    return pl.pallas_call(
        pack_rows_kernel,
        out_shape=(jax.ShapeDtypeStruct((2 * row_count, wide), jnp.bfloat16),) * 4,
        in_specs=[SMEM, ANY, ANY],
        out_specs=(VMEM,) * 4,
        scratch_shapes=[pltpu.SemaphoreType.DMA((8,))],
        compiler_params=pltpu.CompilerParams(vmem_limit_bytes=32 * 1024 * 1024),
    )(place, queries, output_gradient)


def own_keys(mine, paired, crossed):
    rows = 4 * (mine.shape[0] - META_ROWS)
    row = jax.ShapeDtypeStruct((1, rows), jnp.float32)
    own = jax.ShapeDtypeStruct((rows + META_ROWS, mine.shape[1]), jnp.bfloat16)
    return pl.pallas_call(
        own_kernel,
        out_shape=(own, row, row),
        in_specs=[VMEM] * 3,
        out_specs=(VMEM,) * 3,
        compiler_params=pltpu.CompilerParams(vmem_limit_bytes=32 * 1024 * 1024),
    )(mine, paired, crossed)


PLANE = ("xh", "core")
FINAL = ("xh", "core", "y", "xl")
RING = 8


def swapped(array, axes, by, count):
    return lax.ppermute(array, axes, [(i, i ^ by) for i in range(count)])


def turned(array, by):
    return lax.ppermute(array, "z", [(i, (i + by) % RING) for i in range(RING)])


def plus(*arrays):
    return sum(a.astype(jnp.float32) for a in arrays).astype(jnp.bfloat16)


def on_device(queries, key_vectors, value_vectors, output_gradient, positions, segments):
    window_count, row_count, _ = queries.shape
    across, pair = lax.axis_index("xh"), lax.axis_index("core")
    place = across * 2 + pair

    spot = place.reshape(1).astype(jnp.int32)
    code = jnp.pad(segments * CODE_SPAN + positions, ((0, 0), (0, 128 - row_count)))
    tied = lax.optimization_barrier
    mine, to_pair, across_part = pack_keys(spot, code, key_vectors, value_vectors)
    paired = swapped(to_pair, PLANE, 1, 4)
    spot, to_pair = tied((spot, to_pair))
    loads = pack_rows(spot, queries, output_gradient)
    crossed = swapped(jnp.stack([across_part, paired[1]]), PLANE, 2, 4)
    crossed, far_rows = tied((crossed, loads[2:4]))
    row_arrays = [loads[0], swapped(loads[1], PLANE, 1, 4)] + [swapped(far_rows[r - 2], PLANE, r, 4) for r in (2, 3)]
    own, low, high = own_keys(mine, paired, crossed)

    below, above = [own], [own]
    for _ in range(2):
        below.append(turned(below[-1], 1))
        above.append(turned(above[-1], -1))
    below.append(turned(below[2], 1))
    above.append(turned(above[2], -1))
    opposite = turned(own, RING // 2)
    state = stats(low, high, row_arrays, [own, below[1], above[1], below[2], above[2]], None)
    state, below[3], above[3] = tied((state, below[3], above[3]))
    state = stats(low, high, row_arrays, [below[3], above[3]], state)
    state, opposite = tied((state, opposite))

    def gradients(pieces, before, last=False):
        return grads(spot, low, high, state, row_arrays, pieces, before, last)

    dq, far_grad, state = gradients([opposite], None)
    crossing = turned(far_grad, RING // 2)
    dq, to_up, to_down = gradients([above[3], below[3]], dq)
    for k in (2, 1, 0):
        spot, dq, to_up, to_down = tied((spot, dq, to_up, to_down))
        up, down = turned(to_up, 1), turned(to_down, -1)
        if k:
            dq, up_grad, down_grad = gradients([above[k], below[k]], dq)
            if k == 1:
                crossing, dq = tied((crossing, dq))
            dq, up_grad, down_grad, up, down = tied((dq, up_grad, down_grad, up, down))
            to_up, to_down = plus(up_grad, up), plus(down_grad, down)
    dq, own_grad = gradients([own], dq, True)
    dq, own_grad, up, down = tied((dq, own_grad, up, down))
    dkv_own = plus(own_grad, up, down, crossing)

    flip = dkv_own.reshape((2, 2) + dkv_own.shape[1:])
    flip = jnp.where(across == 1, flip[::-1], flip)
    flip = jnp.where(pair == 1, flip[:, ::-1], flip)

    heads = KEY_VALUE_HEADS
    out_rows = row_count // heads
    split = GROUP * HEAD_SIZE
    leaving = dq.at[:, :, split:].set(flip.reshape(dkv_own.shape)).reshape(window_count * heads, out_rows, split + 2 * HEAD_SIZE)
    final = lax.all_to_all(leaving, FINAL, 0, 0, tiled=True)

    def merged(array):
        width = array.shape[-1]
        return array.reshape(window_count, heads, out_rows, width).transpose(0, 2, 1, 3).reshape(window_count, out_rows, heads * width)

    return (
        merged(final[..., 0:split]),
        merged(final[..., split:split + HEAD_SIZE]),
        merged(final[..., split + HEAD_SIZE:]),
    )


def solution(mesh):
    fine = Mesh(mesh.devices.reshape(2, RING, 2, 4, 2), ("xh", "z", "core", "y", "xl"))
    ctx, head = ("xh", "z", "core"), ("y", "xl")
    vectors = P(None, ctx, head)
    out = P(None, ctx + head, None)
    return jax.shard_map(
        on_device,
        mesh=fine,
        in_specs=(vectors, vectors, vectors, vectors, P(None, ctx), P(None, ctx)),
        out_specs=(out, out, out),
        check_vma=False,
    )
```

```python
import functools
import math

import jax
import jax.numpy as jnp
from jax import lax
from jax.experimental import pallas as pl
from jax.experimental.pallas import tpu as pltpu
from jax.sharding import Mesh, PartitionSpec as P

QUERY_HEADS = 64
KEY_VALUE_HEADS = 8
HEAD_SIZE = 128
GROUP = QUERY_HEADS // KEY_VALUE_HEADS
NEG_BIG = -1e30
CODE_SPAN = 2048
META_ROWS = 16
HEADS_PER_STEP = 4
SCALE = 1.0 / math.sqrt(HEAD_SIZE)
EXP2_SCALE = SCALE * math.log2(math.e)

NT = (((1,), (1,)), ((), ()))
NN = (((1,), (0,)), ((), ()))


def dot(a, b, dims):
    return lax.dot_general(a, b, dims, preferred_element_type=jnp.float32)


def key_spans(piece_refs):
    spans, start = [], 0
    for ref in piece_refs:
        size = ref.shape[0] - META_ROWS
        spans.append((ref, slice(start, start + size), size))
        start += size
    return spans, start


def keys_of(ref, size):
    return ref[0:size, 0:HEAD_SIZE]


def values_of(ref, size):
    return ref[0:size, HEAD_SIZE:2 * HEAD_SIZE]


def fill_bias(bias_ref, spans, low_ref, high_ref, row_count):
    rows = low_ref.shape[1]
    for ref, part, size in spans:
        digits = ref[size:size + META_ROWS, :].astype(jnp.float32)
        codes = digits[:, 0:128] * 128.0 + digits[:, 128:256]
        for b in range(size // row_count):
            column = jnp.broadcast_to(codes[b:b + 1, :], (128, 128)).T[0:row_count, :]
            begin = part.start + b * row_count
            for r in range(rows // 128):
                low = low_ref[:, r * 128:(r + 1) * 128]
                high = high_ref[:, r * 128:(r + 1) * 128]
                allowed = (column >= low) & (column <= high)
                bias_ref[begin:begin + row_count, r * 128:(r + 1) * 128] = jnp.where(allowed, 0.0, NEG_BIG)


def rows_of(row_refs, lanes, row_count):
    q = jnp.concatenate([ref[0:row_count, lanes] for ref in row_refs], axis=0)
    do = jnp.concatenate([ref[row_count:2 * row_count, lanes] for ref in row_refs], axis=0)
    return q, do


def absorbed(top, total, cross, scores, softmax_grads):
    rows = top.shape[1]
    new = top
    for s in scores:
        peak = jnp.max(s.reshape(s.shape[0] // 8, 8, rows), axis=0)
        new = jnp.maximum(new, jnp.max(peak, axis=0, keepdims=True))
    factor = jnp.exp2(top - new)
    total, cross = total * factor, cross * factor
    weights = [jnp.exp2(s - new) for s in scores]
    for p, dp in zip(weights, softmax_grads):
        part_sum = jnp.sum(p.reshape(p.shape[0] // 8, 8, rows), axis=0)
        part_dot = jnp.sum((p * dp).reshape(p.shape[0] // 8, 8, rows), axis=0)
        total = total + jnp.sum(part_sum, axis=0, keepdims=True)
        cross = cross + jnp.sum(part_dot, axis=0, keepdims=True)
    return new, total, cross, weights


def stats_kernel(first, count, low_ref, high_ref, *refs):
    row_refs, piece_refs, rest = refs[0:4], refs[4:4 + count], refs[4 + count:]
    state_ref, bias_ref = rest[-2:]
    rows = low_ref.shape[1]
    row_count = rows // 4
    spans, _ = key_spans(piece_refs)
    fill_bias(bias_ref, spans, low_ref, high_ref, row_count)

    def step(g, carry):
        for j in range(HEADS_PER_STEP):
            h = g * HEADS_PER_STEP + j
            lanes = pl.ds(pl.multiple_of(h * HEAD_SIZE, HEAD_SIZE), HEAD_SIZE)
            q, do = rows_of(row_refs, lanes, row_count)
            if first:
                top = jnp.full((1, rows), NEG_BIG, jnp.float32)
                total = jnp.zeros((1, rows), jnp.float32)
                cross = jnp.zeros((1, rows), jnp.float32)
            else:
                top, total, cross = rest[0][h, 0:1, :], rest[0][h, 1:2, :], rest[0][h, 2:3, :]
            for ref, part, size in spans:
                s = dot(keys_of(ref, size), q, NT) * EXP2_SCALE + bias_ref[part, :]
                dp = dot(values_of(ref, size), do, NT)
                top, total, cross = absorbed(top, total, cross, [s], [dp])[0:3]
            state_ref[h, 0:1, :] = top
            state_ref[h, 1:2, :] = total
            state_ref[h, 2:3, :] = cross
        return carry

    lax.fori_loop(0, GROUP // HEADS_PER_STEP, step, 0)


def grads_kernel(first, last, count, place_ref, low_ref, high_ref, state_ref, *refs):
    row_refs, piece_refs, rest = refs[0:4], refs[4:4 + count], refs[4 + count:]
    if not first:
        before_ref, rest = rest[0], rest[1:]
    dq_ref, out_refs, rest = rest[0], rest[1:1 + count], rest[1 + count:]
    if first:
        final_ref, rest = rest[0], rest[1:]
    bias_ref, kt_ref, ds_ref, acc_ref = rest
    rows = low_ref.shape[1]
    row_count = rows // 4
    heads = HEADS_PER_STEP
    spans, keys = key_spans(piece_refs)
    fill_bias(bias_ref, spans, low_ref, high_ref, row_count)
    for ref, part, size in spans:
        kt_ref[:, part] = keys_of(ref, size).T
    acc_ref[...] = jnp.zeros_like(acc_ref)
    place = place_ref[0]

    def step(g, carry):
        q, do, lanes, p_low, ds_low = [], [], [], [], []
        for j in range(heads):
            h = g * heads + j
            lanes.append(pl.ds(pl.multiple_of(h * HEAD_SIZE, HEAD_SIZE), HEAD_SIZE))
            one_q, one_do = rows_of(row_refs, lanes[j], row_count)
            q.append(one_q)
            do.append(one_do)

            def products(ref, part, size):
                s = dot(keys_of(ref, size), one_q, NT) * EXP2_SCALE + bias_ref[part, :]
                return s, dot(values_of(ref, size), one_do, NT)

            if first:
                pairs = [products(*span) for span in spans]
                top, total, cross, weights = absorbed(
                    state_ref[h, 0:1, :], state_ref[h, 1:2, :], state_ref[h, 2:3, :],
                    [s for s, _ in pairs], [dp for _, dp in pairs])
                inverse = 1.0 / total
                delta = cross * inverse
                final_ref[h, 0:1, :] = top + jnp.log2(total)
                final_ref[h, 1:2, :] = delta
                softmax = [p * inverse for p in weights]
                softmax_grads = [dp for _, dp in pairs]
            else:
                offset, delta = state_ref[h, 0:1, :], state_ref[h, 1:2, :]
                softmax, softmax_grads = [], []
                for span in spans:
                    s, dp = products(*span)
                    softmax.append(jnp.exp2(s - offset))
                    softmax_grads.append(dp)
            p_low.append([p.astype(jnp.bfloat16) for p in softmax])
            ds_low.append([(p * (dp - delta)).astype(jnp.bfloat16) for p, dp in zip(softmax, softmax_grads)])
        q_all, do_all = jnp.concatenate(q, axis=0), jnp.concatenate(do, axis=0)
        for i, (ref, part, size) in enumerate(spans):
            p_all = jnp.concatenate([p_low[j][i] for j in range(heads)], axis=1)
            ds_all = jnp.concatenate([ds_low[j][i] for j in range(heads)], axis=1)
            ds_ref[part, :] = ds_all
            acc_ref[part, HEAD_SIZE:2 * HEAD_SIZE] += dot(p_all, do_all, NN)
            acc_ref[part, 0:HEAD_SIZE] += dot(ds_all, q_all, NN)
        dqt = dot(kt_ref[...], ds_ref[...], NN)
        for j in range(heads):
            part = dqt[:, j * rows:(j + 1) * rows]
            if not first:
                part = part + before_ref[g * heads + j]
            if last:
                dq = (part * SCALE).T.astype(jnp.bfloat16)
                for r in range(4):
                    dq_ref[place ^ r, :, lanes[j]] = dq[r * row_count:(r + 1) * row_count, :]
            else:
                dq_ref[g * heads + j] = part
        return carry

    lax.fori_loop(0, GROUP // heads, step, 0)
    for out_ref, (_, part, size) in zip(out_refs, spans):
        shape = (size // row_count, row_count, HEAD_SIZE)
        out_ref[:, :, 0:HEAD_SIZE] = (acc_ref[part, 0:HEAD_SIZE] * SCALE).astype(jnp.bfloat16).reshape(shape)
        out_ref[:, :, HEAD_SIZE:2 * HEAD_SIZE] = acc_ref[part, HEAD_SIZE:2 * HEAD_SIZE].astype(jnp.bfloat16).reshape(shape)


VMEM = pl.BlockSpec(memory_space=pltpu.VMEM)
SMEM = pl.BlockSpec(memory_space=pltpu.SMEM)
ANY = pl.BlockSpec(memory_space=pltpu.HBM)


def stats(low, high, row_arrays, pieces, state):
    rows = low.shape[1]
    keys = sum(piece.shape[0] - META_ROWS for piece in pieces)
    first = state is None
    inputs = (low, high, *row_arrays, *pieces) + (() if first else (state,))
    return pl.pallas_call(
        functools.partial(stats_kernel, first, len(pieces)),
        out_shape=jax.ShapeDtypeStruct((GROUP, 8, rows), jnp.float32),
        in_specs=[VMEM] * len(inputs),
        out_specs=VMEM,
        scratch_shapes=[pltpu.VMEM((keys, rows), jnp.float32)],
        compiler_params=pltpu.CompilerParams(vmem_limit_bytes=32 * 1024 * 1024),
        cost_estimate=pl.CostEstimate(
            flops=8 * keys * rows * HEAD_SIZE * GROUP, bytes_accessed=1024 * 1024,
            transcendentals=keys * rows * GROUP),
    )(*inputs)


def grads(place, low, high, state, row_arrays, pieces, before, last):
    rows = low.shape[1]
    row_count = rows // 4
    keys = sum(piece.shape[0] - META_ROWS for piece in pieces)
    width = 2 * HEAD_SIZE
    first = before is None
    inputs = (low, high, state, *row_arrays, *pieces) + (() if first else (before,))
    parts = tuple(jax.ShapeDtypeStruct((4, row_count, width), jnp.bfloat16) for piece in pieces)
    extra = (jax.ShapeDtypeStruct((GROUP, 8, rows), jnp.float32),) if first else ()
    if last:
        dq = jax.ShapeDtypeStruct((4, row_count, GROUP * HEAD_SIZE + width), jnp.bfloat16)
    else:
        dq = jax.ShapeDtypeStruct((GROUP, HEAD_SIZE, rows), jnp.float32)
    return pl.pallas_call(
        functools.partial(grads_kernel, first, last, len(pieces)),
        out_shape=(dq,) + parts + extra,
        in_specs=[SMEM] + [VMEM] * len(inputs),
        out_specs=(VMEM,) * (1 + len(parts) + len(extra)),
        scratch_shapes=[
            pltpu.VMEM((keys, rows), jnp.float32),
            pltpu.VMEM((HEAD_SIZE, keys), jnp.bfloat16),
            pltpu.VMEM((keys, HEADS_PER_STEP * rows), jnp.bfloat16),
            pltpu.VMEM((keys, width), jnp.float32),
        ],
        compiler_params=pltpu.CompilerParams(vmem_limit_bytes=32 * 1024 * 1024),
        cost_estimate=pl.CostEstimate(
            flops=16 * keys * rows * HEAD_SIZE * GROUP, bytes_accessed=2 * 1024 * 1024,
            transcendentals=keys * rows * GROUP),
    )(place, *inputs)


def copies(pairs, sems):
    started = [pltpu.make_async_copy(source, target, sems.at[i]) for i, (source, target) in enumerate(pairs)]
    for copy in started:
        copy.start()
    for copy in started:
        copy.wait()


def pack_keys_kernel(place_ref, code_ref, k_ref, v_ref, self_ref, pair_ref, across_ref, sems):
    row_count = k_ref.shape[1]
    place = place_ref[0]
    targets = ((0, self_ref), (1, pair_ref.at[0]), (3, pair_ref.at[1]), (2, across_ref))
    pairs = []
    for r, target in targets:
        pairs.append((k_ref.at[place ^ r], target.at[0:row_count, 0:HEAD_SIZE]))
        pairs.append((v_ref.at[place ^ r], target.at[0:row_count, HEAD_SIZE:2 * HEAD_SIZE]))
    for r, target in targets:
        code = code_ref[pl.ds(place ^ r, 1), :]
        for i, digit in enumerate((code >> 7, code & 127)):
            spread = jnp.broadcast_to(digit.astype(jnp.float32), (META_ROWS, 128)).astype(jnp.bfloat16)
            target[row_count:row_count + META_ROWS, i * 128:(i + 1) * 128] = spread
    copies(pairs, sems)


def pack_rows_kernel(place_ref, q_ref, do_ref, *refs):
    out_refs, sems = refs[0:4], refs[4]
    row_count = q_ref.shape[1]
    place = place_ref[0]
    pairs = []
    for r, target in enumerate(out_refs):
        pairs.append((q_ref.at[place ^ r], target.at[0:row_count]))
        pairs.append((do_ref.at[place ^ r], target.at[row_count:2 * row_count]))
    copies(pairs, sems)


def own_kernel(self_ref, pair_ref, across_ref, own_ref, low_ref, high_ref):
    row_count = self_ref.shape[0] - META_ROWS
    line = lax.broadcasted_iota(jnp.int32, (META_ROWS, 2 * HEAD_SIZE), 0)
    meta = jnp.zeros((META_ROWS, 2 * HEAD_SIZE), jnp.float32)
    codes = []
    for r, value in enumerate((self_ref[...], pair_ref[0], across_ref[0], across_ref[1])):
        own_ref[r * row_count:(r + 1) * row_count, :] = value[0:row_count, :]
        digits = value[row_count:, :].astype(jnp.float32)
        meta = jnp.where(line == r, digits, meta)
        codes.append(digits[0:8, 0:128] * 128.0 + digits[0:8, 128:256])
    own_ref[4 * row_count:, :] = meta.astype(jnp.bfloat16)
    lane = lax.broadcasted_iota(jnp.int32, (8, 128), 1)
    for i in range(2):
        code = jnp.where(lane < row_count, codes[2 * i], pltpu.roll(codes[2 * i + 1], row_count, 1))[0:1, :]
        high_ref[:, i * 128:(i + 1) * 128] = code
        low_ref[:, i * 128:(i + 1) * 128] = jnp.floor(code * (1.0 / CODE_SPAN)) * CODE_SPAN


def pack_keys(place, code, key_vectors, value_vectors):
    lines = key_vectors.shape[1] + META_ROWS
    one = jax.ShapeDtypeStruct((lines, 2 * HEAD_SIZE), jnp.bfloat16)
    two = jax.ShapeDtypeStruct((2, lines, 2 * HEAD_SIZE), jnp.bfloat16)
    return pl.pallas_call(
        pack_keys_kernel,
        out_shape=(one, two, one),
        in_specs=[SMEM, VMEM, ANY, ANY],
        out_specs=(VMEM,) * 3,
        scratch_shapes=[pltpu.SemaphoreType.DMA((8,))],
        compiler_params=pltpu.CompilerParams(vmem_limit_bytes=32 * 1024 * 1024),
    )(place, code, key_vectors, value_vectors)


def pack_rows(place, queries, output_gradient):
    row_count, wide = queries.shape[1:]
    return pl.pallas_call(
        pack_rows_kernel,
        out_shape=(jax.ShapeDtypeStruct((2 * row_count, wide), jnp.bfloat16),) * 4,
        in_specs=[SMEM, ANY, ANY],
        out_specs=(VMEM,) * 4,
        scratch_shapes=[pltpu.SemaphoreType.DMA((8,))],
        compiler_params=pltpu.CompilerParams(vmem_limit_bytes=32 * 1024 * 1024),
    )(place, queries, output_gradient)


def own_keys(mine, paired, crossed):
    rows = 4 * (mine.shape[0] - META_ROWS)
    row = jax.ShapeDtypeStruct((1, rows), jnp.float32)
    own = jax.ShapeDtypeStruct((rows + META_ROWS, mine.shape[1]), jnp.bfloat16)
    return pl.pallas_call(
        own_kernel,
        out_shape=(own, row, row),
        in_specs=[VMEM] * 3,
        out_specs=(VMEM,) * 3,
        compiler_params=pltpu.CompilerParams(vmem_limit_bytes=32 * 1024 * 1024),
    )(mine, paired, crossed)


PLANE = ("xh", "core")
FINAL = ("xh", "core", "y", "xl")
RING = 8


def swapped(array, axes, by, count):
    return lax.ppermute(array, axes, [(i, i ^ by) for i in range(count)])


def turned(array, by):
    return lax.ppermute(array, "z", [(i, (i + by) % RING) for i in range(RING)])


def plus(*arrays):
    return sum(a.astype(jnp.float32) for a in arrays).astype(jnp.bfloat16)


def on_device(queries, key_vectors, value_vectors, output_gradient, positions, segments):
    window_count, row_count, _ = queries.shape
    across, pair = lax.axis_index("xh"), lax.axis_index("core")
    place = across * 2 + pair

    spot = place.reshape(1).astype(jnp.int32)
    code = jnp.pad(segments * CODE_SPAN + positions, ((0, 0), (0, 128 - row_count)))
    tied = lax.optimization_barrier
    mine, to_pair, across_part = pack_keys(spot, code, key_vectors, value_vectors)
    paired = swapped(to_pair, PLANE, 1, 4)
    spot, to_pair = tied((spot, to_pair))
    loads = pack_rows(spot, queries, output_gradient)
    crossed = swapped(jnp.stack([across_part, paired[1]]), PLANE, 2, 4)
    crossed, far_rows = tied((crossed, loads[2:4]))
    row_arrays = [loads[0], swapped(loads[1], PLANE, 1, 4)] + [swapped(far_rows[r - 2], PLANE, r, 4) for r in (2, 3)]
    own, low, high = own_keys(mine, paired, crossed)

    below, above = [own], [own]
    for _ in range(2):
        below.append(turned(below[-1], 1))
        above.append(turned(above[-1], -1))
    below[2], row_arrays[1:3] = tied((below[2], row_arrays[1:3]))
    below.append(turned(below[2], 1))
    above.append(turned(above[2], -1))
    below[3], row_arrays = tied((below[3], row_arrays))
    opposite = turned(below[3], 1)
    state = stats(low, high, row_arrays, [own, *below[1:], *above[1:]], None)
    state, opposite = tied((state, opposite))

    def gradients(pieces, before, last=False):
        return grads(spot, low, high, state, row_arrays, pieces, before, last)

    dq, to_up, state = gradients([opposite], None)
    spot, dq, to_up = tied((spot, dq, to_up))
    up = turned(to_up, 1)
    dq, up_grad, down_grad = gradients([above[3], below[3]], dq)
    dq, up_grad, down_grad, up = tied((dq, up_grad, down_grad, up))
    to_up, to_down = plus(up_grad, up), down_grad
    for k in (2, 1, 0):
        spot, dq, to_up, to_down = tied((spot, dq, to_up, to_down))
        up, down = turned(to_up, 1), turned(to_down, -1)
        if k:
            dq, up_grad, down_grad = gradients([above[k], below[k]], dq)
            dq, up_grad, down_grad, up, down = tied((dq, up_grad, down_grad, up, down))
            to_up, to_down = plus(up_grad, up), plus(down_grad, down)
    dq, own_grad = gradients([own], dq, True)
    dq, own_grad, up, down = tied((dq, own_grad, up, down))
    dkv_own = plus(own_grad, up, down)

    flip = dkv_own.reshape((2, 2) + dkv_own.shape[1:])
    flip = jnp.where(across == 1, flip[::-1], flip)
    flip = jnp.where(pair == 1, flip[:, ::-1], flip)

    heads = KEY_VALUE_HEADS
    out_rows = row_count // heads
    split = GROUP * HEAD_SIZE
    leaving = dq.at[:, :, split:].set(flip.reshape(dkv_own.shape)).reshape(window_count * heads, out_rows, split + 2 * HEAD_SIZE)
    final = lax.all_to_all(leaving, FINAL, 0, 0, tiled=True)

    def merged(array):
        width = array.shape[-1]
        return array.reshape(window_count, heads, out_rows, width).transpose(0, 2, 1, 3).reshape(window_count, out_rows, heads * width)

    return (
        merged(final[..., 0:split]),
        merged(final[..., split:split + HEAD_SIZE]),
        merged(final[..., split + HEAD_SIZE:]),
    )


def solution(mesh):
    fine = Mesh(mesh.devices.reshape(2, RING, 2, 4, 2), ("xh", "z", "core", "y", "xl"))
    ctx, head = ("xh", "z", "core"), ("y", "xl")
    vectors = P(None, ctx, head)
    out = P(None, ctx + head, None)
    return jax.shard_map(
        on_device,
        mesh=fine,
        in_specs=(vectors, vectors, vectors, vectors, P(None, ctx), P(None, ctx)),
        out_specs=(out, out, out),
        check_vma=False,
    )
```
